32 devices in a mesh: tok: 4 (over y, x), hid: 8 (over z, core).
Axes of the slice: x: 2, y: 2, z: 4, core: 2. Of those that a mesh axis runs over, the one named last changes fastest.
Arguments:
- tokens: bfloat16 [512, 8192], P('tok', 'hid'), may hold values from -6 to 6
- gate_weight: bfloat16 [8192, 16384], P('tok', 'hid'), may hold values from -0.09375 to 0.09375
- up_weight: bfloat16 [8192, 16384], P('tok', 'hid'), may hold values from -0.09375 to 0.09375
- down_weight: bfloat16 [16384, 8192], P('hid', 'tok'), may hold values from -0.0625 to 0.0625
- gate_keep: int32 [64, 128], P('tok', 'hid'), may hold values from 0 to 1, as said below
- up_keep: int32 [64, 128], P('tok', 'hid'), may hold values from 0 to 1, as said below
- down_keep: int32 [128, 64], P('hid', 'tok'), may hold values from 0 to 1, as said below
Outputs:
- mixed: bfloat16 [512, 8192], P('hid', 'tok')
The draws below stay inside these ranges and needn't reach their ends.
Inputs may be any that keep to these rules, and one draw needn't show every extreme that they name: `gate_keep`: in every device's shard of 16 x 16 blocks of a mask, between 64 and 128 blocks are kept; in every mask some shard keeps exactly 128. Shards of down_keep are 16 x 16. `up_keep`: as for gate_keep, drawn independently. `down_keep`: as for gate_keep, drawn independently.
All inputs are finite; a program needn't handle non-finite values.
Results may differ from the reference program's by a relative error of at most 0.0049.
Values may be sent and summed in bfloat16 or wider, within the bound.
No kernel may reach another device: no remote copies, remote signals or barrier semaphores. Data moves between devices by JAX's collectives and lax.ppermute only.
A program may use at most 256 MiB of HBM per device.

```python
import jax
import jax.numpy as jnp
from jax import lax

D = 8192
FF = 16384
BLK = 128
TOKENS = 512
N_TOK = 4
N_HID = 8


def keep_pattern(key, tiles_r, tiles_c, split_r, split_c):
    shard_r = tiles_r // split_r
    shard_c = tiles_c // split_c
    per_shard = shard_r * shard_c
    capacity = per_shard // 2
    lowest = per_shard // 4
    shard_count = split_r * split_c
    key_count, key_pick, key_perm = jax.random.split(key, 3)
    counts = jax.random.randint(key_count, (shard_count,), lowest, capacity + 1)
    chosen = jax.random.randint(key_pick, (), 0, shard_count)
    counts = jnp.where(jnp.arange(shard_count) == chosen, capacity, counts)
    orders = jax.vmap(lambda sub_key: jax.random.permutation(sub_key, per_shard))(jax.random.split(key_perm, shard_count))
    kept = (orders < counts[:, None]).astype(jnp.int32)
    kept = kept.reshape(split_r, split_c, shard_r, shard_c).transpose(0, 2, 1, 3)
    return kept.reshape(tiles_r, tiles_c)


def draw_gate_keep(key, part):
    return keep_pattern(jax.random.fold_in(key, 11), D // BLK, FF // BLK, N_TOK, N_HID)


def draw_up_keep(key, part):
    return keep_pattern(jax.random.fold_in(key, 23), D // BLK, FF // BLK, N_TOK, N_HID)


def draw_down_keep(key, part):
    return keep_pattern(jax.random.fold_in(key, 37), FF // BLK, D // BLK, N_HID, N_TOK)


def level_of(rng, shape, cuts, low, high):
    factor_of = 1.0
    for axis_at, parts in cuts:
        heights = jax.random.uniform(jax.random.fold_in(jax.random.fold_in(rng, 6), axis_at), (parts,), jnp.float32, low / len(cuts), high / len(cuts))
        factor_of = factor_of * jnp.repeat(jnp.exp(heights), shape[axis_at] // parts).reshape((-1,) + (1,) * (len(shape) - 1 - axis_at))
    return factor_of


def scatter_about(key, extent, deviation, limit, shards=(), kind=jnp.bfloat16):
    gain = level_of(key, extent, shards, -0.22, 0.18) if shards else 1.0
    result = jax.random.normal(key, extent, jnp.float32) * deviation * gain
    return jnp.minimum(jnp.maximum(result, -limit), limit).astype(kind)


def setup_inputs(seed: int = 0) -> dict:
    keys = jax.random.split(jax.random.key(seed), 8)
    return {
        "tokens": scatter_about(keys[0], (TOKENS, D), 1.0, 6.0, ((0, 4), (1, 8))),
        "gate_weight": scatter_about(keys[1], (D, FF), (D // 2) ** -0.5, 0.09375, ((0, 4), (1, 8))),
        "up_weight": scatter_about(keys[2], (D, FF), (D // 2) ** -0.5, 0.09375, ((0, 4), (1, 8))),
        "down_weight": scatter_about(keys[3], (FF, D), (FF // 2) ** -0.5, 0.0625, ((0, 8), (1, 4))),
        "gate_keep": draw_gate_keep(jax.random.fold_in(keys[7], 71), 0),
        "up_keep": draw_up_keep(jax.random.fold_in(keys[7], 71), 0),
        "down_keep": draw_down_keep(jax.random.fold_in(keys[7], 71), 0),
    }


def prune_blocks(weight, keep_mask):
    row_count, col_count = weight.shape
    tiles = weight.reshape(row_count // BLK, BLK, col_count // BLK, BLK)
    kept = tiles * keep_mask[:, None, :, None].astype(weight.dtype)
    return kept.reshape(row_count, col_count)


def reference(tokens, gate_weight, up_weight, down_weight, gate_keep, up_keep, down_keep):
    gate_out = jnp.dot(tokens, prune_blocks(gate_weight, gate_keep), preferred_element_type=jnp.float32)
    up_out = jnp.dot(tokens, prune_blocks(up_weight, up_keep), preferred_element_type=jnp.float32)
    hidden = (jax.nn.silu(gate_out) * up_out).astype(jnp.bfloat16)
    down_pruned = prune_blocks(down_weight, down_keep)
    width_part = FF // N_HID
    hidden_parts = hidden.reshape(hidden.shape[0], N_HID, width_part).transpose(1, 0, 2)
    down_parts = down_pruned.reshape(N_HID, width_part, down_pruned.shape[1])

    def add_part(total, pieces):
        term = jnp.dot(pieces[0], pieces[1], preferred_element_type=jnp.float32)
        return total + term, None

    start = jnp.zeros((hidden.shape[0], down_pruned.shape[1]), jnp.float32)
    mixed, _ = lax.scan(add_part, start, (hidden_parts, down_parts))
    return mixed.astype(jnp.bfloat16)
```

```python
import functools

import jax
import jax.numpy as jnp
from jax import lax
from jax.experimental import pallas as pl
from jax.experimental.pallas import tpu as pltpu
from jax.sharding import PartitionSpec as P

AXES = ("tok", "hid")
VMEM_BYTES = 48 * 1024 * 1024


def masked_tile(weight_ref, keep_ref, out_ref, first_col):
    block_rows = keep_ref.shape[0]
    side = weight_ref.shape[0] // block_rows
    for i in range(block_rows):
        for j in range(weight_ref.shape[1] // side):
            rows, cols = pl.ds(i * side, side), pl.ds(j * side, side)
            block = weight_ref[rows, cols]
            kept = keep_ref[i, first_col + j] != 0
            out_ref[rows, cols] = jnp.where(kept, block, jnp.zeros_like(block))


def gate_up_kernel(n, place_ref, gate_keep, up_keep, *refs):
    own, other = refs[:n], refs[n : 2 * n]
    gate_ref, up_ref, mine_ref = refs[2 * n : 2 * n + 3]
    away = refs[2 * n + 3 : 3 * n + 2]
    x, gate_w, up_w = refs[3 * n + 2 :]
    rows, half = own[0].shape
    step = pl.program_id(0)

    @pl.when(step == 0)
    def _():
        core = place_ref[2]
        for k in range(n):
            at = pl.ds(k * rows, rows)
            x[at, pl.ds(pl.multiple_of(core * half, half), half)] = own[k][...]
            x[at, pl.ds(pl.multiple_of((1 - core) * half, half), half)] = other[k][...]

    side = gate_ref.shape[0] // gate_keep.shape[0]
    first_col = step * (gate_ref.shape[1] // side)
    for which, (weight, keep, dense) in enumerate(((gate_ref, gate_keep, gate_w), (up_ref, up_keep, up_w))):
        masked_tile(weight, keep, dense, first_col)
        product = jnp.dot(x[...], dense[...], preferred_element_type=jnp.float32)
        mine_ref[which] = product[:rows]
        for k in range(1, n):
            away[k - 1][which] = product[k * rows : (k + 1) * rows].astype(jnp.bfloat16)


def gate_up(place, own, other, gate_weight, up_weight, gate_keep, up_keep):
    n = len(own)
    rows, half = own[0].shape
    depth, width = gate_weight.shape
    tile = min(width, 256)
    whole = pl.BlockSpec((rows, half), lambda i, *_: (0, 0))
    strip = pl.BlockSpec((depth, tile), lambda i, *_: (0, i))
    out = pl.BlockSpec((2, rows, tile), lambda i, *_: (0, 0, i))
    return pl.pallas_call(
        functools.partial(gate_up_kernel, n),
        grid_spec=pltpu.PrefetchScalarGridSpec(
            num_scalar_prefetch=3,
            grid=(width // tile,),
            in_specs=[whole] * (2 * n) + [strip, strip],
            out_specs=[out] * n,
            scratch_shapes=[
                pltpu.VMEM((n * rows, depth), jnp.bfloat16),
                pltpu.VMEM((depth, tile), jnp.bfloat16),
                pltpu.VMEM((depth, tile), jnp.bfloat16),
            ],
        ),
        out_shape=[jax.ShapeDtypeStruct((2, rows, width), jnp.float32)]
        + [jax.ShapeDtypeStruct((2, rows, width), jnp.bfloat16)] * (n - 1),
        compiler_params=pltpu.CompilerParams(vmem_limit_bytes=VMEM_BYTES),
        cost_estimate=pl.CostEstimate(
            flops=4 * n * rows * depth * width, bytes_accessed=4 * depth * width, transcendentals=0
        ),
        name="gate_up",
    )(place, gate_keep, up_keep, *own, *other, gate_weight, up_weight)


def hidden_kernel(mine_ref, *refs):
    arrived, out_ref = refs[:-1], refs[-1]
    gate, up = mine_ref[0], mine_ref[1]
    for part in arrived:
        gate += part[0].astype(jnp.float32)
        up += part[1].astype(jnp.float32)
    out_ref[...] = (gate / (1.0 + jnp.exp(-gate)) * up).astype(jnp.bfloat16)


def activate(mine, arrived):
    _, rows, width = mine.shape
    tile = min(width, 512)
    spec = pl.BlockSpec((2, rows, tile), lambda i: (0, 0, i))
    return pl.pallas_call(
        hidden_kernel,
        grid=(width // tile,),
        in_specs=[spec] * (1 + len(arrived)),
        out_specs=pl.BlockSpec((rows, tile), lambda i: (0, i)),
        out_shape=jax.ShapeDtypeStruct((rows, width), jnp.bfloat16),
        compiler_params=pltpu.CompilerParams(vmem_limit_bytes=VMEM_BYTES),
        name="hidden",
    )(mine, *arrived)


def down_kernel(n, place_ref, keep_ref, *refs):
    parts = refs[:n]
    weight_ref, mine_ref, other_ref, h, dense = refs[n:]
    rows = parts[0].shape[0]
    step = pl.program_id(0)

    @pl.when(step == 0)
    def _():
        for k in range(n):
            h[k * rows : (k + 1) * rows] = parts[k][...]

    side = weight_ref.shape[0] // keep_ref.shape[0]
    masked_tile(weight_ref, keep_ref, dense, step * (weight_ref.shape[1] // side))
    product = jnp.dot(h[...], dense[...], preferred_element_type=jnp.float32)
    tok, z, core = place_ref[0], place_ref[1], place_ref[2]
    half = rows // 2
    for k in range(n):
        slot = tok ^ z ^ k
        low = product[k * rows : k * rows + half]
        high = product[k * rows + half : (k + 1) * rows]
        mine_ref[slot] = jnp.where(core == 0, low, high)
        other_ref[slot] = jnp.where(core == 0, high, low).astype(jnp.bfloat16)


def down(place, parts, weight, keep):
    n = len(parts)
    rows = parts[0].shape[0]
    depth, width = weight.shape
    tile = min(width, 256)
    out = pl.BlockSpec((n, rows // 2, tile), lambda i, *_: (0, 0, i))
    return pl.pallas_call(
        functools.partial(down_kernel, n),
        grid_spec=pltpu.PrefetchScalarGridSpec(
            num_scalar_prefetch=2,
            grid=(width // tile,),
            in_specs=[pl.BlockSpec((rows, depth), lambda i, *_: (0, 0))] * n
            + [pl.BlockSpec((depth, tile), lambda i, *_: (0, i))],
            out_specs=[out, out],
            scratch_shapes=[
                pltpu.VMEM((n * rows, depth), jnp.bfloat16),
                pltpu.VMEM((depth, tile), jnp.bfloat16),
            ],
        ),
        out_shape=[
            jax.ShapeDtypeStruct((n, rows // 2, width), jnp.float32),
            jax.ShapeDtypeStruct((n, rows // 2, width), jnp.bfloat16),
        ],
        compiler_params=pltpu.CompilerParams(vmem_limit_bytes=VMEM_BYTES),
        cost_estimate=pl.CostEstimate(
            flops=2 * n * rows * depth * width, bytes_accessed=2 * depth * width, transcendentals=0
        ),
        name="down",
    )(place, keep, *parts, weight)


def pick(parts, index):
    chosen = parts[0]
    for i in range(1, len(parts)):
        chosen = jnp.where(index == i, parts[i], chosen)
    return chosen


def local(n_tok, n_hid, tokens, gate_weight, up_weight, down_weight, gate_keep, up_keep, down_keep):
    n_z = n_hid // 2
    tok, hid = lax.axis_index("tok"), lax.axis_index("hid")
    z, core = hid // 2, hid % 2
    place = jnp.stack([tok, z, core]).astype(jnp.int32)

    def send(value, to):
        perm = []
        for t in range(n_tok):
            for zz in range(n_z):
                for c in range(2):
                    a, b, d = to(t, zz, c)
                    perm.append((t * n_hid + zz * 2 + c, a * n_hid + b * 2 + d))
        return lax.ppermute(value, AXES, perm)

    def across_tok(value, k):
        return send(value, lambda t, zz, c: (t ^ k, zz, c))

    def across_z(value, j):
        return send(value, lambda t, zz, c: (t, zz ^ j, c))

    def across_core(value):
        return send(value, lambda t, zz, c: (t, zz, 1 - c))

    along_z = [tokens] + [across_z(tokens, j) for j in range(1, n_z)]
    picked = [pick(along_z, z ^ tok ^ k) for k in range(n_tok)]
    own = [picked[0]] + [across_tok(picked[k], k) for k in range(1, n_tok)]
    other = [across_core(part) for part in own]

    sums = gate_up(place, own, other, gate_weight, up_weight, gate_keep, up_keep)
    arrived = [across_tok(sums[k], k) for k in range(1, n_tok)]
    hidden = activate(sums[0], arrived)
    parts = [hidden] + [across_tok(hidden, k) for k in range(1, n_tok)]

    mine, theirs = down(place, parts, down_weight, down_keep)
    paired = across_core(theirs)
    out = mine[0] + paired[0].astype(jnp.float32)
    for j in range(1, n_z):
        both = (mine[j] + paired[j].astype(jnp.float32)).astype(jnp.bfloat16)
        out += across_z(both, j).astype(jnp.float32)
    return out.astype(jnp.bfloat16)


def solution(mesh):
    n_tok, n_hid = mesh.shape["tok"], mesh.shape["hid"]
    return jax.shard_map(
        functools.partial(local, n_tok, n_hid),
        mesh=mesh,
        in_specs=(
            P("tok", "hid"),
            P("tok", "hid"),
            P("tok", "hid"),
            P("hid", "tok"),
            P("tok", "hid"),
            P("tok", "hid"),
            P("hid", "tok"),
        ),
        out_specs=P("hid", "tok"),
        check_vma=False,
    )
```

```python
import functools

import jax
import jax.numpy as jnp
from jax import lax
from jax.experimental import pallas as pl
from jax.experimental.pallas import tpu as pltpu
from jax.sharding import PartitionSpec as P

AXES = ("tok", "hid")
BATCHES = 2
VMEM_BYTES = 48 * 1024 * 1024


def masked_tile(weight_ref, keep_ref, out_ref, first_col):
    block_rows = keep_ref.shape[0]
    side = weight_ref.shape[0] // block_rows
    for i in range(block_rows):
        for j in range(weight_ref.shape[1] // side):
            rows, cols = pl.ds(i * side, side), pl.ds(j * side, side)
            block = weight_ref[rows, cols]
            kept = keep_ref[i, first_col + j] != 0
            out_ref[rows, cols] = jnp.where(kept, block, jnp.zeros_like(block))


def gate_up_kernel(place_ref, gate_keep, up_keep, own_ref, other_ref, gate_ref, up_ref, keep_ref, send_ref, x, gate_w, up_w):
    n, rows, half = own_ref.shape
    step = pl.program_id(0)

    @pl.when(step == 0)
    def _():
        core = place_ref[0]
        mine = pl.ds(pl.multiple_of(core * half, half), half)
        others = pl.ds(pl.multiple_of((1 - core) * half, half), half)
        for p in range(n):
            at = pl.ds(p * rows, rows)
            x[at, mine] = own_ref[p]
            x[at, others] = other_ref[mirror(p, n)]

    side = gate_ref.shape[0] // gate_keep.shape[0]
    first_col = step * (gate_ref.shape[1] // side)
    for which, (weight, keep, dense) in enumerate(((gate_ref, gate_keep, gate_w), (up_ref, up_keep, up_w))):
        masked_tile(weight, keep, dense, first_col)
        product = jnp.dot(x[...], dense[...], preferred_element_type=jnp.float32)
        for p in range(n // 2):
            q = p + n // 2
            keep_ref[p, which] = product[p * rows : (p + 1) * rows]
            send_ref[p, which] = product[q * rows : (q + 1) * rows].astype(jnp.bfloat16)


def gate_up(place, own, other, gate_weight, up_weight, gate_keep, up_keep):
    n, rows, half = own.shape
    depth, width = gate_weight.shape
    tile = min(width, 256)
    whole = pl.BlockSpec((n, rows, half), lambda i, *_: (0, 0, 0))
    strip = pl.BlockSpec((depth, tile), lambda i, *_: (0, i))
    out = pl.BlockSpec((n // 2, 2, rows, tile), lambda i, *_: (0, 0, 0, i))
    return pl.pallas_call(
        gate_up_kernel,
        grid_spec=pltpu.PrefetchScalarGridSpec(
            num_scalar_prefetch=3,
            grid=(width // tile,),
            in_specs=[whole, whole, strip, strip],
            out_specs=[out, out],
            scratch_shapes=[
                pltpu.VMEM((n * rows, depth), jnp.bfloat16),
                pltpu.VMEM((depth, tile), jnp.bfloat16),
                pltpu.VMEM((depth, tile), jnp.bfloat16),
            ],
        ),
        out_shape=[
            jax.ShapeDtypeStruct((n // 2, 2, rows, width), jnp.float32),
            jax.ShapeDtypeStruct((n // 2, 2, rows, width), jnp.bfloat16),
        ],
        compiler_params=pltpu.CompilerParams(vmem_limit_bytes=VMEM_BYTES),
        cost_estimate=pl.CostEstimate(
            flops=4 * n * rows * depth * width, bytes_accessed=4 * depth * width, transcendentals=0
        ),
        name="gate_up",
    )(place, gate_keep, up_keep, own, other, gate_weight, up_weight)


def activate(gate, up):
    return (gate / (1.0 + jnp.exp(-gate)) * up).astype(jnp.bfloat16)


def down_kernel(n, place_ref, keep_ref, *refs):
    parts = refs[:n]
    weight_ref, mine_ref, other_ref, h, dense = refs[n:]
    rows = parts[0].shape[0]
    step = pl.program_id(0)

    @pl.when(step == 0)
    def _():
        for p in range(n):
            h[p * rows : (p + 1) * rows] = parts[p][...]

    side = weight_ref.shape[0] // keep_ref.shape[0]
    masked_tile(weight_ref, keep_ref, dense, step * (weight_ref.shape[1] // side))
    product = jnp.dot(h[...], dense[...], preferred_element_type=jnp.float32)
    core = place_ref[0]
    half = rows // 2
    for p in range(n):
        slot = place_ref[1 + p]
        low = product[p * rows : p * rows + half]
        high = product[p * rows + half : (p + 1) * rows]
        mine_ref[slot] = jnp.where(core == 0, low, high)
        other_ref[slot] = jnp.where(core == 0, high, low).astype(jnp.bfloat16)


def down(place, parts, weight, keep):
    n = len(parts)
    rows = parts[0].shape[0]
    depth, width = weight.shape
    tile = min(width, 256)
    out = pl.BlockSpec((n, rows // 2, tile), lambda i, *_: (0, 0, i))
    return pl.pallas_call(
        functools.partial(down_kernel, n),
        grid_spec=pltpu.PrefetchScalarGridSpec(
            num_scalar_prefetch=2,
            grid=(width // tile,),
            in_specs=[pl.BlockSpec((rows, depth), lambda i, *_: (0, 0))] * n
            + [pl.BlockSpec((depth, tile), lambda i, *_: (0, i))],
            out_specs=[out, out],
            scratch_shapes=[
                pltpu.VMEM((n * rows, depth), jnp.bfloat16),
                pltpu.VMEM((depth, tile), jnp.bfloat16),
            ],
        ),
        out_shape=[
            jax.ShapeDtypeStruct((n, rows // 2, width), jnp.float32),
            jax.ShapeDtypeStruct((n, rows // 2, width), jnp.bfloat16),
        ],
        compiler_params=pltpu.CompilerParams(vmem_limit_bytes=VMEM_BYTES),
        cost_estimate=pl.CostEstimate(
            flops=2 * n * rows * depth * width, bytes_accessed=2 * depth * width, transcendentals=0
        ),
        name="down",
    )(place, keep, *parts, weight)


def pick(parts, index):
    chosen = parts[0]
    for i in range(1, len(parts)):
        chosen = jnp.where(index == i, parts[i], chosen)
    return chosen


def mirror(p, n):
    out = 0
    while n > 1:
        out, p, n = out * 2 + p % 2, p // 2, n // 2
    return out


def local(n_tok, n_hid, tokens, gate_weight, up_weight, down_weight, gate_keep, up_keep, down_keep):
    n_z = n_hid // 2
    tok, hid = lax.axis_index("tok"), lax.axis_index("hid")
    z, core = hid // 2, hid % 2
    offsets = [jnp.where(core == 0, p, mirror(p, n_tok)) for p in range(n_tok)]
    place = jnp.stack([core] + [tok ^ z ^ off for off in offsets]).astype(jnp.int32)

    def send(value, to):
        perm = []
        for t in range(n_tok):
            for zz in range(n_z):
                for c in range(2):
                    a, b, d = to(t, zz, c)
                    perm.append((t * n_hid + zz * 2 + c, a * n_hid + b * 2 + d))
        return lax.ppermute(value, AXES, perm)

    def across_tok(value, p):
        return send(value, lambda t, zz, c: (t ^ (p if c == 0 else mirror(p, n_tok)), zz, c))

    def across_z(value, j):
        return send(value, lambda t, zz, c: (t, zz ^ j, c))

    def across_core(value):
        return send(value, lambda t, zz, c: (t, zz, 1 - c))

    def spread(block):
        along_z = [block] + [across_z(block, j) for j in range(1, n_z)]
        picked = [pick(along_z, z ^ tok ^ off) for off in offsets]
        own = jnp.stack([picked[0]] + [across_tok(picked[p], p) for p in range(1, n_tok)])
        return own, across_core(own)

    def middle(own, other):
        kept, sent = gate_up(place, own, other, gate_weight, up_weight, gate_keep, up_keep)
        left = n_tok // 2
        kept = [kept]
        while True:
            kept.append(across_tok(sent, left))
            if left == 1:
                break
            left //= 2
            sent = sum(part[left : 2 * left].astype(jnp.float32) for part in kept).astype(jnp.bfloat16)
        total = sum(part[0].astype(jnp.float32) for part in kept)
        parts = [activate(total[0], total[1])]
        while left < n_tok:
            parts += [across_tok(part, left) for part in parts]
            left *= 2
        return parts

    def finish(parts):
        mine, theirs = down(place, parts, down_weight, down_keep)
        paired = across_core(theirs)
        out = mine[0] + paired[0].astype(jnp.float32)
        for j in range(1, n_z):
            both = (mine[j] + paired[j].astype(jnp.float32)).astype(jnp.bfloat16)
            out += across_z(both, j).astype(jnp.float32)
        return out.astype(jnp.bfloat16)

    rows, features = tokens.shape
    piece = rows // (2 * BATCHES)
    split = tokens.reshape(2, BATCHES, piece, features)
    batches = [split[:, s].reshape(2 * piece, features) for s in range(BATCHES)]
    ready = [spread(block) for block in batches]
    hidden = [middle(*pair) for pair in ready]
    return jnp.concatenate([finish(parts) for parts in hidden], axis=0)


def solution(mesh):
    n_tok, n_hid = mesh.shape["tok"], mesh.shape["hid"]
    return jax.shard_map(
        functools.partial(local, n_tok, n_hid),
        mesh=mesh,
        in_specs=(
            P("tok", "hid"),
            P("tok", "hid"),
            P("tok", "hid"),
            P("hid", "tok"),
            P("tok", "hid"),
            P("tok", "hid"),
            P("hid", "tok"),
        ),
        out_specs=P("hid", "tok"),
        check_vma=False,
    )
```

```python
import functools

import jax
import jax.numpy as jnp
from jax import lax
from jax.experimental import pallas as pl
from jax.experimental.pallas import tpu as pltpu
from jax.sharding import PartitionSpec as P

AXES = ("tok", "hid")
BATCHES = 2
VMEM_BYTES = 48 * 1024 * 1024


def masked_product(x_ref, weight_ref, keep_ref):
    block_rows, width = keep_ref.shape
    side = weight_ref.shape[0] // block_rows
    group = min(4, block_rows)
    total = None
    for first in range(0, block_rows, group):
        strips = []
        for i in range(first, first + group):
            keep = jnp.broadcast_to(keep_ref[i : i + 1, :], (16, width)).astype(jnp.bfloat16)
            block = weight_ref[i * side : (i + 1) * side, :].reshape(side // 16, 16, width)
            strips.append((block * keep[None]).reshape(side, width))
        term = jnp.dot(
            x_ref[:, first * side : (first + group) * side],
            jnp.concatenate(strips, axis=0),
            preferred_element_type=jnp.float32,
        )
        total = term if total is None else total + term
    return total


def widen(keep_mask, width):
    return jnp.repeat(keep_mask.astype(jnp.float32), width // keep_mask.shape[1], axis=1)


def gate_up_kernel(place_ref, own_ref, other_ref, gate_ref, up_ref, gate_keep, up_keep, *refs):
    keep_ref, send_ref, x = refs[-3:]
    n, rows, half = own_ref.shape
    step = pl.program_id(0)

    @pl.when(step == 0)
    def _():
        core = place_ref[0]
        mine = pl.ds(pl.multiple_of(core * half, half), half)
        others = pl.ds(pl.multiple_of((1 - core) * half, half), half)
        for p in range(n):
            at = pl.ds(p * rows, rows)
            x[at, mine] = own_ref[p]
            x[at, others] = other_ref[mirror(p, n)]

    for which, (weight, keep) in enumerate(((gate_ref, gate_keep), (up_ref, up_keep))):
        product = masked_product(x, weight, keep)
        for p in range(n // 2):
            q = p + n // 2
            keep_ref[p, which] = product[p * rows : (p + 1) * rows]
            send_ref[p, which] = product[q * rows : (q + 1) * rows].astype(jnp.bfloat16)


def gate_up(place, own, other, gate_weight, up_weight, gate_keep, up_keep, after):
    n, rows, half = own.shape
    depth, width = gate_weight.shape
    tile = min(width, 256)
    whole = pl.BlockSpec((n, rows, half), lambda i, *_: (0, 0, 0))
    strip = pl.BlockSpec((depth, tile), lambda i, *_: (0, i))
    mask = pl.BlockSpec((gate_keep.shape[0], tile), lambda i, *_: (0, i))
    out = pl.BlockSpec((n // 2, 2, rows, tile), lambda i, *_: (0, 0, 0, i))
    return pl.pallas_call(
        gate_up_kernel,
        grid_spec=pltpu.PrefetchScalarGridSpec(
            num_scalar_prefetch=1,
            grid=(width // tile,),
            in_specs=[whole, whole, strip, strip, mask, mask] + [pl.BlockSpec(memory_space=pl.ANY)] * len(after),
            out_specs=[out, out],
            scratch_shapes=[pltpu.VMEM((n * rows, depth), jnp.bfloat16)],
        ),
        out_shape=[
            jax.ShapeDtypeStruct((n // 2, 2, rows, width), jnp.float32),
            jax.ShapeDtypeStruct((n // 2, 2, rows, width), jnp.bfloat16),
        ],
        compiler_params=pltpu.CompilerParams(vmem_limit_bytes=VMEM_BYTES),
        cost_estimate=pl.CostEstimate(
            flops=4 * n * rows * depth * width, bytes_accessed=4 * depth * width, transcendentals=0
        ),
        name="gate_up",
    )(place, own, other, gate_weight, up_weight, gate_keep, up_keep, *after)


def activate(gate, up):
    return (gate / (1.0 + jnp.exp(-gate)) * up).astype(jnp.bfloat16)


def down_kernel(n, place_ref, *refs):
    parts = refs[:n]
    weight_ref, keep_ref = refs[n : n + 2]
    mine_ref, other_ref, h = refs[-3:]
    rows = parts[0].shape[0]
    step = pl.program_id(0)

    @pl.when(step == 0)
    def _():
        for p in range(n):
            h[p * rows : (p + 1) * rows] = parts[p][...]

    product = masked_product(h, weight_ref, keep_ref)
    core = place_ref[0]
    half = rows // 2
    for p in range(n):
        slot = place_ref[1 + p]
        low = product[p * rows : p * rows + half]
        high = product[p * rows + half : (p + 1) * rows]
        mine_ref[slot] = jnp.where(core == 0, low, high)
        other_ref[slot] = jnp.where(core == 0, high, low).astype(jnp.bfloat16)


def down(place, parts, weight, keep, after):
    n = len(parts)
    rows = parts[0].shape[0]
    depth, width = weight.shape
    tile = min(width, 256)
    out = pl.BlockSpec((n, rows // 2, tile), lambda i, *_: (0, 0, i))
    return pl.pallas_call(
        functools.partial(down_kernel, n),
        grid_spec=pltpu.PrefetchScalarGridSpec(
            num_scalar_prefetch=1,
            grid=(width // tile,),
            in_specs=[pl.BlockSpec((rows, depth), lambda i, *_: (0, 0))] * n
            + [pl.BlockSpec((depth, tile), lambda i, *_: (0, i))]
            + [pl.BlockSpec((keep.shape[0], tile), lambda i, *_: (0, i))]
            + [pl.BlockSpec(memory_space=pl.ANY)] * len(after),
            out_specs=[out, out],
            scratch_shapes=[pltpu.VMEM((n * rows, depth), jnp.bfloat16)],
        ),
        out_shape=[
            jax.ShapeDtypeStruct((n, rows // 2, width), jnp.float32),
            jax.ShapeDtypeStruct((n, rows // 2, width), jnp.bfloat16),
        ],
        compiler_params=pltpu.CompilerParams(vmem_limit_bytes=VMEM_BYTES),
        cost_estimate=pl.CostEstimate(
            flops=2 * n * rows * depth * width, bytes_accessed=2 * depth * width, transcendentals=0
        ),
        name="down",
    )(place, *parts, weight, keep, *after)


def pick_kernel(n, order_ref, *refs):
    outs = refs[-n:]
    for p in range(n):
        for i in range(n):

            @pl.when(order_ref[p] == i)
            def _():
                outs[p][...] = refs[i][...]


def pick(order, parts, after):
    n = len(parts)
    spec = pl.BlockSpec(memory_space=pltpu.VMEM)
    return pl.pallas_call(
        functools.partial(pick_kernel, n),
        grid_spec=pltpu.PrefetchScalarGridSpec(
            num_scalar_prefetch=1,
            grid=(),
            in_specs=[spec] * n + [pl.BlockSpec(memory_space=pl.ANY)] * len(after),
            out_specs=[spec] * n,
        ),
        out_shape=[jax.ShapeDtypeStruct(parts[0].shape, parts[0].dtype)] * n,
        compiler_params=pltpu.CompilerParams(vmem_limit_bytes=VMEM_BYTES),
        name="pick",
    )(order, *parts, *after)


def join_kernel(n, *refs):
    for p in range(n):
        refs[-1][p] = refs[p][...]


def join(parts, after):
    n = len(parts)
    spec = pl.BlockSpec(memory_space=pltpu.VMEM)
    return pl.pallas_call(
        functools.partial(join_kernel, n),
        in_specs=[spec] * n + [pl.BlockSpec(memory_space=pl.ANY)] * len(after),
        out_specs=spec,
        out_shape=jax.ShapeDtypeStruct((n,) + parts[0].shape, parts[0].dtype),
        compiler_params=pltpu.CompilerParams(vmem_limit_bytes=VMEM_BYTES),
        name="join",
    )(*parts, *after)


def mirror(p, n):
    out = 0
    while n > 1:
        out, p, n = out * 2 + p % 2, p // 2, n // 2
    return out


def local(n_tok, n_hid, tokens, gate_weight, up_weight, down_weight, gate_keep, up_keep, down_keep):
    n_z = n_hid // 2
    tok, hid = lax.axis_index("tok"), lax.axis_index("hid")
    z, core = hid // 2, hid % 2
    offsets = [jnp.where(core == 0, p, mirror(p, n_tok)) for p in range(n_tok)]
    place = jnp.stack([core] + [tok ^ z ^ off for off in offsets]).astype(jnp.int32)

    def send(value, to):
        perm = []
        for t in range(n_tok):
            for zz in range(n_z):
                for c in range(2):
                    a, b, d = to(t, zz, c)
                    perm.append((t * n_hid + zz * 2 + c, a * n_hid + b * 2 + d))
        return lax.ppermute(value, AXES, perm)

    def across_tok(value, p):
        return send(value, lambda t, zz, c: (t ^ (p if c == 0 else mirror(p, n_tok)), zz, c))

    def across_z(value, j):
        return send(value, lambda t, zz, c: (t, zz ^ j, c))

    def across_core(value):
        return send(value, lambda t, zz, c: (t, zz, 1 - c))

    def along(block):
        return pick(place[1:], [block] + [across_z(block, j) for j in range(1, n_z)], ())

    def spread(picked, after):
        own = join([picked[0]] + [across_tok(picked[p], p) for p in range(1, n_tok)], after)
        return own, across_core(own)

    def halve(kept, sent):
        left = n_tok // 2
        kept = [kept]
        while True:
            kept.append(across_tok(sent, left))
            if left == 1:
                break
            left //= 2
            sent = sum(part[left : 2 * left].astype(jnp.float32) for part in kept).astype(jnp.bfloat16)
        total = sum(part[0].astype(jnp.float32) for part in kept)
        parts = [activate(total[0], total[1])]
        while left < n_tok:
            parts += [across_tok(part, left) for part in parts]
            left *= 2
        return parts

    def combine(mine, theirs):
        paired = across_core(theirs)
        sums = [mine[j] + paired[j].astype(jnp.float32) for j in range(n_z)]
        return sums[0], [part.astype(jnp.bfloat16) for part in sums[1:]]

    rows, features = tokens.shape
    piece = rows // (2 * BATCHES)
    split = tokens.reshape(2, BATCHES, piece, features)
    gate_wide = widen(gate_keep, gate_weight.shape[1])
    up_wide = widen(up_keep, up_weight.shape[1])
    down_wide = widen(down_keep, down_weight.shape[1])
    blocks = [split[:, s].reshape(2 * piece, features) for s in range(BATCHES)]
    picked = [along(block) for block in blocks]
    hidden, before = [], ()
    for s in range(BATCHES):
        own, other = spread(picked[s], before)
        after = picked[s + 1] if s + 1 < BATCHES else ()
        kept, sent = gate_up(place, own, other, gate_weight, up_weight, gate_wide, up_wide, after)
        before = (sent,)
        hidden.append(halve(kept, sent))
    out, after = [], []
    for s, parts in enumerate(hidden):
        after += [later[0] for later in hidden[s + 1 : s + 2]]
        mine, theirs = down(place, parts, down_weight, down_wide, after)
        total, sent = combine(mine, theirs)
        after = [across_z(sent[j - 1], j) for j in range(1, n_z)]
        for part in after:
            total += part.astype(jnp.float32)
        out.append(total.astype(jnp.bfloat16))
    return jnp.concatenate(out, axis=0)


def solution(mesh):
    n_tok, n_hid = mesh.shape["tok"], mesh.shape["hid"]
    return jax.shard_map(
        functools.partial(local, n_tok, n_hid),
        mesh=mesh,
        in_specs=(
            P("tok", "hid"),
            P("tok", "hid"),
            P("tok", "hid"),
            P("hid", "tok"),
            P("tok", "hid"),
            P("tok", "hid"),
            P("hid", "tok"),
        ),
        out_specs=P("hid", "tok"),
        check_vma=False,
    )
```

```python
import functools

import jax
import jax.numpy as jnp
from jax import lax
from jax.experimental import pallas as pl
from jax.experimental.pallas import tpu as pltpu
from jax.sharding import PartitionSpec as P

AXES = ("tok", "hid")
BATCHES = 2
TILE = 512
VMEM_BYTES = 48 * 1024 * 1024


def masked_product(x_ref, weight_ref, keep_ref):
    block_rows, width = keep_ref.shape
    side = weight_ref.shape[0] // block_rows
    group = min(4, block_rows)
    total = None
    for first in range(0, block_rows, group):
        strips = []
        for i in range(first, first + group):
            keep = jnp.broadcast_to(keep_ref[i : i + 1, :], (16, width)).astype(jnp.bfloat16)
            block = weight_ref[i * side : (i + 1) * side, :].reshape(side // 16, 16, width)
            strips.append((block * keep[None]).reshape(side, width))
        term = jnp.dot(
            x_ref[:, first * side : (first + group) * side],
            jnp.concatenate(strips, axis=0),
            preferred_element_type=jnp.float32,
        )
        total = term if total is None else total + term
    return total


def widen(keep_mask, width):
    return jnp.repeat(keep_mask.astype(jnp.float32), width // keep_mask.shape[1], axis=1)


def gate_up_kernel(n, place_ref, *refs):
    own, other = refs[:n], refs[n : 2 * n]
    gate_ref, up_ref, gate_keep, up_keep, keep_ref, send_ref, x = refs[2 * n :]
    _, piece, half = own[0].shape
    rows = 2 * piece

    @pl.when(pl.program_id(0) == 0)
    def _():
        core = place_ref[0]
        mine = pl.ds(pl.multiple_of(core * half, half), half)
        others = pl.ds(pl.multiple_of((1 - core) * half, half), half)
        for k in range(n):
            at = pl.ds(pl.multiple_of(place_ref[1 + n + k] * rows, rows), rows)
            x[at, mine] = own[k][...].reshape(rows, half)
            x[at, others] = other[k][...].reshape(rows, half)

    for which, (weight, keep) in enumerate(((gate_ref, gate_keep), (up_ref, up_keep))):
        product = masked_product(x, weight, keep)
        for p in range(n // 2):
            q = p + n // 2
            keep_ref[p, which] = product[p * rows : (p + 1) * rows]
            send_ref[p, which] = product[q * rows : (q + 1) * rows].astype(jnp.bfloat16)


def gate_up(place, batch, own, other, gate_weight, up_weight, gate_keep, up_keep):
    n = len(own)
    _, whole, half = own[0].shape
    piece = whole // BATCHES
    rows = 2 * piece
    depth, width = gate_weight.shape
    tile = min(width, TILE)
    part = pl.BlockSpec((2, piece, half), lambda i, *_: (0, batch, 0))
    strip = pl.BlockSpec((depth, tile), lambda i, *_: (0, i))
    mask = pl.BlockSpec((gate_keep.shape[0], tile), lambda i, *_: (0, i))
    out = pl.BlockSpec((n // 2, 2, rows, tile), lambda i, *_: (0, 0, 0, i))
    return pl.pallas_call(
        functools.partial(gate_up_kernel, n),
        grid_spec=pltpu.PrefetchScalarGridSpec(
            num_scalar_prefetch=1,
            grid=(width // tile,),
            in_specs=[part] * (2 * n) + [strip, strip, mask, mask],
            out_specs=[out, out],
            scratch_shapes=[pltpu.VMEM((n * rows, depth), jnp.bfloat16)],
        ),
        out_shape=[
            jax.ShapeDtypeStruct((n // 2, 2, rows, width), jnp.float32),
            jax.ShapeDtypeStruct((n // 2, 2, rows, width), jnp.bfloat16),
        ],
        compiler_params=pltpu.CompilerParams(vmem_limit_bytes=VMEM_BYTES),
        cost_estimate=pl.CostEstimate(
            flops=4 * n * rows * depth * width, bytes_accessed=4 * depth * width, transcendentals=0
        ),
        name="gate_up",
    )(place, *own, *other, gate_weight, up_weight, gate_keep, up_keep)


def activate(gate, up):
    return (gate / (1.0 + jnp.exp(-gate)) * up).astype(jnp.bfloat16)


def down_kernel(n, place_ref, *refs):
    parts = refs[:n]
    weight_ref, keep_ref = refs[n : n + 2]
    mine_ref, other_ref, h = refs[-3:]
    rows = parts[0].shape[0]
    step = pl.program_id(0)

    @pl.when(step == 0)
    def _():
        for p in range(n):
            h[p * rows : (p + 1) * rows] = parts[p][...]

    product = masked_product(h, weight_ref, keep_ref)
    core = place_ref[0]
    half = rows // 2
    for p in range(n):
        slot = place_ref[1 + p]
        low = product[p * rows : p * rows + half]
        high = product[p * rows + half : (p + 1) * rows]
        mine_ref[slot] = jnp.where(core == 0, low, high)
        other_ref[slot] = jnp.where(core == 0, high, low).astype(jnp.bfloat16)


def down(place, parts, weight, keep, after):
    n = len(parts)
    rows = parts[0].shape[0]
    depth, width = weight.shape
    tile = min(width, TILE)
    out = pl.BlockSpec((n, rows // 2, tile), lambda i, *_: (0, 0, i))
    return pl.pallas_call(
        functools.partial(down_kernel, n),
        grid_spec=pltpu.PrefetchScalarGridSpec(
            num_scalar_prefetch=1,
            grid=(width // tile,),
            in_specs=[pl.BlockSpec((rows, depth), lambda i, *_: (0, 0))] * n
            + [pl.BlockSpec((depth, tile), lambda i, *_: (0, i))]
            + [pl.BlockSpec((keep.shape[0], tile), lambda i, *_: (0, i))]
            + [pl.BlockSpec(memory_space=pl.ANY)] * len(after),
            out_specs=[out, out],
            scratch_shapes=[pltpu.VMEM((n * rows, depth), jnp.bfloat16)],
        ),
        out_shape=[
            jax.ShapeDtypeStruct((n, rows // 2, width), jnp.float32),
            jax.ShapeDtypeStruct((n, rows // 2, width), jnp.bfloat16),
        ],
        compiler_params=pltpu.CompilerParams(vmem_limit_bytes=VMEM_BYTES),
        cost_estimate=pl.CostEstimate(
            flops=2 * n * rows * depth * width, bytes_accessed=2 * depth * width, transcendentals=0
        ),
        name="down",
    )(place, *parts, weight, keep, *after)


def mirror(p, n):
    out = 0
    while n > 1:
        out, p, n = out * 2 + p % 2, p // 2, n // 2
    return out


def local(n_tok, n_hid, tokens, gate_weight, up_weight, down_weight, gate_keep, up_keep, down_keep):
    n_z = n_hid // 2
    tok, hid = lax.axis_index("tok"), lax.axis_index("hid")
    z, core = hid // 2, hid % 2
    offsets = [jnp.where(core == 0, p, mirror(p, n_tok)) for p in range(n_tok)]
    positions = [sum(jnp.where(off == tok ^ z ^ k, p, 0) for p, off in enumerate(offsets)) for k in range(n_tok)]
    place = jnp.stack([core] + [tok ^ z ^ off for off in offsets] + positions).astype(jnp.int32)

    def send(value, to):
        perm = []
        for t in range(n_tok):
            for zz in range(n_z):
                for c in range(2):
                    a, b, d = to(t, zz, c)
                    perm.append((t * n_hid + zz * 2 + c, a * n_hid + b * 2 + d))
        return lax.ppermute(value, AXES, perm)

    def across_tok(value, p):
        return send(value, lambda t, zz, c: (t ^ (p if c == 0 else mirror(p, n_tok)), zz, c))

    def across_z(value, j):
        return send(value, lambda t, zz, c: (t, zz ^ j, c))

    def across_core(value):
        return send(value, lambda t, zz, c: (t, zz, 1 - c))

    def halve(kept, sent):
        left = n_tok // 2
        kept = [kept]
        while True:
            kept.append(across_tok(sent, left))
            if left == 1:
                break
            left //= 2
            sent = sum(part[left : 2 * left].astype(jnp.float32) for part in kept).astype(jnp.bfloat16)
        total = sum(part[0].astype(jnp.float32) for part in kept)
        parts = [activate(total[0], total[1])]
        while left < n_tok:
            parts += [across_tok(part, left) for part in parts]
            left *= 2
        return parts

    def combine(mine, theirs):
        paired = across_core(theirs)
        sums = [mine[j] + paired[j].astype(jnp.float32) for j in range(n_z)]
        return sums[0], [part.astype(jnp.bfloat16) for part in sums[1:]]

    rows, features = tokens.shape
    gate_wide = widen(gate_keep, gate_weight.shape[1])
    up_wide = widen(up_keep, up_weight.shape[1])
    down_wide = widen(down_keep, down_weight.shape[1])
    moved = [send(tokens, lambda t, zz, c: (zz, t ^ k, c)) for k in range(n_z)]
    swapped = [across_core(block) for block in moved]
    own = [block.reshape(2, rows // 2, features) for block in moved]
    other = [block.reshape(2, rows // 2, features) for block in swapped]
    hidden = []
    for s in range(BATCHES):
        kept, sent = gate_up(place, s, own, other, gate_weight, up_weight, gate_wide, up_wide)
        hidden.append(halve(kept, sent))
    out, after = [], []
    for s, parts in enumerate(hidden):
        after += [later[1] for later in hidden[s + 1 : s + 2]]
        mine, theirs = down(place, parts, down_weight, down_wide, after)
        total, sent = combine(mine, theirs)
        after = [across_z(sent[j - 1], j) for j in range(1, n_z)]
        for part in after:
            total += part.astype(jnp.float32)
        out.append(total.astype(jnp.bfloat16))
    return jnp.concatenate(out, axis=0)


def solution(mesh):
    n_tok, n_hid = mesh.shape["tok"], mesh.shape["hid"]
    return jax.shard_map(
        functools.partial(local, n_tok, n_hid),
        mesh=mesh,
        in_specs=(
            P("tok", "hid"),
            P("tok", "hid"),
            P("tok", "hid"),
            P("hid", "tok"),
            P("tok", "hid"),
            P("tok", "hid"),
            P("hid", "tok"),
        ),
        out_specs=P("hid", "tok"),
        check_vma=False,
    )
```

```python
import functools

import jax
import jax.numpy as jnp
from jax import lax
from jax.experimental import pallas as pl
from jax.experimental.pallas import tpu as pltpu
from jax.sharding import PartitionSpec as P

AXES = ("tok", "hid")
BATCHES = 2
TILE = 512
VMEM_BYTES = 48 * 1024 * 1024


def masked_product(x_ref, weight_ref, keep_ref):
    block_rows, width = keep_ref.shape
    side = weight_ref.shape[0] // block_rows
    group = min(4, block_rows)
    total = None
    for first in range(0, block_rows, group):
        strips = []
        for i in range(first, first + group):
            keep = jnp.broadcast_to(keep_ref[i : i + 1, :], (16, width)).astype(jnp.bfloat16)
            block = weight_ref[i * side : (i + 1) * side, :].reshape(side // 16, 16, width)
            strips.append((block * keep[None]).reshape(side, width))
        term = jnp.dot(
            x_ref[:, first * side : (first + group) * side],
            jnp.concatenate(strips, axis=0),
            preferred_element_type=jnp.float32,
        )
        total = term if total is None else total + term
    return total


def widen(keep_mask, width):
    return jnp.repeat(keep_mask.astype(jnp.float32), width // keep_mask.shape[1], axis=1)


def gate_up_kernel(n, place_ref, *refs):
    own, other = refs[:n], refs[n : 2 * n]
    gate_ref, up_ref, gate_keep, up_keep, keep_ref, send_ref, x = refs[2 * n :]
    _, piece, half = own[0].shape
    rows = 2 * piece

    @pl.when(pl.program_id(0) == 0)
    def _():
        core = place_ref[0]
        mine = pl.ds(pl.multiple_of(core * half, half), half)
        others = pl.ds(pl.multiple_of((1 - core) * half, half), half)
        for k in range(n):
            at = pl.ds(pl.multiple_of(place_ref[1 + n + k] * rows, rows), rows)
            x[at, mine] = own[k][...].reshape(rows, half)
            x[at, others] = other[k][...].reshape(rows, half)

    for which, (weight, keep) in enumerate(((gate_ref, gate_keep), (up_ref, up_keep))):
        product = masked_product(x, weight, keep)
        for p in range(n // 2):
            q = p + n // 2
            keep_ref[p, which] = product[p * rows : (p + 1) * rows]
            send_ref[p, which] = product[q * rows : (q + 1) * rows].astype(jnp.bfloat16)


def gate_up(place, batch, own, other, gate_weight, up_weight, gate_keep, up_keep):
    n = len(own)
    _, whole, half = own[0].shape
    piece = whole // BATCHES
    rows = 2 * piece
    depth, width = gate_weight.shape
    tile = min(width, TILE)
    part = pl.BlockSpec((2, piece, half), lambda i, *_: (0, batch, 0))
    strip = pl.BlockSpec((depth, tile), lambda i, *_: (0, i))
    mask = pl.BlockSpec((gate_keep.shape[0], tile), lambda i, *_: (0, i))
    out = pl.BlockSpec((n // 2, 2, rows, tile), lambda i, *_: (0, 0, 0, i))
    return pl.pallas_call(
        functools.partial(gate_up_kernel, n),
        grid_spec=pltpu.PrefetchScalarGridSpec(
            num_scalar_prefetch=1,
            grid=(width // tile,),
            in_specs=[part] * (2 * n) + [strip, strip, mask, mask],
            out_specs=[out, out],
            scratch_shapes=[pltpu.VMEM((n * rows, depth), jnp.bfloat16)],
        ),
        out_shape=[
            jax.ShapeDtypeStruct((n // 2, 2, rows, width), jnp.float32),
            jax.ShapeDtypeStruct((n // 2, 2, rows, width), jnp.bfloat16),
        ],
        compiler_params=pltpu.CompilerParams(vmem_limit_bytes=VMEM_BYTES),
        cost_estimate=pl.CostEstimate(
            flops=4 * n * rows * depth * width, bytes_accessed=4 * depth * width, transcendentals=0
        ),
        name="gate_up",
    )(place, *own, *other, gate_weight, up_weight, gate_keep, up_keep)


def add_kernel(n, *refs):
    total = refs[0][...].astype(jnp.float32)
    for ref in refs[1:n]:
        total += ref[...].astype(jnp.float32)
    refs[-1][...] = total.astype(jnp.bfloat16)


def add_slots(parts, first, count, after):
    _, two, rows, width = parts[0].shape
    return pl.pallas_call(
        functools.partial(add_kernel, len(parts)),
        grid=(count, two),
        in_specs=[pl.BlockSpec((1, 1, rows, width), lambda i, j: (first + i, j, 0, 0))] * len(parts)
        + [pl.BlockSpec(memory_space=pl.ANY)] * len(after),
        out_specs=pl.BlockSpec((1, 1, rows, width), lambda i, j: (i, j, 0, 0)),
        out_shape=jax.ShapeDtypeStruct((count, two, rows, width), jnp.bfloat16),
        compiler_params=pltpu.CompilerParams(vmem_limit_bytes=VMEM_BYTES),
        name="add_slots",
    )(*parts, *after)


def activate_kernel(n, *refs):
    gate = refs[0][0, 0].astype(jnp.float32)
    up = refs[0][0, 1].astype(jnp.float32)
    for ref in refs[1:n]:
        gate += ref[0, 0].astype(jnp.float32)
        up += ref[0, 1].astype(jnp.float32)
    refs[-1][...] = (gate / (1.0 + jnp.exp(-gate)) * up).astype(jnp.bfloat16)


def activate(parts, after):
    _, two, rows, width = parts[0].shape
    tile = width // 2
    return pl.pallas_call(
        functools.partial(activate_kernel, len(parts)),
        grid=(width // tile,),
        in_specs=[pl.BlockSpec((1, two, rows, tile), lambda i: (0, 0, 0, i))] * len(parts)
        + [pl.BlockSpec(memory_space=pl.ANY)] * len(after),
        out_specs=pl.BlockSpec((rows, tile), lambda i: (0, i)),
        out_shape=jax.ShapeDtypeStruct((rows, width), jnp.bfloat16),
        compiler_params=pltpu.CompilerParams(vmem_limit_bytes=VMEM_BYTES),
        name="hidden",
    )(*parts, *after)


def down_kernel(n, place_ref, *refs):
    parts = refs[:n]
    weight_ref, keep_ref = refs[n : n + 2]
    mine_ref, other_ref, h = refs[-3:]
    rows = parts[0].shape[0]
    step = pl.program_id(0)

    @pl.when(step == 0)
    def _():
        for p in range(n):
            h[p * rows : (p + 1) * rows] = parts[p][...]

    product = masked_product(h, weight_ref, keep_ref)
    core = place_ref[0]
    half = rows // 2
    for p in range(n):
        slot = place_ref[1 + p]
        low = product[p * rows : p * rows + half]
        high = product[p * rows + half : (p + 1) * rows]
        mine_ref[slot] = jnp.where(core == 0, low, high)
        other_ref[slot] = jnp.where(core == 0, high, low).astype(jnp.bfloat16)


def down(place, parts, weight, keep, after):
    n = len(parts)
    rows = parts[0].shape[0]
    depth, width = weight.shape
    tile = min(width, TILE)
    out = pl.BlockSpec((n, rows // 2, tile), lambda i, *_: (0, 0, i))
    return pl.pallas_call(
        functools.partial(down_kernel, n),
        grid_spec=pltpu.PrefetchScalarGridSpec(
            num_scalar_prefetch=1,
            grid=(width // tile,),
            in_specs=[pl.BlockSpec((rows, depth), lambda i, *_: (0, 0))] * n
            + [pl.BlockSpec((depth, tile), lambda i, *_: (0, i))]
            + [pl.BlockSpec((keep.shape[0], tile), lambda i, *_: (0, i))]
            + [pl.BlockSpec(memory_space=pl.ANY)] * len(after),
            out_specs=[out, out],
            scratch_shapes=[pltpu.VMEM((n * rows, depth), jnp.bfloat16)],
        ),
        out_shape=[
            jax.ShapeDtypeStruct((n, rows // 2, width), jnp.float32),
            jax.ShapeDtypeStruct((n, rows // 2, width), jnp.bfloat16),
        ],
        compiler_params=pltpu.CompilerParams(vmem_limit_bytes=VMEM_BYTES),
        cost_estimate=pl.CostEstimate(
            flops=2 * n * rows * depth * width, bytes_accessed=2 * depth * width, transcendentals=0
        ),
        name="down",
    )(place, *parts, weight, keep, *after)


def mirror(p, n):
    out = 0
    while n > 1:
        out, p, n = out * 2 + p % 2, p // 2, n // 2
    return out


def local(n_tok, n_hid, tokens, gate_weight, up_weight, down_weight, gate_keep, up_keep, down_keep):
    n_z = n_hid // 2
    tok, hid = lax.axis_index("tok"), lax.axis_index("hid")
    z, core = hid // 2, hid % 2
    offsets = [jnp.where(core == 0, p, mirror(p, n_tok)) for p in range(n_tok)]
    positions = [sum(jnp.where(off == tok ^ z ^ k, p, 0) for p, off in enumerate(offsets)) for k in range(n_tok)]
    place = jnp.stack([core] + [tok ^ z ^ off for off in offsets] + positions).astype(jnp.int32)

    def send(value, to):
        perm = []
        for t in range(n_tok):
            for zz in range(n_z):
                for c in range(2):
                    a, b, d = to(t, zz, c)
                    perm.append((t * n_hid + zz * 2 + c, a * n_hid + b * 2 + d))
        return lax.ppermute(value, AXES, perm)

    def across_tok(value, p):
        return send(value, lambda t, zz, c: (t ^ (p if c == 0 else mirror(p, n_tok)), zz, c))

    def across_z(value, j):
        return send(value, lambda t, zz, c: (t, zz ^ j, c))

    def across_core(value):
        return send(value, lambda t, zz, c: (t, zz, 1 - c))

    def halve(kept, sent, after):
        left = n_tok // 2
        kept = [kept]
        while True:
            kept.append(across_tok(sent, left))
            if left == 1:
                return kept
            left //= 2
            sent = add_slots(kept, left, left, after)

    def gather(part):
        parts, left = [part], 1
        while left < n_tok:
            parts += [across_tok(part, left) for part in parts]
            left *= 2
        return parts

    def combine(mine, theirs):
        paired = across_core(theirs)
        sums = [mine[j] + paired[j].astype(jnp.float32) for j in range(n_z)]
        return sums[0], [part.astype(jnp.bfloat16) for part in sums[1:]]

    rows, features = tokens.shape
    gate_wide = widen(gate_keep, gate_weight.shape[1])
    up_wide = widen(up_keep, up_weight.shape[1])
    down_wide = widen(down_keep, down_weight.shape[1])
    moved = [send(tokens, lambda t, zz, c: (zz, t ^ k, c)) for k in range(n_z)]
    swapped = [across_core(block) for block in moved]
    own = [block.reshape(2, rows // 2, features) for block in moved]
    other = [block.reshape(2, rows // 2, features) for block in swapped]
    sums = [gate_up(place, s, own, other, gate_weight, up_weight, gate_wide, up_wide) for s in range(BATCHES)]
    out, before_add, before_hidden, before_down = [], [], [], []
    for kept, sent in sums:
        kept = halve(kept, sent, before_add)
        parts = gather(activate(kept, before_hidden))
        mine, theirs = down(place, parts, down_weight, down_wide, before_down)
        total, sent = combine(mine, theirs)
        arrived = [across_z(sent[j - 1], j) for j in range(1, n_z)]
        for part in arrived:
            total += part.astype(jnp.float32)
        out.append(total.astype(jnp.bfloat16))
        before_add, before_hidden, before_down = [parts[1]], [theirs], arrived
    return jnp.concatenate(out, axis=0)


def solution(mesh):
    n_tok, n_hid = mesh.shape["tok"], mesh.shape["hid"]
    return jax.shard_map(
        functools.partial(local, n_tok, n_hid),
        mesh=mesh,
        in_specs=(
            P("tok", "hid"),
            P("tok", "hid"),
            P("tok", "hid"),
            P("hid", "tok"),
            P("tok", "hid"),
            P("tok", "hid"),
            P("hid", "tok"),
        ),
        out_specs=P("hid", "tok"),
        check_vma=False,
    )
```

```python
import functools

import jax
import jax.numpy as jnp
from jax import lax
from jax.experimental import pallas as pl
from jax.experimental.pallas import tpu as pltpu
from jax.sharding import PartitionSpec as P

AXES = ("tok", "hid")
BATCHES = 2
TILE = 512
VMEM_BYTES = 48 * 1024 * 1024


def masked_product(x_ref, weight_ref, keep_ref):
    block_rows, width = keep_ref.shape
    side = weight_ref.shape[0] // block_rows
    group = min(4, block_rows)
    total = None
    for first in range(0, block_rows, group):
        strips = []
        for i in range(first, first + group):
            keep = jnp.broadcast_to(keep_ref[i : i + 1, :], (16, width)).astype(jnp.bfloat16)
            block = weight_ref[i * side : (i + 1) * side, :].reshape(side // 16, 16, width)
            strips.append((block * keep[None]).reshape(side, width))
        term = jnp.dot(
            x_ref[:, first * side : (first + group) * side],
            jnp.concatenate(strips, axis=0),
            preferred_element_type=jnp.float32,
        )
        total = term if total is None else total + term
    return total


def widen(keep_mask, width):
    return jnp.repeat(keep_mask.astype(jnp.float32), width // keep_mask.shape[1], axis=1)


def gate_up_kernel(n, place_ref, own_ref, other_ref, gate_ref, up_ref, gate_keep, up_keep, *refs):
    outs, x = refs[:4], refs[4]
    _, rows, half = own_ref.shape

    @pl.when(pl.program_id(0) == 0)
    def _():
        core = place_ref[0]
        mine = pl.ds(pl.multiple_of(core * half, half), half)
        others = pl.ds(pl.multiple_of((1 - core) * half, half), half)
        for k in range(n):
            at = pl.ds(pl.multiple_of(place_ref[1 + n + k] * rows, rows), rows)
            x[at, mine] = own_ref[k]
            x[at, others] = other_ref[k]

    for which, (weight, keep) in enumerate(((gate_ref, gate_keep), (up_ref, up_keep))):
        product = masked_product(x, weight, keep)
        for p in range(n):
            offset = p if which == 0 else mirror(p, n)
            term = product[offset * rows : (offset + 1) * rows]
            if p < n // 2:
                outs[which][p] = term
            else:
                outs[2 + which][p - n // 2] = term.astype(jnp.bfloat16)


def gate_up(place, own, other, gate_weight, up_weight, gate_keep, up_keep):
    n, rows, half = own.shape
    depth, width = gate_weight.shape
    tile = min(width, TILE)
    whole = pl.BlockSpec((n, rows, half), lambda i, *_: (0, 0, 0))
    strip = pl.BlockSpec((depth, tile), lambda i, *_: (0, i))
    mask = pl.BlockSpec((gate_keep.shape[0], tile), lambda i, *_: (0, i))
    out = pl.BlockSpec((n // 2, rows, tile), lambda i, *_: (0, 0, i))
    return pl.pallas_call(
        functools.partial(gate_up_kernel, n),
        grid_spec=pltpu.PrefetchScalarGridSpec(
            num_scalar_prefetch=1,
            grid=(width // tile,),
            in_specs=[whole, whole, strip, strip, mask, mask],
            out_specs=[out] * 4,
            scratch_shapes=[pltpu.VMEM((n * rows, depth), jnp.bfloat16)],
        ),
        out_shape=[jax.ShapeDtypeStruct((n // 2, rows, width), jnp.float32)] * 2
        + [jax.ShapeDtypeStruct((n // 2, rows, width), jnp.bfloat16)] * 2,
        compiler_params=pltpu.CompilerParams(vmem_limit_bytes=VMEM_BYTES),
        cost_estimate=pl.CostEstimate(
            flops=4 * n * rows * depth * width, bytes_accessed=4 * depth * width, transcendentals=0
        ),
        name="gate_up",
    )(place, own, other, gate_weight, up_weight, gate_keep, up_keep)


def total_of(refs):
    total = refs[0][...].astype(jnp.float32)
    for ref in refs[1:]:
        total += ref[...].astype(jnp.float32)
    return total


def add_kernel(n, *refs):
    refs[-2][...] = total_of(refs[:n]).astype(jnp.bfloat16)
    refs[-1][...] = total_of(refs[n : 2 * n]).astype(jnp.bfloat16)


def add_slots(gate_parts, up_parts, first, count, after):
    _, rows, width = gate_parts[0].shape
    n = len(gate_parts)
    return pl.pallas_call(
        functools.partial(add_kernel, n),
        grid=(count,),
        in_specs=[pl.BlockSpec((1, rows, width), lambda i: (first + i, 0, 0))] * (2 * n)
        + [pl.BlockSpec(memory_space=pl.ANY)] * len(after),
        out_specs=[pl.BlockSpec((1, rows, width), lambda i: (i, 0, 0))] * 2,
        out_shape=[jax.ShapeDtypeStruct((count, rows, width), jnp.bfloat16)] * 2,
        compiler_params=pltpu.CompilerParams(vmem_limit_bytes=VMEM_BYTES),
        name="add_slots",
    )(*gate_parts, *up_parts, *after)


def activate_kernel(n, *refs):
    gate = total_of(refs[:n])[0]
    up = total_of(refs[n : 2 * n])[0]
    refs[-1][...] = (gate / (1.0 + jnp.exp(-gate)) * up).astype(jnp.bfloat16)


def activate(gate_parts, up_parts, after):
    _, rows, width = gate_parts[0].shape
    tile = width // 2
    n = len(gate_parts)
    return pl.pallas_call(
        functools.partial(activate_kernel, n),
        grid=(width // tile,),
        in_specs=[pl.BlockSpec((1, rows, tile), lambda i: (0, 0, i))] * (2 * n)
        + [pl.BlockSpec(memory_space=pl.ANY)] * len(after),
        out_specs=pl.BlockSpec((rows, tile), lambda i: (0, i)),
        out_shape=jax.ShapeDtypeStruct((rows, width), jnp.bfloat16),
        compiler_params=pltpu.CompilerParams(vmem_limit_bytes=VMEM_BYTES),
        name="hidden",
    )(*gate_parts, *up_parts, *after)


def down_kernel(n, place_ref, *refs):
    parts = refs[:n]
    weight_ref, keep_ref = refs[n : n + 2]
    mine_ref, other_ref, h = refs[-3:]
    rows = parts[0].shape[0]
    step = pl.program_id(0)

    @pl.when(step == 0)
    def _():
        for p in range(n):
            h[p * rows : (p + 1) * rows] = parts[p][...]

    product = masked_product(h, weight_ref, keep_ref)
    core = place_ref[0]
    half = rows // 2
    for p in range(n):
        slot = place_ref[1 + p]
        low = product[p * rows : p * rows + half]
        high = product[p * rows + half : (p + 1) * rows]
        mine_ref[slot] = jnp.where(core == 0, low, high)
        other_ref[slot] = jnp.where(core == 0, high, low).astype(jnp.bfloat16)


def down(place, parts, weight, keep, after):
    n = len(parts)
    rows = parts[0].shape[0]
    depth, width = weight.shape
    tile = min(width, TILE)
    out = pl.BlockSpec((n, rows // 2, tile), lambda i, *_: (0, 0, i))
    return pl.pallas_call(
        functools.partial(down_kernel, n),
        grid_spec=pltpu.PrefetchScalarGridSpec(
            num_scalar_prefetch=1,
            grid=(width // tile,),
            in_specs=[pl.BlockSpec((rows, depth), lambda i, *_: (0, 0))] * n
            + [pl.BlockSpec((depth, tile), lambda i, *_: (0, i))]
            + [pl.BlockSpec((keep.shape[0], tile), lambda i, *_: (0, i))]
            + [pl.BlockSpec(memory_space=pl.ANY)] * len(after),
            out_specs=[out, out],
            scratch_shapes=[pltpu.VMEM((n * rows, depth), jnp.bfloat16)],
        ),
        out_shape=[
            jax.ShapeDtypeStruct((n, rows // 2, width), jnp.float32),
            jax.ShapeDtypeStruct((n, rows // 2, width), jnp.bfloat16),
        ],
        compiler_params=pltpu.CompilerParams(vmem_limit_bytes=VMEM_BYTES),
        cost_estimate=pl.CostEstimate(
            flops=2 * n * rows * depth * width, bytes_accessed=2 * depth * width, transcendentals=0
        ),
        name="down",
    )(place, *parts, weight, keep, *after)


def join_kernel(n, *refs):
    for k in range(n):
        refs[-1][k] = refs[k][...]


def join(blocks, after):
    n = len(blocks)
    spec = pl.BlockSpec(memory_space=pltpu.VMEM)
    return pl.pallas_call(
        functools.partial(join_kernel, n),
        in_specs=[spec] * n + [pl.BlockSpec(memory_space=pl.ANY)] * len(after),
        out_specs=spec,
        out_shape=jax.ShapeDtypeStruct((n,) + blocks[0].shape, blocks[0].dtype),
        compiler_params=pltpu.CompilerParams(vmem_limit_bytes=VMEM_BYTES),
        name="join",
    )(*blocks, *after)


def mirror(p, n):
    out = 0
    while n > 1:
        out, p, n = out * 2 + p % 2, p // 2, n // 2
    return out


def local(n_tok, n_hid, tokens, gate_weight, up_weight, down_weight, gate_keep, up_keep, down_keep):
    n_z = n_hid // 2
    tok, hid = lax.axis_index("tok"), lax.axis_index("hid")
    z, core = hid // 2, hid % 2
    offsets = [jnp.where(core == 0, p, mirror(p, n_tok)) for p in range(n_tok)]
    place = jnp.stack([core] + [tok ^ z ^ off for off in offsets] + [tok ^ z ^ k for k in range(n_z)])
    place = place.astype(jnp.int32)

    def send(value, to):
        perm = []
        for t in range(n_tok):
            for zz in range(n_z):
                for c in range(2):
                    a, b, d = to(t, zz, c)
                    perm.append((t * n_hid + zz * 2 + c, a * n_hid + b * 2 + d))
        return lax.ppermute(value, AXES, perm)

    def across_tok(value, p):
        return send(value, lambda t, zz, c: (t ^ (p if c == 0 else mirror(p, n_tok)), zz, c))

    def across_z(value, j):
        return send(value, lambda t, zz, c: (t, zz ^ j, c))

    def across_core(value):
        return send(value, lambda t, zz, c: (t, zz, 1 - c))

    def halve(gate_kept, up_kept, gate_sent, up_sent, after):
        left = n_tok // 2
        gate_parts, up_parts = [gate_kept], [up_kept]
        while True:
            turned = mirror(left, n_tok)
            gate_parts.append(send(gate_sent, lambda t, zz, c: (t ^ left, zz, c)))
            up_parts.append(send(up_sent, lambda t, zz, c: (t ^ turned, zz, c)))
            if left == 1:
                return gate_parts, up_parts
            left //= 2
            gate_sent, up_sent = add_slots(gate_parts, up_parts, left, left, after)

    def gather(part):
        parts, left = [part], 1
        while left < n_tok:
            parts += [across_tok(part, left) for part in parts]
            left *= 2
        return parts

    def combine(mine, theirs):
        paired = across_core(theirs)
        sums = [mine[j] + paired[j].astype(jnp.float32) for j in range(n_z)]
        return sums[0], [part.astype(jnp.bfloat16) for part in sums[1:]]

    rows, features = tokens.shape
    piece = rows // (2 * BATCHES)
    split = tokens.reshape(2, BATCHES, piece, features)
    gate_wide = widen(gate_keep, gate_weight.shape[1])
    up_wide = widen(up_keep, up_weight.shape[1])
    down_wide = widen(down_keep, down_weight.shape[1])
    moved = []
    for s in range(BATCHES):
        block = split[:, s].reshape(2 * piece, features)
        moved.append([send(block, lambda t, zz, c: (zz, t ^ k, c)) for k in range(n_z)])
    sums, before_swap = [], []
    for blocks in moved:
        own = join(blocks, before_swap)
        sums.append(gate_up(place, own, across_core(own), gate_weight, up_weight, gate_wide, up_wide))
        before_swap = [sums[-1][2]]
    out, before_add, before_hidden, before_down = [], [], [], []
    for terms in sums:
        parts = gather(activate(*halve(*terms, before_add), before_hidden))
        mine, theirs = down(place, parts, down_weight, down_wide, before_down)
        total, sent = combine(mine, theirs)
        arrived = [across_z(sent[j - 1], j) for j in range(1, n_z)]
        for part in arrived:
            total += part.astype(jnp.float32)
        out.append(total.astype(jnp.bfloat16))
        before_add, before_hidden, before_down = [parts[1]], sent, arrived
    return jnp.concatenate(out, axis=0)


def solution(mesh):
    n_tok, n_hid = mesh.shape["tok"], mesh.shape["hid"]
    return jax.shard_map(
        functools.partial(local, n_tok, n_hid),
        mesh=mesh,
        in_specs=(
            P("tok", "hid"),
            P("tok", "hid"),
            P("tok", "hid"),
            P("hid", "tok"),
            P("tok", "hid"),
            P("tok", "hid"),
            P("hid", "tok"),
        ),
        out_specs=P("hid", "tok"),
        check_vma=False,
    )
```

```python
import functools

import jax
import jax.numpy as jnp
from jax import lax
from jax.experimental import pallas as pl
from jax.experimental.pallas import tpu as pltpu
from jax.sharding import PartitionSpec as P

AXES = ("tok", "hid")
BATCHES = 2
TILE = 512
VMEM_BYTES = 48 * 1024 * 1024


def masked_product(x_ref, weight_ref, keep_ref):
    block_rows, width = keep_ref.shape
    side = weight_ref.shape[0] // block_rows
    strips = []
    for i in range(block_rows):
        keep = jnp.broadcast_to(keep_ref[i : i + 1, :], (16, width)).astype(jnp.bfloat16)
        block = weight_ref[i * side : (i + 1) * side, :].reshape(side // 16, 16, width)
        strips.append((block * keep[None]).reshape(side, width))
    return jnp.dot(x_ref[...], jnp.concatenate(strips, axis=0), preferred_element_type=jnp.float32)


def widen(keep_mask, width):
    return jnp.repeat(keep_mask.astype(jnp.float32), width // keep_mask.shape[1], axis=1)


def gate_up_kernel(n, place_ref, *refs):
    own, other = refs[:n], refs[n : 2 * n]
    gate_ref, up_ref, gate_keep, up_keep = refs[2 * n : 2 * n + 4]
    outs, x = refs[2 * n + 4 : 2 * n + 8], refs[2 * n + 8]
    _, piece, half = own[0].shape
    rows = 2 * piece

    @pl.when(pl.program_id(0) == 0)
    def _():
        core = place_ref[0]
        mine = pl.ds(pl.multiple_of(core * half, half), half)
        others = pl.ds(pl.multiple_of((1 - core) * half, half), half)
        for k in range(n):
            at = pl.ds(pl.multiple_of(place_ref[1 + n + k] * rows, rows), rows)
            x[at, mine] = own[k][...].reshape(rows, half)
            x[at, others] = other[k][...].reshape(rows, half)

    for which, (weight, keep) in enumerate(((gate_ref, gate_keep), (up_ref, up_keep))):
        product = masked_product(x, weight, keep)
        for p in range(n):
            offset = p if which == 0 else mirror(p, n)
            term = product[offset * rows : (offset + 1) * rows]
            if p < n // 2:
                outs[which][p] = term
            else:
                outs[2 + which][p - n // 2] = term.astype(jnp.bfloat16)


def gate_up(place, batch, own, other, gate_weight, up_weight, gate_keep, up_keep):
    n = len(own)
    _, whole, half = own[0].shape
    piece = whole // BATCHES
    rows = 2 * piece
    depth, width = gate_weight.shape
    tile = min(width, TILE)
    part = pl.BlockSpec((2, piece, half), lambda i, *_: (0, batch, 0))
    strip = pl.BlockSpec((depth, tile), lambda i, *_: (0, i))
    mask = pl.BlockSpec((gate_keep.shape[0], tile), lambda i, *_: (0, i))
    out = pl.BlockSpec((n // 2, rows, tile), lambda i, *_: (0, 0, i))
    return pl.pallas_call(
        functools.partial(gate_up_kernel, n),
        grid_spec=pltpu.PrefetchScalarGridSpec(
            num_scalar_prefetch=1,
            grid=(width // tile,),
            in_specs=[part] * (2 * n) + [strip, strip, mask, mask],
            out_specs=[out] * 4,
            scratch_shapes=[pltpu.VMEM((n * rows, depth), jnp.bfloat16)],
        ),
        out_shape=[jax.ShapeDtypeStruct((n // 2, rows, width), jnp.float32)] * 2
        + [jax.ShapeDtypeStruct((n // 2, rows, width), jnp.bfloat16)] * 2,
        compiler_params=pltpu.CompilerParams(vmem_limit_bytes=VMEM_BYTES),
        cost_estimate=pl.CostEstimate(
            flops=4 * n * rows * depth * width, bytes_accessed=4 * depth * width, transcendentals=0
        ),
        name="gate_up",
    )(place, *own, *other, gate_weight, up_weight, gate_keep, up_keep)


def total_of(refs):
    total = refs[0][...].astype(jnp.float32)
    for ref in refs[1:]:
        total += ref[...].astype(jnp.float32)
    return total


def add_kernel(n, *refs):
    refs[-2][...] = total_of(refs[:n]).astype(jnp.bfloat16)
    refs[-1][...] = total_of(refs[n : 2 * n]).astype(jnp.bfloat16)


def add_slots(gate_parts, up_parts, first, count, after):
    _, rows, width = gate_parts[0].shape
    n = len(gate_parts)
    return pl.pallas_call(
        functools.partial(add_kernel, n),
        grid=(count,),
        in_specs=[pl.BlockSpec((1, rows, width), lambda i: (first + i, 0, 0))] * (2 * n)
        + [pl.BlockSpec(memory_space=pl.ANY)] * len(after),
        out_specs=[pl.BlockSpec((1, rows, width), lambda i: (i, 0, 0))] * 2,
        out_shape=[jax.ShapeDtypeStruct((count, rows, width), jnp.bfloat16)] * 2,
        compiler_params=pltpu.CompilerParams(vmem_limit_bytes=VMEM_BYTES),
        name="add_slots",
    )(*gate_parts, *up_parts, *after)


def activate_kernel(n, *refs):
    gate = total_of(refs[:n])[0]
    up = total_of(refs[n : 2 * n])[0]
    refs[-1][...] = (gate / (1.0 + jnp.exp(-gate)) * up).astype(jnp.bfloat16)


def activate(gate_parts, up_parts, after):
    _, rows, width = gate_parts[0].shape
    tile = width // 2
    n = len(gate_parts)
    return pl.pallas_call(
        functools.partial(activate_kernel, n),
        grid=(width // tile,),
        in_specs=[pl.BlockSpec((1, rows, tile), lambda i: (0, 0, i))] * (2 * n)
        + [pl.BlockSpec(memory_space=pl.ANY)] * len(after),
        out_specs=pl.BlockSpec((rows, tile), lambda i: (0, i)),
        out_shape=jax.ShapeDtypeStruct((rows, width), jnp.bfloat16),
        compiler_params=pltpu.CompilerParams(vmem_limit_bytes=VMEM_BYTES),
        name="hidden",
    )(*gate_parts, *up_parts, *after)


def down_kernel(n, place_ref, *refs):
    parts = refs[:n]
    weight_ref, keep_ref = refs[n : n + 2]
    mine_ref, other_ref, h = refs[-3:]
    rows = parts[0].shape[0]
    step = pl.program_id(0)

    @pl.when(step == 0)
    def _():
        for p in range(n):
            h[p * rows : (p + 1) * rows] = parts[p][...]

    product = masked_product(h, weight_ref, keep_ref)
    core = place_ref[0]
    half = rows // 2
    for p in range(n):
        slot = place_ref[1 + p]
        low = product[p * rows : p * rows + half]
        high = product[p * rows + half : (p + 1) * rows]
        mine_ref[slot] = jnp.where(core == 0, low, high)
        other_ref[slot] = jnp.where(core == 0, high, low).astype(jnp.bfloat16)


def down(place, parts, weight, keep, after):
    n = len(parts)
    rows = parts[0].shape[0]
    depth, width = weight.shape
    tile = min(width, TILE)
    out = pl.BlockSpec((n, rows // 2, tile), lambda i, *_: (0, 0, i))
    return pl.pallas_call(
        functools.partial(down_kernel, n),
        grid_spec=pltpu.PrefetchScalarGridSpec(
            num_scalar_prefetch=1,
            grid=(width // tile,),
            in_specs=[pl.BlockSpec((rows, depth), lambda i, *_: (0, 0))] * n
            + [pl.BlockSpec((depth, tile), lambda i, *_: (0, i))]
            + [pl.BlockSpec((keep.shape[0], tile), lambda i, *_: (0, i))]
            + [pl.BlockSpec(memory_space=pl.ANY)] * len(after),
            out_specs=[out, out],
            scratch_shapes=[pltpu.VMEM((n * rows, depth), jnp.bfloat16)],
        ),
        out_shape=[
            jax.ShapeDtypeStruct((n, rows // 2, width), jnp.float32),
            jax.ShapeDtypeStruct((n, rows // 2, width), jnp.bfloat16),
        ],
        compiler_params=pltpu.CompilerParams(vmem_limit_bytes=VMEM_BYTES),
        cost_estimate=pl.CostEstimate(
            flops=2 * n * rows * depth * width, bytes_accessed=2 * depth * width, transcendentals=0
        ),
        name="down",
    )(place, *parts, weight, keep, *after)


def mirror(p, n):
    out = 0
    while n > 1:
        out, p, n = out * 2 + p % 2, p // 2, n // 2
    return out


def local(n_tok, n_hid, tokens, gate_weight, up_weight, down_weight, gate_keep, up_keep, down_keep):
    n_z = n_hid // 2
    tok, hid = lax.axis_index("tok"), lax.axis_index("hid")
    z, core = hid // 2, hid % 2
    offsets = [jnp.where(core == 0, p, mirror(p, n_tok)) for p in range(n_tok)]
    place = jnp.stack([core] + [tok ^ z ^ off for off in offsets] + [tok ^ z ^ k for k in range(n_z)])
    place = place.astype(jnp.int32)

    def send(value, to):
        perm = []
        for t in range(n_tok):
            for zz in range(n_z):
                for c in range(2):
                    a, b, d = to(t, zz, c)
                    perm.append((t * n_hid + zz * 2 + c, a * n_hid + b * 2 + d))
        return lax.ppermute(value, AXES, perm)

    def across_tok(value, p):
        return send(value, lambda t, zz, c: (t ^ (p if c == 0 else mirror(p, n_tok)), zz, c))

    def across_z(value, j):
        return send(value, lambda t, zz, c: (t, zz ^ j, c))

    def across_core(value):
        return send(value, lambda t, zz, c: (t, zz, 1 - c))

    def halve(gate_kept, up_kept, gate_sent, up_sent, after):
        left = n_tok // 2
        gate_parts, up_parts = [gate_kept], [up_kept]
        while True:
            turned = mirror(left, n_tok)
            gate_parts.append(send(gate_sent, lambda t, zz, c: (t ^ left, zz, c)))
            up_parts.append(send(up_sent, lambda t, zz, c: (t ^ turned, zz, c)))
            if left == 1:
                return gate_parts, up_parts
            left //= 2
            gate_sent, up_sent = add_slots(gate_parts, up_parts, left, left, after)

    def gather(part):
        parts, left = [part], 1
        while left < n_tok:
            parts += [across_tok(part, left) for part in parts]
            left *= 2
        return parts

    def combine(mine, theirs):
        paired = across_core(theirs)
        sums = [mine[j] + paired[j].astype(jnp.float32) for j in range(n_z)]
        return sums[0], [part.astype(jnp.bfloat16) for part in sums[1:]]

    rows, features = tokens.shape
    gate_wide = widen(gate_keep, gate_weight.shape[1])
    up_wide = widen(up_keep, up_weight.shape[1])
    down_wide = widen(down_keep, down_weight.shape[1])
    moved = [send(tokens, lambda t, zz, c: (zz, t ^ k, c)) for k in range(n_z)]
    swapped = [across_core(block) for block in moved]
    own = [block.reshape(2, rows // 2, features) for block in moved]
    other = [block.reshape(2, rows // 2, features) for block in swapped]
    sums = [gate_up(place, s, own, other, gate_weight, up_weight, gate_wide, up_wide) for s in range(BATCHES)]
    out, before_add, before_hidden, before_down = [], [], [], []
    for s, terms in enumerate(sums):
        before_add += [later[2] for later in sums[s + 1 : s + 2]]
        parts = gather(activate(*halve(*terms, before_add), before_hidden))
        mine, theirs = down(place, parts, down_weight, down_wide, before_down)
        total, sent = combine(mine, theirs)
        arrived = [across_z(sent[j - 1], j) for j in range(1, n_z)]
        for part in arrived:
            total += part.astype(jnp.float32)
        out.append(total.astype(jnp.bfloat16))
        before_add, before_hidden, before_down = [parts[1]], sent, arrived
    return jnp.concatenate(out, axis=0)


def solution(mesh):
    n_tok, n_hid = mesh.shape["tok"], mesh.shape["hid"]
    return jax.shard_map(
        functools.partial(local, n_tok, n_hid),
        mesh=mesh,
        in_specs=(
            P("tok", "hid"),
            P("tok", "hid"),
            P("tok", "hid"),
            P("hid", "tok"),
            P("tok", "hid"),
            P("tok", "hid"),
            P("hid", "tok"),
        ),
        out_specs=P("hid", "tok"),
        check_vma=False,
    )
```

```python
import functools

import jax
import jax.numpy as jnp
from jax import lax
from jax.experimental import pallas as pl
from jax.experimental.pallas import tpu as pltpu
from jax.sharding import PartitionSpec as P

AXES = ("tok", "hid")
BATCHES = 2
TILE = 512
VMEM_BYTES = 48 * 1024 * 1024


def masked_product(x_ref, weight_ref, keep_ref):
    block_rows, width = keep_ref.shape
    side = weight_ref.shape[0] // block_rows
    strips = []
    for i in range(block_rows):
        keep = jnp.broadcast_to(keep_ref[i : i + 1, :], (16, width)).astype(jnp.bfloat16)
        block = weight_ref[i * side : (i + 1) * side, :].reshape(side // 16, 16, width)
        strips.append((block * keep[None]).reshape(side, width))
    return jnp.dot(x_ref[...], jnp.concatenate(strips, axis=0), preferred_element_type=jnp.float32)


def widen(keep_mask, width):
    return jnp.repeat(keep_mask.astype(jnp.float32), width // keep_mask.shape[1], axis=1)


def gate_up_kernel(place_ref, own_ref, other_ref, gate_ref, up_ref, gate_keep, up_keep, *refs):
    outs, x = refs[:4], refs[4]
    n, rows, half = own_ref.shape

    @pl.when(pl.program_id(0) == 0)
    def _():
        core = place_ref[0]
        mine = pl.ds(pl.multiple_of(core * half, half), half)
        others = pl.ds(pl.multiple_of((1 - core) * half, half), half)
        for k in range(n):
            at = pl.ds(pl.multiple_of(place_ref[1 + n + k] * rows, rows), rows)
            x[at, mine] = own_ref[k]
            x[at, others] = other_ref[k]

    for which, (weight, keep) in enumerate(((gate_ref, gate_keep), (up_ref, up_keep))):
        product = masked_product(x, weight, keep)
        for p in range(n):
            offset = p if which == 0 else mirror(p, n)
            term = product[offset * rows : (offset + 1) * rows]
            if p < n // 2:
                outs[which][p] = term
            else:
                outs[2 + which][p - n // 2] = term.astype(jnp.bfloat16)


def gate_up(place, own, other, gate_weight, up_weight, gate_keep, up_keep):
    n, rows, half = own.shape
    depth, width = gate_weight.shape
    tile = min(width, TILE)
    whole = pl.BlockSpec((n, rows, half), lambda i, *_: (0, 0, 0))
    strip = pl.BlockSpec((depth, tile), lambda i, *_: (0, i))
    mask = pl.BlockSpec((gate_keep.shape[0], tile), lambda i, *_: (0, i))
    out = pl.BlockSpec((n // 2, rows, tile), lambda i, *_: (0, 0, i))
    return pl.pallas_call(
        gate_up_kernel,
        grid_spec=pltpu.PrefetchScalarGridSpec(
            num_scalar_prefetch=1,
            grid=(width // tile,),
            in_specs=[whole, whole, strip, strip, mask, mask],
            out_specs=[out] * 4,
            scratch_shapes=[pltpu.VMEM((n * rows, depth), jnp.bfloat16)],
        ),
        out_shape=[jax.ShapeDtypeStruct((n // 2, rows, width), jnp.float32)] * 2
        + [jax.ShapeDtypeStruct((n // 2, rows, width), jnp.bfloat16)] * 2,
        compiler_params=pltpu.CompilerParams(vmem_limit_bytes=VMEM_BYTES),
        cost_estimate=pl.CostEstimate(
            flops=4 * n * rows * depth * width, bytes_accessed=4 * depth * width, transcendentals=0
        ),
        name="gate_up",
    )(place, own, other, gate_weight, up_weight, gate_keep, up_keep)


def total_of(refs):
    total = refs[0][...].astype(jnp.float32)
    for ref in refs[1:]:
        total += ref[...].astype(jnp.float32)
    return total


def add_kernel(n, *refs):
    refs[-2][...] = total_of(refs[:n]).astype(jnp.bfloat16)
    refs[-1][...] = total_of(refs[n : 2 * n]).astype(jnp.bfloat16)


def add_slots(gate_parts, up_parts, first, count, after):
    _, rows, width = gate_parts[0].shape
    n = len(gate_parts)
    return pl.pallas_call(
        functools.partial(add_kernel, n),
        grid=(count,),
        in_specs=[pl.BlockSpec((1, rows, width), lambda i: (first + i, 0, 0))] * (2 * n)
        + [pl.BlockSpec(memory_space=pl.ANY)] * len(after),
        out_specs=[pl.BlockSpec((1, rows, width), lambda i: (i, 0, 0))] * 2,
        out_shape=[jax.ShapeDtypeStruct((count, rows, width), jnp.bfloat16)] * 2,
        compiler_params=pltpu.CompilerParams(vmem_limit_bytes=VMEM_BYTES),
        name="add_slots",
    )(*gate_parts, *up_parts, *after)


def activate_kernel(n, *refs):
    gate = total_of(refs[:n])[0]
    up = total_of(refs[n : 2 * n])[0]
    refs[-1][...] = (gate / (1.0 + jnp.exp(-gate)) * up).astype(jnp.bfloat16)


def activate(gate_parts, up_parts, after):
    _, rows, width = gate_parts[0].shape
    tile = width // 2
    n = len(gate_parts)
    return pl.pallas_call(
        functools.partial(activate_kernel, n),
        grid=(width // tile,),
        in_specs=[pl.BlockSpec((1, rows, tile), lambda i: (0, 0, i))] * (2 * n)
        + [pl.BlockSpec(memory_space=pl.ANY)] * len(after),
        out_specs=pl.BlockSpec((rows, tile), lambda i: (0, i)),
        out_shape=jax.ShapeDtypeStruct((rows, width), jnp.bfloat16),
        compiler_params=pltpu.CompilerParams(vmem_limit_bytes=VMEM_BYTES),
        name="hidden",
    )(*gate_parts, *up_parts, *after)


def down_kernel(n, place_ref, *refs):
    parts = refs[:n]
    weight_ref, keep_ref = refs[n : n + 2]
    mine_ref, other_ref, h = refs[-3:]
    rows = parts[0].shape[0]
    step = pl.program_id(0)

    @pl.when(step == 0)
    def _():
        for p in range(n):
            h[p * rows : (p + 1) * rows] = parts[p][...]

    product = masked_product(h, weight_ref, keep_ref)
    core = place_ref[0]
    half = rows // 2
    for p in range(n):
        slot = place_ref[1 + p]
        low = product[p * rows : p * rows + half]
        high = product[p * rows + half : (p + 1) * rows]
        mine_ref[slot] = jnp.where(core == 0, low, high)
        other_ref[slot] = jnp.where(core == 0, high, low).astype(jnp.bfloat16)


def down(place, parts, weight, keep, after):
    n = len(parts)
    rows = parts[0].shape[0]
    depth, width = weight.shape
    tile = min(width, TILE)
    out = pl.BlockSpec((n, rows // 2, tile), lambda i, *_: (0, 0, i))
    return pl.pallas_call(
        functools.partial(down_kernel, n),
        grid_spec=pltpu.PrefetchScalarGridSpec(
            num_scalar_prefetch=1,
            grid=(width // tile,),
            in_specs=[pl.BlockSpec((rows, depth), lambda i, *_: (0, 0))] * n
            + [pl.BlockSpec((depth, tile), lambda i, *_: (0, i))]
            + [pl.BlockSpec((keep.shape[0], tile), lambda i, *_: (0, i))]
            + [pl.BlockSpec(memory_space=pl.ANY)] * len(after),
            out_specs=[out, out],
            scratch_shapes=[pltpu.VMEM((n * rows, depth), jnp.bfloat16)],
        ),
        out_shape=[
            jax.ShapeDtypeStruct((n, rows // 2, width), jnp.float32),
            jax.ShapeDtypeStruct((n, rows // 2, width), jnp.bfloat16),
        ],
        compiler_params=pltpu.CompilerParams(vmem_limit_bytes=VMEM_BYTES),
        cost_estimate=pl.CostEstimate(
            flops=2 * n * rows * depth * width, bytes_accessed=2 * depth * width, transcendentals=0
        ),
        name="down",
    )(place, *parts, weight, keep, *after)


def join_kernel(n, *refs):
    for k in range(n):
        refs[-1][k] = refs[k][...]


def join(blocks, after):
    n = len(blocks)
    spec = pl.BlockSpec(memory_space=pltpu.VMEM)
    return pl.pallas_call(
        functools.partial(join_kernel, n),
        in_specs=[spec] * n + [pl.BlockSpec(memory_space=pl.ANY)] * len(after),
        out_specs=spec,
        out_shape=jax.ShapeDtypeStruct((n,) + blocks[0].shape, blocks[0].dtype),
        compiler_params=pltpu.CompilerParams(vmem_limit_bytes=VMEM_BYTES),
        name="join",
    )(*blocks, *after)


def hold_kernel(value_ref, *refs):
    refs[-1][...] = value_ref[...]


def hold(value, after):
    if not after:
        return value
    spec = pl.BlockSpec(memory_space=pltpu.VMEM)
    return pl.pallas_call(
        hold_kernel,
        in_specs=[spec] + [pl.BlockSpec(memory_space=pl.ANY)] * len(after),
        out_specs=spec,
        out_shape=jax.ShapeDtypeStruct(value.shape, value.dtype),
        compiler_params=pltpu.CompilerParams(vmem_limit_bytes=VMEM_BYTES),
        name="hold",
    )(value, *after)


def mirror(p, n):
    out = 0
    while n > 1:
        out, p, n = out * 2 + p % 2, p // 2, n // 2
    return out


def local(n_tok, n_hid, tokens, gate_weight, up_weight, down_weight, gate_keep, up_keep, down_keep):
    n_z = n_hid // 2
    tok, hid = lax.axis_index("tok"), lax.axis_index("hid")
    z, core = hid // 2, hid % 2
    offsets = [jnp.where(core == 0, p, mirror(p, n_tok)) for p in range(n_tok)]
    place = jnp.stack([core] + [tok ^ z ^ off for off in offsets] + [tok ^ z ^ k for k in range(n_z)])
    place = place.astype(jnp.int32)

    def send(value, to):
        perm = []
        for t in range(n_tok):
            for zz in range(n_z):
                for c in range(2):
                    a, b, d = to(t, zz, c)
                    perm.append((t * n_hid + zz * 2 + c, a * n_hid + b * 2 + d))
        return lax.ppermute(value, AXES, perm)

    def across_tok(value, p):
        return send(value, lambda t, zz, c: (t ^ (p if c == 0 else mirror(p, n_tok)), zz, c))

    def across_z(value, j):
        return send(value, lambda t, zz, c: (t, zz ^ j, c))

    def across_core(value):
        return send(value, lambda t, zz, c: (t, zz, 1 - c))

    def halve(gate_kept, up_kept, gate_sent, up_sent, after):
        left = n_tok // 2
        gate_parts, up_parts = [gate_kept], [up_kept]
        while True:
            turned = mirror(left, n_tok)
            gate_parts.append(send(gate_sent, lambda t, zz, c: (t ^ left, zz, c)))
            up_parts.append(send(up_sent, lambda t, zz, c: (t ^ turned, zz, c)))
            if left == 1:
                return gate_parts, up_parts
            left //= 2
            gate_sent, up_sent = add_slots(gate_parts, up_parts, left, left, after)

    def gather(part):
        parts, left = [part], 1
        while left < n_tok:
            parts += [across_tok(part, left) for part in parts]
            left *= 2
        return parts

    def combine(mine, theirs):
        paired = across_core(theirs)
        sums = [mine[j] + paired[j].astype(jnp.float32) for j in range(n_z)]
        return sums[0], [part.astype(jnp.bfloat16) for part in sums[1:]]

    rows, features = tokens.shape
    gate_wide = widen(gate_keep, gate_weight.shape[1])
    up_wide = widen(up_keep, up_weight.shape[1])
    down_wide = widen(down_keep, down_weight.shape[1])
    piece = rows // (2 * BATCHES)
    split = tokens.reshape(2, BATCHES, piece, features)
    moved = []
    for s in range(BATCHES):
        block = split[:, s].reshape(2 * piece, features)
        moved.append([send(block, lambda t, zz, c: (zz, t ^ k, c)) for k in range(n_z)])
    sums, before = [], []
    for s in range(BATCHES):
        own = join(moved[s], before)
        gate_kept, up_kept, gate_sent, up_sent = gate_up(
            place, own, across_core(own), gate_weight, up_weight, gate_wide, up_wide
        )
        gate_sent = hold(gate_sent, [part for later in moved[s + 1 : s + 2] for part in later])
        sums.append((gate_kept, up_kept, gate_sent, up_sent))
        before = [gate_sent]
    hidden = [gather(activate(*halve(*terms, ()), ())) for terms in sums]
    out, arrived = [], []
    for s, parts in enumerate(hidden):
        mine, theirs = down(place, parts, down_weight, down_wide, [later[1] for later in hidden[s + 1 : s + 2]])
        total, sent = combine(mine, hold(theirs, arrived))
        arrived = [across_z(sent[j - 1], j) for j in range(1, n_z)]
        for part in arrived:
            total += part.astype(jnp.float32)
        out.append(total.astype(jnp.bfloat16))
    return jnp.concatenate(out, axis=0)


def solution(mesh):
    n_tok, n_hid = mesh.shape["tok"], mesh.shape["hid"]
    return jax.shard_map(
        functools.partial(local, n_tok, n_hid),
        mesh=mesh,
        in_specs=(
            P("tok", "hid"),
            P("tok", "hid"),
            P("tok", "hid"),
            P("hid", "tok"),
            P("tok", "hid"),
            P("tok", "hid"),
            P("hid", "tok"),
        ),
        out_specs=P("hid", "tok"),
        check_vma=False,
    )
```

```python
import functools

import jax
import jax.numpy as jnp
from jax import lax
from jax.experimental import pallas as pl
from jax.experimental.pallas import tpu as pltpu
from jax.sharding import PartitionSpec as P

AXES = ("tok", "hid")
BATCHES = 2
TILE = 512
VMEM_BYTES = 48 * 1024 * 1024


def masked_product(x_ref, weight_ref, keep_ref):
    block_rows, width = keep_ref.shape
    side = weight_ref.shape[0] // block_rows
    strips = []
    for i in range(block_rows):
        keep = jnp.broadcast_to(keep_ref[i : i + 1, :], (16, width)).astype(jnp.bfloat16)
        block = weight_ref[i * side : (i + 1) * side, :].reshape(side // 16, 16, width)
        strips.append((block * keep[None]).reshape(side, width))
    return jnp.dot(x_ref[...], jnp.concatenate(strips, axis=0), preferred_element_type=jnp.float32)


def widen(keep_mask, width):
    return jnp.repeat(keep_mask.astype(jnp.float32), width // keep_mask.shape[1], axis=1)


def gate_up_kernel(place_ref, own_ref, other_ref, gate_ref, up_ref, gate_keep, up_keep, *refs):
    outs, x = refs[:4], refs[4]
    n, rows, half = own_ref.shape

    @pl.when(pl.program_id(0) == 0)
    def _():
        core = place_ref[0]
        mine = pl.ds(pl.multiple_of(core * half, half), half)
        others = pl.ds(pl.multiple_of((1 - core) * half, half), half)
        for k in range(n):
            at = pl.ds(pl.multiple_of(place_ref[1 + n + k] * rows, rows), rows)
            x[at, mine] = own_ref[k]
            x[at, others] = other_ref[k]

    for which, (weight, keep) in enumerate(((gate_ref, gate_keep), (up_ref, up_keep))):
        product = masked_product(x, weight, keep)
        for p in range(n):
            offset = p if which == 0 else mirror(p, n)
            term = product[offset * rows : (offset + 1) * rows]
            if p < n // 2:
                outs[which][p] = term
            else:
                outs[2 + which][p - n // 2] = term.astype(jnp.bfloat16)


def gate_up(place, own, other, gate_weight, up_weight, gate_keep, up_keep):
    n, rows, half = own.shape
    depth, width = gate_weight.shape
    tile = min(width, TILE)
    whole = pl.BlockSpec((n, rows, half), lambda i, *_: (0, 0, 0))
    strip = pl.BlockSpec((depth, tile), lambda i, *_: (0, i))
    mask = pl.BlockSpec((gate_keep.shape[0], tile), lambda i, *_: (0, i))
    out = pl.BlockSpec((n // 2, rows, tile), lambda i, *_: (0, 0, i))
    return pl.pallas_call(
        gate_up_kernel,
        grid_spec=pltpu.PrefetchScalarGridSpec(
            num_scalar_prefetch=1,
            grid=(width // tile,),
            in_specs=[whole, whole, strip, strip, mask, mask],
            out_specs=[out] * 4,
            scratch_shapes=[pltpu.VMEM((n * rows, depth), jnp.bfloat16)],
        ),
        out_shape=[jax.ShapeDtypeStruct((n // 2, rows, width), jnp.float32)] * 2
        + [jax.ShapeDtypeStruct((n // 2, rows, width), jnp.bfloat16)] * 2,
        compiler_params=pltpu.CompilerParams(vmem_limit_bytes=VMEM_BYTES),
        cost_estimate=pl.CostEstimate(
            flops=4 * n * rows * depth * width, bytes_accessed=4 * depth * width, transcendentals=0
        ),
        name="gate_up",
    )(place, own, other, gate_weight, up_weight, gate_keep, up_keep)


def total_of(refs):
    total = refs[0][...].astype(jnp.float32)
    for ref in refs[1:]:
        total += ref[...].astype(jnp.float32)
    return total


def add_kernel(n, *refs):
    refs[-2][...] = total_of(refs[:n]).astype(jnp.bfloat16)
    refs[-1][...] = total_of(refs[n : 2 * n]).astype(jnp.bfloat16)


def add_slots(gate_parts, up_parts, first, count, after):
    _, rows, width = gate_parts[0].shape
    n = len(gate_parts)
    return pl.pallas_call(
        functools.partial(add_kernel, n),
        grid=(count,),
        in_specs=[pl.BlockSpec((1, rows, width), lambda i: (first + i, 0, 0))] * (2 * n)
        + [pl.BlockSpec(memory_space=pl.ANY)] * len(after),
        out_specs=[pl.BlockSpec((1, rows, width), lambda i: (i, 0, 0))] * 2,
        out_shape=[jax.ShapeDtypeStruct((count, rows, width), jnp.bfloat16)] * 2,
        compiler_params=pltpu.CompilerParams(vmem_limit_bytes=VMEM_BYTES),
        name="add_slots",
    )(*gate_parts, *up_parts, *after)


def activate_kernel(n, *refs):
    gate = total_of(refs[:n])[0]
    up = total_of(refs[n : 2 * n])[0]
    refs[-1][...] = (gate / (1.0 + jnp.exp(-gate)) * up).astype(jnp.bfloat16)


def activate(gate_parts, up_parts, after):
    _, rows, width = gate_parts[0].shape
    tile = width // 2
    n = len(gate_parts)
    return pl.pallas_call(
        functools.partial(activate_kernel, n),
        grid=(width // tile,),
        in_specs=[pl.BlockSpec((1, rows, tile), lambda i: (0, 0, i))] * (2 * n)
        + [pl.BlockSpec(memory_space=pl.ANY)] * len(after),
        out_specs=pl.BlockSpec((rows, tile), lambda i: (0, i)),
        out_shape=jax.ShapeDtypeStruct((rows, width), jnp.bfloat16),
        compiler_params=pltpu.CompilerParams(vmem_limit_bytes=VMEM_BYTES),
        name="hidden",
    )(*gate_parts, *up_parts, *after)


def down_kernel(n, place_ref, *refs):
    parts = refs[:n]
    weight_ref, keep_ref = refs[n : n + 2]
    mine_ref, other_ref, h = refs[-3:]
    rows = parts[0].shape[0]
    step = pl.program_id(0)

    @pl.when(step == 0)
    def _():
        for p in range(n):
            h[p * rows : (p + 1) * rows] = parts[p][...]

    product = masked_product(h, weight_ref, keep_ref)
    core = place_ref[0]
    half = rows // 2
    for p in range(n):
        slot = place_ref[1 + p]
        low = product[p * rows : p * rows + half]
        high = product[p * rows + half : (p + 1) * rows]
        mine_ref[slot] = jnp.where(core == 0, low, high)
        other_ref[slot] = jnp.where(core == 0, high, low).astype(jnp.bfloat16)


def down(place, parts, weight, keep, after):
    n = len(parts)
    rows = parts[0].shape[0]
    depth, width = weight.shape
    tile = min(width, TILE)
    out = pl.BlockSpec((n, rows // 2, tile), lambda i, *_: (0, 0, i))
    return pl.pallas_call(
        functools.partial(down_kernel, n),
        grid_spec=pltpu.PrefetchScalarGridSpec(
            num_scalar_prefetch=1,
            grid=(width // tile,),
            in_specs=[pl.BlockSpec((rows, depth), lambda i, *_: (0, 0))] * n
            + [pl.BlockSpec((depth, tile), lambda i, *_: (0, i))]
            + [pl.BlockSpec((keep.shape[0], tile), lambda i, *_: (0, i))]
            + [pl.BlockSpec(memory_space=pl.ANY)] * len(after),
            out_specs=[out, out],
            scratch_shapes=[pltpu.VMEM((n * rows, depth), jnp.bfloat16)],
        ),
        out_shape=[
            jax.ShapeDtypeStruct((n, rows // 2, width), jnp.float32),
            jax.ShapeDtypeStruct((n, rows // 2, width), jnp.bfloat16),
        ],
        compiler_params=pltpu.CompilerParams(vmem_limit_bytes=VMEM_BYTES),
        cost_estimate=pl.CostEstimate(
            flops=2 * n * rows * depth * width, bytes_accessed=2 * depth * width, transcendentals=0
        ),
        name="down",
    )(place, *parts, weight, keep, *after)


def join_kernel(n, *refs):
    for k in range(n):
        refs[-1][k] = refs[k][...]


def join(blocks, after):
    n = len(blocks)
    spec = pl.BlockSpec(memory_space=pltpu.VMEM)
    return pl.pallas_call(
        functools.partial(join_kernel, n),
        in_specs=[spec] * n + [pl.BlockSpec(memory_space=pl.ANY)] * len(after),
        out_specs=spec,
        out_shape=jax.ShapeDtypeStruct((n,) + blocks[0].shape, blocks[0].dtype),
        compiler_params=pltpu.CompilerParams(vmem_limit_bytes=VMEM_BYTES),
        name="join",
    )(*blocks, *after)


def hold_kernel(value_ref, *refs):
    refs[-1][...] = value_ref[...]


def hold(value, after):
    if not after:
        return value
    spec = pl.BlockSpec(memory_space=pltpu.VMEM)
    return pl.pallas_call(
        hold_kernel,
        in_specs=[spec] + [pl.BlockSpec(memory_space=pl.ANY)] * len(after),
        out_specs=spec,
        out_shape=jax.ShapeDtypeStruct(value.shape, value.dtype),
        compiler_params=pltpu.CompilerParams(vmem_limit_bytes=VMEM_BYTES),
        name="hold",
    )(value, *after)


def mirror(p, n):
    out = 0
    while n > 1:
        out, p, n = out * 2 + p % 2, p // 2, n // 2
    return out


def local(n_tok, n_hid, tokens, gate_weight, up_weight, down_weight, gate_keep, up_keep, down_keep):
    n_z = n_hid // 2
    tok, hid = lax.axis_index("tok"), lax.axis_index("hid")
    z, core = hid // 2, hid % 2
    offsets = [jnp.where(core == 0, p, mirror(p, n_tok)) for p in range(n_tok)]
    place = jnp.stack([core] + [tok ^ z ^ off for off in offsets] + [tok ^ z ^ k for k in range(n_z)])
    place = place.astype(jnp.int32)

    def send(value, to):
        perm = []
        for t in range(n_tok):
            for zz in range(n_z):
                for c in range(2):
                    a, b, d = to(t, zz, c)
                    perm.append((t * n_hid + zz * 2 + c, a * n_hid + b * 2 + d))
        return lax.ppermute(value, AXES, perm)

    def across_tok(value, p):
        return send(value, lambda t, zz, c: (t ^ (p if c == 0 else mirror(p, n_tok)), zz, c))

    def across_z(value, j):
        return send(value, lambda t, zz, c: (t, zz ^ j, c))

    def across_core(value):
        return send(value, lambda t, zz, c: (t, zz, 1 - c))

    def halve(gate_kept, up_kept, gate_sent, up_sent, after):
        left = n_tok // 2
        gate_parts, up_parts = [gate_kept], [up_kept]
        while True:
            turned = mirror(left, n_tok)
            gate_parts.append(send(gate_sent, lambda t, zz, c: (t ^ left, zz, c)))
            up_parts.append(send(up_sent, lambda t, zz, c: (t ^ turned, zz, c)))
            if left == 1:
                return gate_parts, up_parts, gate_sent
            left //= 2
            gate_sent, up_sent = add_slots(gate_parts, up_parts, left, left, after)

    def gather(part):
        parts, left = [part], 1
        while left < n_tok:
            parts += [across_tok(part, left) for part in parts]
            left *= 2
        return parts

    def combine(mine, theirs):
        paired = across_core(theirs)
        sums = [mine[j] + paired[j].astype(jnp.float32) for j in range(n_z)]
        return sums[0], [part.astype(jnp.bfloat16) for part in sums[1:]]

    rows, features = tokens.shape
    gate_wide = widen(gate_keep, gate_weight.shape[1])
    up_wide = widen(up_keep, up_weight.shape[1])
    down_wide = widen(down_keep, down_weight.shape[1])
    piece = rows // (2 * BATCHES)
    split = tokens.reshape(2, BATCHES, piece, features)
    moved = []
    for s in range(BATCHES):
        block = split[:, s].reshape(2 * piece, features)
        moved.append([send(block, lambda t, zz, c: (zz, t ^ k, c)) for k in range(n_z)])
    sums, before = [], []
    for s in range(BATCHES):
        own = join(moved[s], before)
        gate_kept, up_kept, gate_sent, up_sent = gate_up(
            place, own, across_core(own), gate_weight, up_weight, gate_wide, up_wide
        )
        gate_sent = hold(gate_sent, [part for later in moved[s + 1 : s + 2] for part in later])
        sums.append((gate_kept, up_kept, gate_sent, up_sent))
        before = [gate_sent]
    out, beside = [], []
    halved = halve(*sums[0], [later[2] for later in sums[1:2]])
    for s in range(BATCHES):
        gate_parts, up_parts, _ = halved
        parts = gather(activate(gate_parts, up_parts, ()))
        before_down = []
        if s + 1 < BATCHES:
            halved = halve(*sums[s + 1], [parts[1]] + [later[2] for later in sums[s + 2 : s + 3]])
            before_down = [halved[2]]
            beside = beside + [halved[0][-1], halved[1][-1]]
        mine, theirs = down(place, parts, down_weight, down_wide, before_down)
        total, sent = combine(mine, hold(theirs, beside))
        beside = [across_z(sent[j - 1], j) for j in range(1, n_z)]
        for part in beside:
            total += part.astype(jnp.float32)
        out.append(total.astype(jnp.bfloat16))
    return jnp.concatenate(out, axis=0)


def solution(mesh):
    n_tok, n_hid = mesh.shape["tok"], mesh.shape["hid"]
    return jax.shard_map(
        functools.partial(local, n_tok, n_hid),
        mesh=mesh,
        in_specs=(
            P("tok", "hid"),
            P("tok", "hid"),
            P("tok", "hid"),
            P("hid", "tok"),
            P("tok", "hid"),
            P("tok", "hid"),
            P("hid", "tok"),
        ),
        out_specs=P("hid", "tok"),
        check_vma=False,
    )
```

```python
import functools

import jax
import jax.numpy as jnp
from jax import lax
from jax.experimental import pallas as pl
from jax.experimental.pallas import tpu as pltpu
from jax.sharding import PartitionSpec as P

AXES = ("tok", "hid")
BATCHES = 2
TILE = 512
VMEM_BYTES = 44 * 1024 * 1024


def masked_product(x_ref, weight_ref, keep_ref):
    block_rows, width = keep_ref.shape
    side = weight_ref.shape[0] // block_rows
    strips = []
    for i in range(block_rows):
        keep = jnp.broadcast_to(keep_ref[i : i + 1, :], (16, width)).astype(jnp.bfloat16)
        block = weight_ref[i * side : (i + 1) * side, :].reshape(side // 16, 16, width)
        strips.append((block * keep[None]).reshape(side, width))
    return jnp.dot(x_ref[...], jnp.concatenate(strips, axis=0), preferred_element_type=jnp.float32)


def widen(keep_mask, width):
    return jnp.repeat(keep_mask.astype(jnp.float32), width // keep_mask.shape[1], axis=1)


def project_kernel(n, place_ref, *refs):
    own, other = refs[:n], refs[n : 2 * n]
    weight_ref, mask_ref = refs[2 * n : 2 * n + 2]
    kept_ref, sent_ref, x = refs[-3:]
    rows, half = own[0].shape

    @pl.when(pl.program_id(0) == 0)
    def _():
        core = place_ref[0]
        mine = pl.ds(pl.multiple_of(core * half, half), half)
        others = pl.ds(pl.multiple_of((1 - core) * half, half), half)
        for k in range(n):
            at = pl.ds(pl.multiple_of(place_ref[1 + n + k] * rows, rows), rows)
            x[at, mine] = own[k][...]
            x[at, others] = other[k][...]

    product = masked_product(x, weight_ref, mask_ref)
    for p in range(n // 2):
        q = p + n // 2
        kept_ref[p] = product[p * rows : (p + 1) * rows]
        sent_ref[p] = product[q * rows : (q + 1) * rows].astype(jnp.bfloat16)


def project(place, own, other, weight, keep, after):
    n = len(own)
    rows, half = own[0].shape
    depth, width = weight.shape
    tile = min(width, TILE)
    part = pl.BlockSpec((rows, half), lambda i, *_: (0, 0))
    out = pl.BlockSpec((n // 2, rows, tile), lambda i, *_: (0, 0, i))
    return pl.pallas_call(
        functools.partial(project_kernel, n),
        grid_spec=pltpu.PrefetchScalarGridSpec(
            num_scalar_prefetch=1,
            grid=(width // tile,),
            in_specs=[part] * (2 * n)
            + [pl.BlockSpec((depth, tile), lambda i, *_: (0, i))]
            + [pl.BlockSpec((keep.shape[0], tile), lambda i, *_: (0, i))]
            + [pl.BlockSpec(memory_space=pl.ANY)] * len(after),
            out_specs=[out, out],
            scratch_shapes=[pltpu.VMEM((n * rows, depth), jnp.bfloat16)],
        ),
        out_shape=[
            jax.ShapeDtypeStruct((n // 2, rows, width), jnp.float32),
            jax.ShapeDtypeStruct((n // 2, rows, width), jnp.bfloat16),
        ],
        compiler_params=pltpu.CompilerParams(vmem_limit_bytes=VMEM_BYTES),
        cost_estimate=pl.CostEstimate(
            flops=2 * n * rows * depth * width, bytes_accessed=2 * depth * width, transcendentals=0
        ),
        name="project",
    )(place, *own, *other, weight, keep, *after)


def total_of(refs):
    total = refs[0][...].astype(jnp.float32)
    for ref in refs[1:]:
        total += ref[...].astype(jnp.float32)
    return total


def add_kernel(n, *refs):
    refs[-1][...] = total_of(refs[:n]).astype(jnp.bfloat16)


def add_slots(parts, first, count, after):
    _, rows, width = parts[0].shape
    n = len(parts)
    return pl.pallas_call(
        functools.partial(add_kernel, n),
        grid=(count,),
        in_specs=[pl.BlockSpec((1, rows, width), lambda i: (first + i, 0, 0))] * n
        + [pl.BlockSpec(memory_space=pl.ANY)] * len(after),
        out_specs=pl.BlockSpec((1, rows, width), lambda i: (i, 0, 0)),
        out_shape=jax.ShapeDtypeStruct((count, rows, width), jnp.bfloat16),
        compiler_params=pltpu.CompilerParams(vmem_limit_bytes=VMEM_BYTES),
        name="add_slots",
    )(*parts, *after)


def activate_kernel(n, *refs):
    gate = total_of(refs[:n])
    up = total_of(refs[n : 2 * n])
    result = gate / (1.0 + jnp.exp(-gate)) * up
    refs[-1][...] = result.reshape(refs[-1].shape).astype(jnp.bfloat16)


def activate(gate_parts, up_parts, batch):
    _, rows, width = gate_parts[0].shape
    tile = width // 2
    n = len(gate_parts)
    piece = rows // (2 * BATCHES)
    parts = [part.reshape(part.shape[0] * 2, rows // 2, width) for part in gate_parts + up_parts]
    return pl.pallas_call(
        functools.partial(activate_kernel, n),
        grid=(width // tile,),
        in_specs=[pl.BlockSpec((2, piece, tile), lambda i: (0, batch, i))] * (2 * n),
        out_specs=pl.BlockSpec((2 * piece, tile), lambda i: (0, i)),
        out_shape=jax.ShapeDtypeStruct((2 * piece, width), jnp.bfloat16),
        compiler_params=pltpu.CompilerParams(vmem_limit_bytes=VMEM_BYTES),
        name="hidden",
    )(*parts)


def down_kernel(n, place_ref, *refs):
    parts = refs[:n]
    weight_ref, keep_ref = refs[n : n + 2]
    mine_ref, other_ref, h = refs[-3:]
    rows = parts[0].shape[0]
    step = pl.program_id(0)

    @pl.when(step == 0)
    def _():
        for p in range(n):
            h[p * rows : (p + 1) * rows] = parts[p][...]

    product = masked_product(h, weight_ref, keep_ref)
    core = place_ref[0]
    half = rows // 2
    for p in range(n):
        slot = place_ref[1 + p]
        low = product[p * rows : p * rows + half]
        high = product[p * rows + half : (p + 1) * rows]
        mine_ref[slot] = jnp.where(core == 0, low, high)
        other_ref[slot] = jnp.where(core == 0, high, low).astype(jnp.bfloat16)


def down(place, parts, weight, keep, after):
    n = len(parts)
    rows = parts[0].shape[0]
    depth, width = weight.shape
    tile = min(width, TILE)
    out = pl.BlockSpec((n, rows // 2, tile), lambda i, *_: (0, 0, i))
    return pl.pallas_call(
        functools.partial(down_kernel, n),
        grid_spec=pltpu.PrefetchScalarGridSpec(
            num_scalar_prefetch=1,
            grid=(width // tile,),
            in_specs=[pl.BlockSpec((rows, depth), lambda i, *_: (0, 0))] * n
            + [pl.BlockSpec((depth, tile), lambda i, *_: (0, i))]
            + [pl.BlockSpec((keep.shape[0], tile), lambda i, *_: (0, i))]
            + [pl.BlockSpec(memory_space=pl.ANY)] * len(after),
            out_specs=[out, out],
            scratch_shapes=[pltpu.VMEM((n * rows, depth), jnp.bfloat16)],
        ),
        out_shape=[
            jax.ShapeDtypeStruct((n, rows // 2, width), jnp.float32),
            jax.ShapeDtypeStruct((n, rows // 2, width), jnp.bfloat16),
        ],
        compiler_params=pltpu.CompilerParams(vmem_limit_bytes=VMEM_BYTES),
        cost_estimate=pl.CostEstimate(
            flops=2 * n * rows * depth * width, bytes_accessed=2 * depth * width, transcendentals=0
        ),
        name="down",
    )(place, *parts, weight, keep, *after)


def hold_kernel(value_ref, *refs):
    refs[-1][...] = value_ref[...]


def hold(value, after):
    if not after:
        return value
    spec = pl.BlockSpec(memory_space=pltpu.VMEM)
    return pl.pallas_call(
        hold_kernel,
        in_specs=[spec] + [pl.BlockSpec(memory_space=pl.ANY)] * len(after),
        out_specs=spec,
        out_shape=jax.ShapeDtypeStruct(value.shape, value.dtype),
        compiler_params=pltpu.CompilerParams(vmem_limit_bytes=VMEM_BYTES),
        name="hold",
    )(value, *after)


def mirror(p, n):
    out = 0
    while n > 1:
        out, p, n = out * 2 + p % 2, p // 2, n // 2
    return out


def local(n_tok, n_hid, tokens, gate_weight, up_weight, down_weight, gate_keep, up_keep, down_keep):
    n_z = n_hid // 2
    tok, hid = lax.axis_index("tok"), lax.axis_index("hid")
    z, core = hid // 2, hid % 2
    offsets = [jnp.where(core == 0, p, mirror(p, n_tok)) for p in range(n_tok)]
    positions = [sum(jnp.where(off == tok ^ z ^ k, p, 0) for p, off in enumerate(offsets)) for k in range(n_tok)]
    place = jnp.stack([core] + [tok ^ z ^ off for off in offsets] + positions).astype(jnp.int32)

    def send(value, to):
        perm = []
        for t in range(n_tok):
            for zz in range(n_z):
                for c in range(2):
                    a, b, d = to(t, zz, c)
                    perm.append((t * n_hid + zz * 2 + c, a * n_hid + b * 2 + d))
        return lax.ppermute(value, AXES, perm)

    def across_tok(value, p):
        return send(value, lambda t, zz, c: (t ^ (p if c == 0 else mirror(p, n_tok)), zz, c))

    def across_z(value, j):
        return send(value, lambda t, zz, c: (t, zz ^ j, c))

    def across_core(value):
        return send(value, lambda t, zz, c: (t, zz, 1 - c))

    def halve(kept, sent, after):
        left = n_tok // 2
        parts = [kept]
        while True:
            parts.append(across_tok(sent, left))
            if left == 1:
                return parts, sent
            left //= 2
            sent = add_slots(parts, left, left, after)

    def gather(part):
        parts, left = [part], 1
        while left < n_tok:
            parts += [across_tok(part, left) for part in parts]
            left *= 2
        return parts

    def combine(mine, theirs):
        paired = across_core(theirs)
        sums = [mine[j] + paired[j].astype(jnp.float32) for j in range(n_z)]
        return sums[0], [part.astype(jnp.bfloat16) for part in sums[1:]]

    gate_wide = widen(gate_keep, gate_weight.shape[1])
    up_wide = widen(up_keep, up_weight.shape[1])
    down_wide = widen(down_keep, down_weight.shape[1])
    own = [send(tokens, lambda t, zz, c: (zz, t ^ k, c)) for k in range(n_z)]
    other = [across_core(block) for block in own]
    gate_kept, gate_sent = project(place, own, other, gate_weight, gate_wide, ())
    up_kept, up_sent = project(place, own, other, up_weight, up_wide, (gate_sent,))
    gate_parts, gate_last = halve(gate_kept, gate_sent, (up_sent,))
    up_parts, _ = halve(up_kept, up_sent, (gate_last,))
    hidden = [gather(activate(gate_parts, up_parts, s)) for s in range(BATCHES)]
    out, beside = [], []
    for s, parts in enumerate(hidden):
        for later in hidden[s + 1 : s + 2]:
            beside = beside + later[1:]
        mine, theirs = down(place, parts, down_weight, down_wide, ())
        total, sent = combine(mine, hold(theirs, beside))
        beside = [across_z(sent[j - 1], j) for j in range(1, n_z)]
        for part in beside:
            total += part.astype(jnp.float32)
        out.append(total.astype(jnp.bfloat16))
    return jnp.concatenate(out, axis=0)


def solution(mesh):
    n_tok, n_hid = mesh.shape["tok"], mesh.shape["hid"]
    return jax.shard_map(
        functools.partial(local, n_tok, n_hid),
        mesh=mesh,
        in_specs=(
            P("tok", "hid"),
            P("tok", "hid"),
            P("tok", "hid"),
            P("hid", "tok"),
            P("tok", "hid"),
            P("tok", "hid"),
            P("hid", "tok"),
        ),
        out_specs=P("hid", "tok"),
        check_vma=False,
    )
```

```python
import functools

import jax
import jax.numpy as jnp
from jax import lax
from jax.experimental import pallas as pl
from jax.experimental.pallas import tpu as pltpu
from jax.sharding import PartitionSpec as P

AXES = ("tok", "hid")
BATCHES = 2
STRIPS = 2
TILE = 512
VMEM_BYTES = 44 * 1024 * 1024


def masked_product(x_ref, weight_ref, keep_ref):
    block_rows, width = keep_ref.shape
    side = weight_ref.shape[0] // block_rows
    strips = []
    for i in range(block_rows):
        keep = jnp.broadcast_to(keep_ref[i : i + 1, :], (16, width)).astype(jnp.bfloat16)
        block = weight_ref[i * side : (i + 1) * side, :].reshape(side // 16, 16, width)
        strips.append((block * keep[None]).reshape(side, width))
    return jnp.dot(x_ref[...], jnp.concatenate(strips, axis=0), preferred_element_type=jnp.float32)


def widen(keep_mask, width):
    return jnp.repeat(keep_mask.astype(jnp.float32), width // keep_mask.shape[1], axis=1)


def project_kernel(n, place_ref, *refs):
    own, other = refs[:n], refs[n : 2 * n]
    gate_ref, up_ref, gate_mask, up_mask = refs[2 * n : 2 * n + 4]
    outs, x = refs[-5:-1], refs[-1]
    rows, half = own[0].shape

    @pl.when(pl.program_id(0) == 0)
    def _():
        core = place_ref[0]
        mine = pl.ds(pl.multiple_of(core * half, half), half)
        others = pl.ds(pl.multiple_of((1 - core) * half, half), half)
        for k in range(n):
            at = pl.ds(pl.multiple_of(place_ref[1 + n + k] * rows, rows), rows)
            x[at, mine] = own[k][...]
            x[at, others] = other[k][...]

    for which, (weight, mask) in enumerate(((gate_ref, gate_mask), (up_ref, up_mask))):
        product = masked_product(x, weight, mask)
        for p in range(n):
            offset = p if which == 0 else mirror(p, n)
            term = product[offset * rows : (offset + 1) * rows]
            if p < n // 2:
                outs[which][p] = term
            else:
                outs[2 + which][p - n // 2] = term.astype(jnp.bfloat16)


def project(place, own, other, weights, masks, strip, after):
    n = len(own)
    rows, half = own[0].shape
    depth, whole = weights[0].shape
    width = whole // STRIPS
    tile = min(width, TILE // 2)
    steps = width // tile
    part = pl.BlockSpec((rows, half), lambda i, *_: (0, 0))
    out = pl.BlockSpec((n // 2, rows, tile), lambda i, *_: (0, 0, i))
    return pl.pallas_call(
        functools.partial(project_kernel, n),
        grid_spec=pltpu.PrefetchScalarGridSpec(
            num_scalar_prefetch=1,
            grid=(steps,),
            in_specs=[part] * (2 * n)
            + [pl.BlockSpec((depth, tile), lambda i, *_: (0, strip * steps + i))] * 2
            + [pl.BlockSpec((masks[0].shape[0], tile), lambda i, *_: (0, strip * steps + i))] * 2
            + [pl.BlockSpec(memory_space=pl.ANY)] * len(after),
            out_specs=[out] * 4,
            scratch_shapes=[pltpu.VMEM((n * rows, depth), jnp.bfloat16)],
        ),
        out_shape=[jax.ShapeDtypeStruct((n // 2, rows, width), jnp.float32)] * 2
        + [jax.ShapeDtypeStruct((n // 2, rows, width), jnp.bfloat16)] * 2,
        compiler_params=pltpu.CompilerParams(vmem_limit_bytes=VMEM_BYTES),
        cost_estimate=pl.CostEstimate(
            flops=4 * n * rows * depth * width, bytes_accessed=4 * depth * width, transcendentals=0
        ),
        name="project",
    )(place, *own, *other, *weights, *masks, *after)


def total_of(refs):
    total = refs[0][...].astype(jnp.float32)
    for ref in refs[1:]:
        total += ref[...].astype(jnp.float32)
    return total


def add_kernel(n, *refs):
    refs[-2][...] = total_of(refs[:n]).astype(jnp.bfloat16)
    refs[-1][...] = total_of(refs[n : 2 * n]).astype(jnp.bfloat16)


def add_slots(gate_parts, up_parts, first, count, after):
    _, rows, width = gate_parts[0].shape
    n = len(gate_parts)
    return pl.pallas_call(
        functools.partial(add_kernel, n),
        grid=(count,),
        in_specs=[pl.BlockSpec((1, rows, width), lambda i: (first + i, 0, 0))] * (2 * n)
        + [pl.BlockSpec(memory_space=pl.ANY)] * len(after),
        out_specs=[pl.BlockSpec((1, rows, width), lambda i: (i, 0, 0))] * 2,
        out_shape=[jax.ShapeDtypeStruct((count, rows, width), jnp.bfloat16)] * 2,
        compiler_params=pltpu.CompilerParams(vmem_limit_bytes=VMEM_BYTES),
        name="add_slots",
    )(*gate_parts, *up_parts, *after)


def activate_kernel(n, *refs):
    out_ref = refs[-1]
    width = out_ref.shape[1] // STRIPS
    for i in range(STRIPS):
        gate = total_of(refs[2 * n * i : 2 * n * i + n])
        up = total_of(refs[2 * n * i + n : 2 * n * (i + 1)])
        result = gate / (1.0 + jnp.exp(-gate)) * up
        out_ref[:, i * width : (i + 1) * width] = result.reshape(-1, width).astype(jnp.bfloat16)


def activate(strips, batch):
    n = len(strips[0][0])
    _, rows, width = strips[0][0][0].shape
    piece = rows // (2 * BATCHES)
    parts = [part for gate_parts, up_parts in strips for part in gate_parts + up_parts]
    parts = [part.reshape(part.shape[0] * 2, rows // 2, width) for part in parts]
    return pl.pallas_call(
        functools.partial(activate_kernel, n),
        grid=(1,),
        in_specs=[pl.BlockSpec((2, piece, width), lambda i: (0, batch, 0))] * len(parts),
        out_specs=pl.BlockSpec((2 * piece, width * STRIPS), lambda i: (0, 0)),
        out_shape=jax.ShapeDtypeStruct((2 * piece, width * STRIPS), jnp.bfloat16),
        compiler_params=pltpu.CompilerParams(vmem_limit_bytes=VMEM_BYTES),
        name="hidden",
    )(*parts)


def down_kernel(n, place_ref, *refs):
    parts = refs[:n]
    weight_ref, keep_ref = refs[n : n + 2]
    mine_ref, other_ref, h = refs[-3:]
    rows = parts[0].shape[0]
    step = pl.program_id(0)

    @pl.when(step == 0)
    def _():
        for p in range(n):
            h[p * rows : (p + 1) * rows] = parts[p][...]

    product = masked_product(h, weight_ref, keep_ref)
    core = place_ref[0]
    half = rows // 2
    for p in range(n):
        slot = place_ref[1 + p]
        low = product[p * rows : p * rows + half]
        high = product[p * rows + half : (p + 1) * rows]
        mine_ref[slot] = jnp.where(core == 0, low, high)
        other_ref[slot] = jnp.where(core == 0, high, low).astype(jnp.bfloat16)


def down(place, parts, weight, keep, after):
    n = len(parts)
    rows = parts[0].shape[0]
    depth, width = weight.shape
    tile = min(width, TILE)
    out = pl.BlockSpec((n, rows // 2, tile), lambda i, *_: (0, 0, i))
    return pl.pallas_call(
        functools.partial(down_kernel, n),
        grid_spec=pltpu.PrefetchScalarGridSpec(
            num_scalar_prefetch=1,
            grid=(width // tile,),
            in_specs=[pl.BlockSpec((rows, depth), lambda i, *_: (0, 0))] * n
            + [pl.BlockSpec((depth, tile), lambda i, *_: (0, i))]
            + [pl.BlockSpec((keep.shape[0], tile), lambda i, *_: (0, i))]
            + [pl.BlockSpec(memory_space=pl.ANY)] * len(after),
            out_specs=[out, out],
            scratch_shapes=[pltpu.VMEM((n * rows, depth), jnp.bfloat16)],
        ),
        out_shape=[
            jax.ShapeDtypeStruct((n, rows // 2, width), jnp.float32),
            jax.ShapeDtypeStruct((n, rows // 2, width), jnp.bfloat16),
        ],
        compiler_params=pltpu.CompilerParams(vmem_limit_bytes=VMEM_BYTES),
        cost_estimate=pl.CostEstimate(
            flops=2 * n * rows * depth * width, bytes_accessed=2 * depth * width, transcendentals=0
        ),
        name="down",
    )(place, *parts, weight, keep, *after)


def hold_kernel(value_ref, *refs):
    refs[-1][...] = value_ref[...]


def hold(value, after):
    if not after:
        return value
    spec = pl.BlockSpec(memory_space=pltpu.VMEM)
    return pl.pallas_call(
        hold_kernel,
        in_specs=[spec] + [pl.BlockSpec(memory_space=pl.ANY)] * len(after),
        out_specs=spec,
        out_shape=jax.ShapeDtypeStruct(value.shape, value.dtype),
        compiler_params=pltpu.CompilerParams(vmem_limit_bytes=VMEM_BYTES),
        name="hold",
    )(value, *after)


def mirror(p, n):
    out = 0
    while n > 1:
        out, p, n = out * 2 + p % 2, p // 2, n // 2
    return out


def local(n_tok, n_hid, tokens, gate_weight, up_weight, down_weight, gate_keep, up_keep, down_keep):
    n_z = n_hid // 2
    tok, hid = lax.axis_index("tok"), lax.axis_index("hid")
    z, core = hid // 2, hid % 2
    offsets = [jnp.where(core == 0, p, mirror(p, n_tok)) for p in range(n_tok)]
    place = jnp.stack([core] + [tok ^ z ^ off for off in offsets] + [tok ^ z ^ k for k in range(n_z)])
    place = place.astype(jnp.int32)

    def send(value, to):
        perm = []
        for t in range(n_tok):
            for zz in range(n_z):
                for c in range(2):
                    a, b, d = to(t, zz, c)
                    perm.append((t * n_hid + zz * 2 + c, a * n_hid + b * 2 + d))
        return lax.ppermute(value, AXES, perm)

    def across_tok(value, p):
        return send(value, lambda t, zz, c: (t ^ (p if c == 0 else mirror(p, n_tok)), zz, c))

    def across_z(value, j):
        return send(value, lambda t, zz, c: (t, zz ^ j, c))

    def across_core(value):
        return send(value, lambda t, zz, c: (t, zz, 1 - c))

    def halve(gate_kept, up_kept, gate_sent, up_sent, after):
        left = n_tok // 2
        gate_parts, up_parts = [gate_kept], [up_kept]
        while True:
            turned = mirror(left, n_tok)
            gate_parts.append(send(gate_sent, lambda t, zz, c: (t ^ left, zz, c)))
            up_parts.append(send(up_sent, lambda t, zz, c: (t ^ turned, zz, c)))
            if left == 1:
                return gate_parts, up_parts, gate_sent
            left //= 2
            gate_sent, up_sent = add_slots(gate_parts, up_parts, left, left, after)

    def gather(part):
        parts, left = [part], 1
        while left < n_tok:
            parts += [across_tok(part, left) for part in parts]
            left *= 2
        return parts

    def combine(mine, theirs):
        paired = across_core(theirs)
        sums = [mine[j] + paired[j].astype(jnp.float32) for j in range(n_z)]
        return sums[0], [part.astype(jnp.bfloat16) for part in sums[1:]]

    gate_wide = widen(gate_keep, gate_weight.shape[1])
    up_wide = widen(up_keep, up_weight.shape[1])
    down_wide = widen(down_keep, down_weight.shape[1])
    own = [send(tokens, lambda t, zz, c: (zz, t ^ k, c)) for k in range(n_z)]
    other = [across_core(block) for block in own]
    weights, masks = (gate_weight, up_weight), (gate_wide, up_wide)
    sums, after = [], ()
    for i in range(STRIPS):
        sums.append(project(place, own, other, weights, masks, i, after))
        after = (sums[i][2],)
    strips = []
    for i in range(STRIPS):
        gate_parts, up_parts, last = halve(*sums[i], after)
        strips.append((gate_parts, up_parts))
        after = (last,)
    hidden = [gather(activate(strips, s)) for s in range(BATCHES)]
    out, beside = [], []
    for s, parts in enumerate(hidden):
        for later in hidden[s + 1 : s + 2]:
            beside = beside + later[1:]
        mine, theirs = down(place, parts, down_weight, down_wide, ())
        total, sent = combine(mine, hold(theirs, beside))
        beside = [across_z(sent[j - 1], j) for j in range(1, n_z)]
        for part in beside:
            total += part.astype(jnp.float32)
        out.append(total.astype(jnp.bfloat16))
    return jnp.concatenate(out, axis=0)


def solution(mesh):
    n_tok, n_hid = mesh.shape["tok"], mesh.shape["hid"]
    return jax.shard_map(
        functools.partial(local, n_tok, n_hid),
        mesh=mesh,
        in_specs=(
            P("tok", "hid"),
            P("tok", "hid"),
            P("tok", "hid"),
            P("hid", "tok"),
            P("tok", "hid"),
            P("tok", "hid"),
            P("hid", "tok"),
        ),
        out_specs=P("hid", "tok"),
        check_vma=False,
    )
```

```python
import functools

import jax
import jax.numpy as jnp
from jax import lax
from jax.experimental import pallas as pl
from jax.experimental.pallas import tpu as pltpu
from jax.sharding import PartitionSpec as P

AXES = ("tok", "hid")
BATCHES = 2
STRIPS = 2
TILE = 512
VMEM_BYTES = 44 * 1024 * 1024


def masked_product(x_ref, weight_ref, keep_ref):
    block_rows, width = keep_ref.shape
    side = weight_ref.shape[0] // block_rows
    strips = []
    for i in range(block_rows):
        keep = jnp.broadcast_to(keep_ref[i : i + 1, :], (16, width)).astype(jnp.bfloat16)
        block = weight_ref[i * side : (i + 1) * side, :].reshape(side // 16, 16, width)
        strips.append((block * keep[None]).reshape(side, width))
    return jnp.dot(x_ref[...], jnp.concatenate(strips, axis=0), preferred_element_type=jnp.float32)


def widen(keep_mask, width):
    return jnp.repeat(keep_mask.astype(jnp.float32), width // keep_mask.shape[1], axis=1)


def project_kernel(n, place_ref, *refs):
    own, other = refs[:n], refs[n : 2 * n]
    gate_ref, up_ref, gate_mask, up_mask = refs[2 * n : 2 * n + 4]
    outs, x = refs[-5:-1], refs[-1]
    rows, half = own[0].shape

    @pl.when(pl.program_id(0) == 0)
    def _():
        core = place_ref[0]
        mine = pl.ds(pl.multiple_of(core * half, half), half)
        others = pl.ds(pl.multiple_of((1 - core) * half, half), half)
        for k in range(n):
            at = pl.ds(pl.multiple_of(place_ref[1 + n + k] * rows, rows), rows)
            x[at, mine] = own[k][...]
            x[at, others] = other[k][...]

    for which, (weight, mask) in enumerate(((gate_ref, gate_mask), (up_ref, up_mask))):
        product = masked_product(x, weight, mask)
        for p in range(n):
            offset = p if which == 0 else mirror(p, n)
            term = product[offset * rows : (offset + 1) * rows]
            if p < n // 2:
                outs[which][p] = term
            else:
                outs[2 + which][p - n // 2] = term.astype(jnp.bfloat16)


def project(place, own, other, weights, masks, strip, after):
    n = len(own)
    rows, half = own[0].shape
    depth, whole = weights[0].shape
    width = whole // STRIPS
    tile = min(width, TILE // 2)
    steps = width // tile
    part = pl.BlockSpec((rows, half), lambda i, *_: (0, 0))
    out = pl.BlockSpec((n // 2, rows, tile), lambda i, *_: (0, 0, i))
    return pl.pallas_call(
        functools.partial(project_kernel, n),
        grid_spec=pltpu.PrefetchScalarGridSpec(
            num_scalar_prefetch=1,
            grid=(steps,),
            in_specs=[part] * (2 * n)
            + [pl.BlockSpec((depth, tile), lambda i, *_: (0, strip * steps + i))] * 2
            + [pl.BlockSpec((masks[0].shape[0], tile), lambda i, *_: (0, strip * steps + i))] * 2
            + [pl.BlockSpec(memory_space=pl.ANY)] * len(after),
            out_specs=[out] * 4,
            scratch_shapes=[pltpu.VMEM((n * rows, depth), jnp.bfloat16)],
        ),
        out_shape=[jax.ShapeDtypeStruct((n // 2, rows, width), jnp.float32)] * 2
        + [jax.ShapeDtypeStruct((n // 2, rows, width), jnp.bfloat16)] * 2,
        compiler_params=pltpu.CompilerParams(vmem_limit_bytes=VMEM_BYTES),
        cost_estimate=pl.CostEstimate(
            flops=4 * n * rows * depth * width, bytes_accessed=4 * depth * width, transcendentals=0
        ),
        name="project",
    )(place, *own, *other, *weights, *masks, *after)


def total_of(refs):
    total = refs[0][...].astype(jnp.float32)
    for ref in refs[1:]:
        total += ref[...].astype(jnp.float32)
    return total


def add_kernel(n, *refs):
    refs[-2][...] = total_of(refs[:n]).astype(jnp.bfloat16)
    refs[-1][...] = total_of(refs[n : 2 * n]).astype(jnp.bfloat16)


def add_slots(gate_parts, up_parts, first, count, after):
    _, rows, width = gate_parts[0].shape
    n = len(gate_parts)
    return pl.pallas_call(
        functools.partial(add_kernel, n),
        grid=(count,),
        in_specs=[pl.BlockSpec((1, rows, width), lambda i: (first + i, 0, 0))] * (2 * n)
        + [pl.BlockSpec(memory_space=pl.ANY)] * len(after),
        out_specs=[pl.BlockSpec((1, rows, width), lambda i: (i, 0, 0))] * 2,
        out_shape=[jax.ShapeDtypeStruct((count, rows, width), jnp.bfloat16)] * 2,
        compiler_params=pltpu.CompilerParams(vmem_limit_bytes=VMEM_BYTES),
        name="add_slots",
    )(*gate_parts, *up_parts, *after)


def activate_kernel(n, *refs):
    out_ref = refs[-1]
    width = out_ref.shape[1] // STRIPS
    for i in range(STRIPS):
        gate = total_of(refs[2 * n * i : 2 * n * i + n])
        up = total_of(refs[2 * n * i + n : 2 * n * (i + 1)])
        result = gate / (1.0 + jnp.exp(-gate)) * up
        out_ref[:, i * width : (i + 1) * width] = result.reshape(-1, width).astype(jnp.bfloat16)


def activate(strips, batch):
    n = len(strips[0][0])
    _, rows, width = strips[0][0][0].shape
    piece = rows // (2 * BATCHES)
    parts = [part for gate_parts, up_parts in strips for part in gate_parts + up_parts]
    parts = [part.reshape(part.shape[0] * 2, rows // 2, width) for part in parts]
    return pl.pallas_call(
        functools.partial(activate_kernel, n),
        grid=(1,),
        in_specs=[pl.BlockSpec((2, piece, width), lambda i: (0, batch, 0))] * len(parts),
        out_specs=pl.BlockSpec((2 * piece, width * STRIPS), lambda i: (0, 0)),
        out_shape=jax.ShapeDtypeStruct((2 * piece, width * STRIPS), jnp.bfloat16),
        compiler_params=pltpu.CompilerParams(vmem_limit_bytes=VMEM_BYTES),
        name="hidden",
    )(*parts)


def down_kernel(n, place_ref, *refs):
    parts = refs[: n * BATCHES]
    weight_ref, keep_ref, mine_ref, other_ref, h = refs[n * BATCHES :]
    rows = parts[0].shape[0]

    @pl.when(pl.program_id(0) == 0)
    def _():
        for i, part in enumerate(parts):
            h[i * rows : (i + 1) * rows] = part[...]

    product = masked_product(h, weight_ref, keep_ref)
    core = place_ref[0]
    half = rows // 2
    for i in range(n * BATCHES):
        batch, slot = i // n, place_ref[1 + i % n]
        low = product[i * rows : i * rows + half]
        high = product[i * rows + half : (i + 1) * rows]
        mine_ref[slot, batch * half : (batch + 1) * half] = jnp.where(core == 0, low, high)
        other_ref[slot, batch * half : (batch + 1) * half] = jnp.where(core == 0, high, low).astype(jnp.bfloat16)


def down(place, hidden, weight, keep, strip):
    n = len(hidden[0])
    parts = [part for batch in hidden for part in batch]
    rows = parts[0].shape[0]
    depth, whole = weight.shape
    width = whole // STRIPS
    tile = min(width, TILE // 2)
    steps = width // tile
    height = rows // 2 * BATCHES
    out = pl.BlockSpec((n, height, tile), lambda i, *_: (0, 0, i))
    return pl.pallas_call(
        functools.partial(down_kernel, n),
        grid_spec=pltpu.PrefetchScalarGridSpec(
            num_scalar_prefetch=1,
            grid=(steps,),
            in_specs=[pl.BlockSpec((rows, depth), lambda i, *_: (0, 0))] * len(parts)
            + [pl.BlockSpec((depth, tile), lambda i, *_: (0, strip * steps + i))]
            + [pl.BlockSpec((keep.shape[0], tile), lambda i, *_: (0, strip * steps + i))],
            out_specs=[out, out],
            scratch_shapes=[pltpu.VMEM((len(parts) * rows, depth), jnp.bfloat16)],
        ),
        out_shape=[
            jax.ShapeDtypeStruct((n, height, width), jnp.float32),
            jax.ShapeDtypeStruct((n, height, width), jnp.bfloat16),
        ],
        compiler_params=pltpu.CompilerParams(vmem_limit_bytes=VMEM_BYTES),
        cost_estimate=pl.CostEstimate(
            flops=2 * len(parts) * rows * depth * width, bytes_accessed=2 * depth * width, transcendentals=0
        ),
        name="down",
    )(place, *parts, weight, keep)


def mirror(p, n):
    out = 0
    while n > 1:
        out, p, n = out * 2 + p % 2, p // 2, n // 2
    return out


def local(n_tok, n_hid, tokens, gate_weight, up_weight, down_weight, gate_keep, up_keep, down_keep):
    n_z = n_hid // 2
    tok, hid = lax.axis_index("tok"), lax.axis_index("hid")
    z, core = hid // 2, hid % 2
    offsets = [jnp.where(core == 0, p, mirror(p, n_tok)) for p in range(n_tok)]
    place = jnp.stack([core] + [tok ^ z ^ off for off in offsets] + [tok ^ z ^ k for k in range(n_z)])
    place = place.astype(jnp.int32)

    def send(value, to):
        perm = []
        for t in range(n_tok):
            for zz in range(n_z):
                for c in range(2):
                    a, b, d = to(t, zz, c)
                    perm.append((t * n_hid + zz * 2 + c, a * n_hid + b * 2 + d))
        return lax.ppermute(value, AXES, perm)

    def across_tok(value, p):
        return send(value, lambda t, zz, c: (t ^ (p if c == 0 else mirror(p, n_tok)), zz, c))

    def across_z(value, j):
        return send(value, lambda t, zz, c: (t, zz ^ j, c))

    def across_core(value):
        return send(value, lambda t, zz, c: (t, zz, 1 - c))

    def halve(gate_kept, up_kept, gate_sent, up_sent, after):
        left = n_tok // 2
        gate_parts, up_parts = [gate_kept], [up_kept]
        while True:
            turned = mirror(left, n_tok)
            gate_parts.append(send(gate_sent, lambda t, zz, c: (t ^ left, zz, c)))
            up_parts.append(send(up_sent, lambda t, zz, c: (t ^ turned, zz, c)))
            if left == 1:
                return gate_parts, up_parts, gate_sent
            left //= 2
            gate_sent, up_sent = add_slots(gate_parts, up_parts, left, left, after)

    def gather(part):
        parts, left = [part], 1
        while left < n_tok:
            parts += [across_tok(part, left) for part in parts]
            left *= 2
        return parts

    def combine(mine, theirs):
        paired = across_core(theirs)
        sums = [mine[j] + paired[j].astype(jnp.float32) for j in range(n_z)]
        return sums[0], [part.astype(jnp.bfloat16) for part in sums[1:]]

    gate_wide = widen(gate_keep, gate_weight.shape[1])
    up_wide = widen(up_keep, up_weight.shape[1])
    down_wide = widen(down_keep, down_weight.shape[1])
    own = [send(tokens, lambda t, zz, c: (zz, t ^ k, c)) for k in range(n_z)]
    other = [across_core(block) for block in own]
    weights, masks = (gate_weight, up_weight), (gate_wide, up_wide)
    sums, after = [], ()
    for i in range(STRIPS):
        sums.append(project(place, own, other, weights, masks, i, after))
        after = (sums[i][2],)
    strips = []
    for i in range(STRIPS):
        gate_parts, up_parts, last = halve(*sums[i], after)
        strips.append((gate_parts, up_parts))
        after = (last,)
    hidden = [gather(activate(strips, s)) for s in range(BATCHES)]
    out = []
    for i in range(STRIPS):
        total, sent = combine(*down(place, hidden, down_weight, down_wide, i))
        for j in range(1, n_z):
            total += across_z(sent[j - 1], j).astype(jnp.float32)
        out.append(total.astype(jnp.bfloat16))
    return jnp.concatenate(out, axis=1)


def solution(mesh):
    n_tok, n_hid = mesh.shape["tok"], mesh.shape["hid"]
    return jax.shard_map(
        functools.partial(local, n_tok, n_hid),
        mesh=mesh,
        in_specs=(
            P("tok", "hid"),
            P("tok", "hid"),
            P("tok", "hid"),
            P("hid", "tok"),
            P("tok", "hid"),
            P("tok", "hid"),
            P("hid", "tok"),
        ),
        out_specs=P("hid", "tok"),
        check_vma=False,
    )
```

```python
import functools

import jax
import jax.numpy as jnp
from jax import lax
from jax.experimental import pallas as pl
from jax.experimental.pallas import tpu as pltpu
from jax.sharding import PartitionSpec as P

AXES = ("tok", "hid")
BATCHES = 2
STRIPS = 2
TILE = 512
VMEM_BYTES = 44 * 1024 * 1024


def masked_product(x_ref, weight_ref, keep_ref):
    block_rows, width = keep_ref.shape
    side = weight_ref.shape[0] // block_rows
    strips = []
    for i in range(block_rows):
        keep = jnp.broadcast_to(keep_ref[i : i + 1, :], (16, width)).astype(jnp.bfloat16)
        block = weight_ref[i * side : (i + 1) * side, :].reshape(side // 16, 16, width)
        strips.append((block * keep[None]).reshape(side, width))
    return jnp.dot(x_ref[...], jnp.concatenate(strips, axis=0), preferred_element_type=jnp.float32)


def widen(keep_mask, width):
    return jnp.repeat(keep_mask.astype(jnp.float32), width // keep_mask.shape[1], axis=1)


def project_kernel(n, place_ref, *refs):
    own, other = refs[:n], refs[n : 2 * n]
    gate_ref, up_ref, gate_mask, up_mask = refs[2 * n : 2 * n + 4]
    outs, x = refs[-5:-1], refs[-1]
    rows, half = own[0].shape

    @pl.when(pl.program_id(0) == 0)
    def _():
        core = place_ref[0]
        mine = pl.ds(pl.multiple_of(core * half, half), half)
        others = pl.ds(pl.multiple_of((1 - core) * half, half), half)
        for k in range(n):
            at = pl.ds(pl.multiple_of(place_ref[1 + n + k] * rows, rows), rows)
            x[at, mine] = own[k][...]
            x[at, others] = other[k][...]

    for which, (weight, mask) in enumerate(((gate_ref, gate_mask), (up_ref, up_mask))):
        product = masked_product(x, weight, mask)
        for p in range(n):
            offset = p if which == 0 else mirror(p, n)
            term = product[offset * rows : (offset + 1) * rows]
            if p < n // 2:
                outs[which][p] = term
            else:
                outs[2 + which][p - n // 2] = term.astype(jnp.bfloat16)


def project(place, own, other, weights, masks, strip, after):
    n = len(own)
    rows, half = own[0].shape
    depth, whole = weights[0].shape
    width = whole // STRIPS
    tile = min(width, TILE // 2)
    steps = width // tile
    part = pl.BlockSpec((rows, half), lambda i, *_: (0, 0))
    out = pl.BlockSpec((n // 2, rows, tile), lambda i, *_: (0, 0, i))
    return pl.pallas_call(
        functools.partial(project_kernel, n),
        grid_spec=pltpu.PrefetchScalarGridSpec(
            num_scalar_prefetch=1,
            grid=(steps,),
            in_specs=[part] * (2 * n)
            + [pl.BlockSpec((depth, tile), lambda i, *_: (0, strip * steps + i))] * 2
            + [pl.BlockSpec((masks[0].shape[0], tile), lambda i, *_: (0, strip * steps + i))] * 2
            + [pl.BlockSpec(memory_space=pl.ANY)] * len(after),
            out_specs=[out] * 4,
            scratch_shapes=[pltpu.VMEM((n * rows, depth), jnp.bfloat16)],
        ),
        out_shape=[jax.ShapeDtypeStruct((n // 2, rows, width), jnp.float32)] * 2
        + [jax.ShapeDtypeStruct((n // 2, rows, width), jnp.bfloat16)] * 2,
        compiler_params=pltpu.CompilerParams(vmem_limit_bytes=VMEM_BYTES),
        cost_estimate=pl.CostEstimate(
            flops=4 * n * rows * depth * width, bytes_accessed=4 * depth * width, transcendentals=0
        ),
        name="project",
    )(place, *own, *other, *weights, *masks, *after)


def total_of(refs):
    total = refs[0][...].astype(jnp.float32)
    for ref in refs[1:]:
        total += ref[...].astype(jnp.float32)
    return total


def add_kernel(n, *refs):
    refs[-2][...] = total_of(refs[:n]).astype(jnp.bfloat16)
    refs[-1][...] = total_of(refs[n : 2 * n]).astype(jnp.bfloat16)


def add_slots(gate_parts, up_parts, first, count, after):
    _, rows, width = gate_parts[0].shape
    n = len(gate_parts)
    return pl.pallas_call(
        functools.partial(add_kernel, n),
        grid=(count,),
        in_specs=[pl.BlockSpec((1, rows, width), lambda i: (first + i, 0, 0))] * (2 * n)
        + [pl.BlockSpec(memory_space=pl.ANY)] * len(after),
        out_specs=[pl.BlockSpec((1, rows, width), lambda i: (i, 0, 0))] * 2,
        out_shape=[jax.ShapeDtypeStruct((count, rows, width), jnp.bfloat16)] * 2,
        compiler_params=pltpu.CompilerParams(vmem_limit_bytes=VMEM_BYTES),
        name="add_slots",
    )(*gate_parts, *up_parts, *after)


def activate_kernel(n, *refs):
    out_ref = refs[-1]
    width = out_ref.shape[1] // STRIPS
    for i in range(STRIPS):
        gate = total_of(refs[2 * n * i : 2 * n * i + n])
        up = total_of(refs[2 * n * i + n : 2 * n * (i + 1)])
        result = gate / (1.0 + jnp.exp(-gate)) * up
        out_ref[:, i * width : (i + 1) * width] = result.reshape(-1, width).astype(jnp.bfloat16)


def activate(strips, batch, after):
    n = len(strips[0][0])
    _, rows, width = strips[0][0][0].shape
    piece = rows // (2 * BATCHES)
    parts = [part for gate_parts, up_parts in strips for part in gate_parts + up_parts]
    parts = [part.reshape(part.shape[0] * 2, rows // 2, width) for part in parts]
    return pl.pallas_call(
        functools.partial(activate_kernel, n),
        grid=(1,),
        in_specs=[pl.BlockSpec((2, piece, width), lambda i: (0, batch, 0))] * len(parts)
        + [pl.BlockSpec(memory_space=pl.ANY)] * len(after),
        out_specs=pl.BlockSpec((2 * piece, width * STRIPS), lambda i: (0, 0)),
        out_shape=jax.ShapeDtypeStruct((2 * piece, width * STRIPS), jnp.bfloat16),
        compiler_params=pltpu.CompilerParams(vmem_limit_bytes=VMEM_BYTES),
        name="hidden",
    )(*parts, *after)


def down_kernel(n, place_ref, *refs):
    parts = refs[:n]
    weight_ref, keep_ref = refs[n : n + 2]
    mine_ref, other_ref, h = refs[-3:]
    rows = parts[0].shape[0]
    step = pl.program_id(0)

    @pl.when(step == 0)
    def _():
        for p in range(n):
            h[p * rows : (p + 1) * rows] = parts[p][...]

    product = masked_product(h, weight_ref, keep_ref)
    core = place_ref[0]
    half = rows // 2
    for p in range(n):
        slot = place_ref[1 + p]
        low = product[p * rows : p * rows + half]
        high = product[p * rows + half : (p + 1) * rows]
        mine_ref[slot] = jnp.where(core == 0, low, high)
        other_ref[slot] = jnp.where(core == 0, high, low).astype(jnp.bfloat16)


def down(place, parts, weight, keep, after):
    n = len(parts)
    rows = parts[0].shape[0]
    depth, width = weight.shape
    tile = min(width, TILE)
    out = pl.BlockSpec((n, rows // 2, tile), lambda i, *_: (0, 0, i))
    return pl.pallas_call(
        functools.partial(down_kernel, n),
        grid_spec=pltpu.PrefetchScalarGridSpec(
            num_scalar_prefetch=1,
            grid=(width // tile,),
            in_specs=[pl.BlockSpec((rows, depth), lambda i, *_: (0, 0))] * n
            + [pl.BlockSpec((depth, tile), lambda i, *_: (0, i))]
            + [pl.BlockSpec((keep.shape[0], tile), lambda i, *_: (0, i))]
            + [pl.BlockSpec(memory_space=pl.ANY)] * len(after),
            out_specs=[out, out],
            scratch_shapes=[pltpu.VMEM((n * rows, depth), jnp.bfloat16)],
        ),
        out_shape=[
            jax.ShapeDtypeStruct((n, rows // 2, width), jnp.float32),
            jax.ShapeDtypeStruct((n, rows // 2, width), jnp.bfloat16),
        ],
        compiler_params=pltpu.CompilerParams(vmem_limit_bytes=VMEM_BYTES),
        cost_estimate=pl.CostEstimate(
            flops=2 * n * rows * depth * width, bytes_accessed=2 * depth * width, transcendentals=0
        ),
        name="down",
    )(place, *parts, weight, keep, *after)


def hold_kernel(value_ref, *refs):
    refs[-1][...] = value_ref[...]


def hold(value, after):
    if not after:
        return value
    spec = pl.BlockSpec(memory_space=pltpu.VMEM)
    return pl.pallas_call(
        hold_kernel,
        in_specs=[spec] + [pl.BlockSpec(memory_space=pl.ANY)] * len(after),
        out_specs=spec,
        out_shape=jax.ShapeDtypeStruct(value.shape, value.dtype),
        compiler_params=pltpu.CompilerParams(vmem_limit_bytes=VMEM_BYTES),
        name="hold",
    )(value, *after)


def finish_kernel(n, *refs):
    out_ref = refs[-1]
    rows = refs[0].shape[0]
    for s in range(BATCHES):
        out_ref[s * rows : (s + 1) * rows] = total_of(refs[n * s : n * (s + 1)]).astype(jnp.bfloat16)


def finish(batches):
    parts = [part for batch in batches for part in batch]
    rows, width = parts[0].shape
    spec = pl.BlockSpec(memory_space=pltpu.VMEM)
    return pl.pallas_call(
        functools.partial(finish_kernel, len(batches[0])),
        in_specs=[spec] * len(parts),
        out_specs=spec,
        out_shape=jax.ShapeDtypeStruct((rows * len(batches), width), jnp.bfloat16),
        compiler_params=pltpu.CompilerParams(vmem_limit_bytes=VMEM_BYTES),
        name="finish",
    )(*parts)


def mirror(p, n):
    out = 0
    while n > 1:
        out, p, n = out * 2 + p % 2, p // 2, n // 2
    return out


def local(n_tok, n_hid, tokens, gate_weight, up_weight, down_weight, gate_keep, up_keep, down_keep):
    n_z = n_hid // 2
    tok, hid = lax.axis_index("tok"), lax.axis_index("hid")
    z, core = hid // 2, hid % 2
    offsets = [jnp.where(core == 0, p, mirror(p, n_tok)) for p in range(n_tok)]
    place = jnp.stack([core] + [tok ^ z ^ off for off in offsets] + [tok ^ z ^ k for k in range(n_z)])
    place = place.astype(jnp.int32)

    def send(value, to):
        perm = []
        for t in range(n_tok):
            for zz in range(n_z):
                for c in range(2):
                    a, b, d = to(t, zz, c)
                    perm.append((t * n_hid + zz * 2 + c, a * n_hid + b * 2 + d))
        return lax.ppermute(value, AXES, perm)

    def across_tok(value, p):
        return send(value, lambda t, zz, c: (t ^ (p if c == 0 else mirror(p, n_tok)), zz, c))

    def across_z(value, j):
        return send(value, lambda t, zz, c: (t, zz ^ j, c))

    def across_core(value):
        return send(value, lambda t, zz, c: (t, zz, 1 - c))

    def halve(gate_kept, up_kept, gate_sent, up_sent, after):
        left = n_tok // 2
        gate_parts, up_parts = [gate_kept], [up_kept]
        while True:
            turned = mirror(left, n_tok)
            gate_parts.append(send(gate_sent, lambda t, zz, c: (t ^ left, zz, c)))
            up_parts.append(send(up_sent, lambda t, zz, c: (t ^ turned, zz, c)))
            if left == 1:
                return gate_parts, up_parts, gate_sent
            left //= 2
            gate_sent, up_sent = add_slots(gate_parts, up_parts, left, left, after)

    def gather(part):
        parts, left = [part], 1
        while left < n_tok:
            parts += [across_tok(part, left) for part in parts]
            left *= 2
        return parts

    def combine(mine, theirs):
        paired = across_core(theirs)
        sums = [mine[j] + paired[j].astype(jnp.float32) for j in range(n_z)]
        return sums[0], [part.astype(jnp.bfloat16) for part in sums[1:]]

    gate_wide = widen(gate_keep, gate_weight.shape[1])
    up_wide = widen(up_keep, up_weight.shape[1])
    down_wide = widen(down_keep, down_weight.shape[1])
    own = [send(tokens, lambda t, zz, c: (zz, t ^ k, c)) for k in range(n_z)]
    other = [across_core(block) for block in own]
    weights, masks = (gate_weight, up_weight), (gate_wide, up_wide)
    sums, after = [], ()
    for i in range(STRIPS):
        sums.append(project(place, own, other, weights, masks, i, after))
        after = (sums[i][2],)
    strips = []
    for i in range(STRIPS):
        gate_parts, up_parts, last = halve(*sums[i], after)
        strips.append((gate_parts, up_parts))
        after = (gate_parts[-1],)
    hidden, after = [], ()
    for s in range(BATCHES):
        hidden.append(gather(activate(strips, s, after)))
        after = tuple(hidden[s][1 << i] for i in range(n_tok.bit_length() - 1))
    out, beside = [], []
    for s, parts in enumerate(hidden):
        for later in hidden[s + 1 : s + 2]:
            beside = beside + later[1:]
        mine, theirs = down(place, parts, down_weight, down_wide, ())
        total, sent = combine(mine, hold(theirs, beside))
        beside = [across_z(sent[j - 1], j) for j in range(1, n_z)]
        out.append([total] + beside)
    return finish(out)


def solution(mesh):
    n_tok, n_hid = mesh.shape["tok"], mesh.shape["hid"]
    return jax.shard_map(
        functools.partial(local, n_tok, n_hid),
        mesh=mesh,
        in_specs=(
            P("tok", "hid"),
            P("tok", "hid"),
            P("tok", "hid"),
            P("hid", "tok"),
            P("tok", "hid"),
            P("tok", "hid"),
            P("hid", "tok"),
        ),
        out_specs=P("hid", "tok"),
        check_vma=False,
    )
```

```python
import functools

import jax
import jax.numpy as jnp
from jax import lax
from jax.experimental import pallas as pl
from jax.experimental.pallas import tpu as pltpu
from jax.sharding import PartitionSpec as P

AXES = ("tok", "hid")
BATCHES = 2
STRIPS = 4
TILE = 512
VMEM_BYTES = 44 * 1024 * 1024


def masked_product(x_ref, weight_ref, keep_ref):
    block_rows, width = keep_ref.shape
    side = weight_ref.shape[0] // block_rows
    strips = []
    for i in range(block_rows):
        keep = jnp.broadcast_to(keep_ref[i : i + 1, :], (16, width)).astype(jnp.bfloat16)
        block = weight_ref[i * side : (i + 1) * side, :].reshape(side // 16, 16, width)
        strips.append((block * keep[None]).reshape(side, width))
    return jnp.dot(x_ref[...], jnp.concatenate(strips, axis=0), preferred_element_type=jnp.float32)


def widen(keep_mask, width):
    return jnp.repeat(keep_mask.astype(jnp.float32), width // keep_mask.shape[1], axis=1)


def project_kernel(n, place_ref, *refs):
    own, other = refs[:n], refs[n : 2 * n]
    gate_ref, up_ref, gate_mask, up_mask = refs[2 * n : 2 * n + 4]
    outs, x = refs[-5:-1], refs[-1]
    rows, half = own[0].shape

    @pl.when(pl.program_id(0) == 0)
    def _():
        core = place_ref[0]
        mine = pl.ds(pl.multiple_of(core * half, half), half)
        others = pl.ds(pl.multiple_of((1 - core) * half, half), half)
        for k in range(n):
            at = pl.ds(pl.multiple_of(place_ref[1 + n + k] * rows, rows), rows)
            x[at, mine] = own[k][...]
            x[at, others] = other[k][...]

    for which, (weight, mask) in enumerate(((gate_ref, gate_mask), (up_ref, up_mask))):
        product = masked_product(x, weight, mask)
        for p in range(n):
            offset = p if which == 0 else mirror(p, n)
            term = product[offset * rows : (offset + 1) * rows]
            if p < n // 2:
                outs[which][p] = term
            else:
                outs[2 + which][p - n // 2] = term.astype(jnp.bfloat16)


def project(place, own, other, weights, masks, strip, after):
    n = len(own)
    rows, half = own[0].shape
    depth, whole = weights[0].shape
    width = whole // STRIPS
    tile = min(width, TILE // 2)
    steps = width // tile
    part = pl.BlockSpec((rows, half), lambda i, *_: (0, 0))
    out = pl.BlockSpec((n // 2, rows, tile), lambda i, *_: (0, 0, i))
    return pl.pallas_call(
        functools.partial(project_kernel, n),
        grid_spec=pltpu.PrefetchScalarGridSpec(
            num_scalar_prefetch=1,
            grid=(steps,),
            in_specs=[part] * (2 * n)
            + [pl.BlockSpec((depth, tile), lambda i, *_: (0, strip * steps + i))] * 2
            + [pl.BlockSpec((masks[0].shape[0], tile), lambda i, *_: (0, strip * steps + i))] * 2
            + [pl.BlockSpec(memory_space=pl.ANY)] * len(after),
            out_specs=[out] * 4,
            scratch_shapes=[pltpu.VMEM((n * rows, depth), jnp.bfloat16)],
        ),
        out_shape=[jax.ShapeDtypeStruct((n // 2, rows, width), jnp.float32)] * 2
        + [jax.ShapeDtypeStruct((n // 2, rows, width), jnp.bfloat16)] * 2,
        compiler_params=pltpu.CompilerParams(vmem_limit_bytes=VMEM_BYTES),
        cost_estimate=pl.CostEstimate(
            flops=4 * n * rows * depth * width, bytes_accessed=4 * depth * width, transcendentals=0
        ),
        name="project",
    )(place, *own, *other, *weights, *masks, *after)


def total_of(refs):
    total = refs[0][...].astype(jnp.float32)
    for ref in refs[1:]:
        total += ref[...].astype(jnp.float32)
    return total


def add_kernel(n, *refs):
    refs[-2][...] = total_of(refs[:n]).astype(jnp.bfloat16)
    refs[-1][...] = total_of(refs[n : 2 * n]).astype(jnp.bfloat16)


def add_slots(gate_parts, up_parts, first, count, after):
    _, rows, width = gate_parts[0].shape
    n = len(gate_parts)
    return pl.pallas_call(
        functools.partial(add_kernel, n),
        grid=(count,),
        in_specs=[pl.BlockSpec((1, rows, width), lambda i: (first + i, 0, 0))] * (2 * n)
        + [pl.BlockSpec(memory_space=pl.ANY)] * len(after),
        out_specs=[pl.BlockSpec((1, rows, width), lambda i: (i, 0, 0))] * 2,
        out_shape=[jax.ShapeDtypeStruct((count, rows, width), jnp.bfloat16)] * 2,
        compiler_params=pltpu.CompilerParams(vmem_limit_bytes=VMEM_BYTES),
        name="add_slots",
    )(*gate_parts, *up_parts, *after)


def activate_kernel(n, *refs):
    out_ref = refs[-1]
    width = out_ref.shape[1] // STRIPS
    for i in range(STRIPS):
        gate = total_of(refs[2 * n * i : 2 * n * i + n])
        up = total_of(refs[2 * n * i + n : 2 * n * (i + 1)])
        result = gate / (1.0 + jnp.exp(-gate)) * up
        out_ref[:, i * width : (i + 1) * width] = result.reshape(-1, width).astype(jnp.bfloat16)


def activate(strips, batch):
    n = len(strips[0][0])
    _, rows, width = strips[0][0][0].shape
    piece = rows // (2 * BATCHES)
    parts = [part for gate_parts, up_parts in strips for part in gate_parts + up_parts]
    parts = [part.reshape(part.shape[0] * 2, rows // 2, width) for part in parts]
    return pl.pallas_call(
        functools.partial(activate_kernel, n),
        grid=(1,),
        in_specs=[pl.BlockSpec((2, piece, width), lambda i: (0, batch, 0))] * len(parts),
        out_specs=pl.BlockSpec((2 * piece, width * STRIPS), lambda i: (0, 0)),
        out_shape=jax.ShapeDtypeStruct((2 * piece, width * STRIPS), jnp.bfloat16),
        compiler_params=pltpu.CompilerParams(vmem_limit_bytes=VMEM_BYTES),
        name="hidden",
    )(*parts)


def down_kernel(n, place_ref, *refs):
    parts = refs[:n]
    weight_ref, keep_ref = refs[n : n + 2]
    mine_ref, other_ref, h = refs[-3:]
    rows = parts[0].shape[0]
    step = pl.program_id(0)

    @pl.when(step == 0)
    def _():
        for p in range(n):
            h[p * rows : (p + 1) * rows] = parts[p][...]

    product = masked_product(h, weight_ref, keep_ref)
    core = place_ref[0]
    half = rows // 2
    for p in range(n):
        slot = place_ref[1 + p]
        low = product[p * rows : p * rows + half]
        high = product[p * rows + half : (p + 1) * rows]
        mine_ref[slot] = jnp.where(core == 0, low, high)
        other_ref[slot] = jnp.where(core == 0, high, low).astype(jnp.bfloat16)


def down(place, parts, weight, keep, after):
    n = len(parts)
    rows = parts[0].shape[0]
    depth, width = weight.shape
    tile = min(width, TILE)
    out = pl.BlockSpec((n, rows // 2, tile), lambda i, *_: (0, 0, i))
    return pl.pallas_call(
        functools.partial(down_kernel, n),
        grid_spec=pltpu.PrefetchScalarGridSpec(
            num_scalar_prefetch=1,
            grid=(width // tile,),
            in_specs=[pl.BlockSpec((rows, depth), lambda i, *_: (0, 0))] * n
            + [pl.BlockSpec((depth, tile), lambda i, *_: (0, i))]
            + [pl.BlockSpec((keep.shape[0], tile), lambda i, *_: (0, i))]
            + [pl.BlockSpec(memory_space=pl.ANY)] * len(after),
            out_specs=[out, out],
            scratch_shapes=[pltpu.VMEM((n * rows, depth), jnp.bfloat16)],
        ),
        out_shape=[
            jax.ShapeDtypeStruct((n, rows // 2, width), jnp.float32),
            jax.ShapeDtypeStruct((n, rows // 2, width), jnp.bfloat16),
        ],
        compiler_params=pltpu.CompilerParams(vmem_limit_bytes=VMEM_BYTES),
        cost_estimate=pl.CostEstimate(
            flops=2 * n * rows * depth * width, bytes_accessed=2 * depth * width, transcendentals=0
        ),
        name="down",
    )(place, *parts, weight, keep, *after)


def hold_kernel(value_ref, *refs):
    refs[-1][...] = value_ref[...]


def hold(value, after):
    if not after:
        return value
    spec = pl.BlockSpec(memory_space=pltpu.VMEM)
    return pl.pallas_call(
        hold_kernel,
        in_specs=[spec] + [pl.BlockSpec(memory_space=pl.ANY)] * len(after),
        out_specs=spec,
        out_shape=jax.ShapeDtypeStruct(value.shape, value.dtype),
        compiler_params=pltpu.CompilerParams(vmem_limit_bytes=VMEM_BYTES),
        name="hold",
    )(value, *after)


def mirror(p, n):
    out = 0
    while n > 1:
        out, p, n = out * 2 + p % 2, p // 2, n // 2
    return out


def local(n_tok, n_hid, tokens, gate_weight, up_weight, down_weight, gate_keep, up_keep, down_keep):
    n_z = n_hid // 2
    tok, hid = lax.axis_index("tok"), lax.axis_index("hid")
    z, core = hid // 2, hid % 2
    offsets = [jnp.where(core == 0, p, mirror(p, n_tok)) for p in range(n_tok)]
    place = jnp.stack([core] + [tok ^ z ^ off for off in offsets] + [tok ^ z ^ k for k in range(n_z)])
    place = place.astype(jnp.int32)

    def send(value, to):
        perm = []
        for t in range(n_tok):
            for zz in range(n_z):
                for c in range(2):
                    a, b, d = to(t, zz, c)
                    perm.append((t * n_hid + zz * 2 + c, a * n_hid + b * 2 + d))
        return lax.ppermute(value, AXES, perm)

    def across_tok(value, p):
        return send(value, lambda t, zz, c: (t ^ (p if c == 0 else mirror(p, n_tok)), zz, c))

    def across_z(value, j):
        return send(value, lambda t, zz, c: (t, zz ^ j, c))

    def across_core(value):
        return send(value, lambda t, zz, c: (t, zz, 1 - c))

    def halve(gate_kept, up_kept, gate_sent, up_sent, after):
        left = n_tok // 2
        gate_parts, up_parts = [gate_kept], [up_kept]
        while True:
            turned = mirror(left, n_tok)
            gate_parts.append(send(gate_sent, lambda t, zz, c: (t ^ left, zz, c)))
            up_parts.append(send(up_sent, lambda t, zz, c: (t ^ turned, zz, c)))
            if left == 1:
                return gate_parts, up_parts, gate_sent
            left //= 2
            gate_sent, up_sent = add_slots(gate_parts, up_parts, left, left, after)

    def gather(part):
        parts, left = [part], 1
        while left < n_tok:
            parts += [across_tok(part, left) for part in parts]
            left *= 2
        return parts

    def combine(mine, theirs):
        paired = across_core(theirs)
        sums = [mine[j] + paired[j].astype(jnp.float32) for j in range(n_z)]
        return sums[0], [part.astype(jnp.bfloat16) for part in sums[1:]]

    gate_wide = widen(gate_keep, gate_weight.shape[1])
    up_wide = widen(up_keep, up_weight.shape[1])
    down_wide = widen(down_keep, down_weight.shape[1])
    own = [send(tokens, lambda t, zz, c: (zz, t ^ k, c)) for k in range(n_z)]
    other = [across_core(block) for block in own]
    weights, masks = (gate_weight, up_weight), (gate_wide, up_wide)
    sums, after = [], ()
    for i in range(STRIPS):
        sums.append(project(place, own, other, weights, masks, i, after))
        after = (sums[i][2],)
    strips = []
    for i in range(STRIPS):
        gate_parts, up_parts, last = halve(*sums[i], after)
        strips.append((gate_parts, up_parts))
        after = (last,)
    hidden = [gather(activate(strips, s)) for s in range(BATCHES)]
    out, beside = [], []
    for s, parts in enumerate(hidden):
        for later in hidden[s + 1 : s + 2]:
            beside = beside + later[1:]
        mine, theirs = down(place, parts, down_weight, down_wide, ())
        total, sent = combine(mine, hold(theirs, beside))
        beside = [across_z(sent[j - 1], j) for j in range(1, n_z)]
        for part in beside:
            total += part.astype(jnp.float32)
        out.append(total.astype(jnp.bfloat16))
    return jnp.concatenate(out, axis=0)


def solution(mesh):
    n_tok, n_hid = mesh.shape["tok"], mesh.shape["hid"]
    return jax.shard_map(
        functools.partial(local, n_tok, n_hid),
        mesh=mesh,
        in_specs=(
            P("tok", "hid"),
            P("tok", "hid"),
            P("tok", "hid"),
            P("hid", "tok"),
            P("tok", "hid"),
            P("tok", "hid"),
            P("hid", "tok"),
        ),
        out_specs=P("hid", "tok"),
        check_vma=False,
    )
```

```python
import functools

import jax
import jax.numpy as jnp
from jax import lax
from jax.experimental import pallas as pl
from jax.experimental.pallas import tpu as pltpu
from jax.sharding import PartitionSpec as P

AXES = ("tok", "hid")
BATCHES = 2
STRIPS = 2
TILE = 512
VMEM_BYTES = 44 * 1024 * 1024


def masked_product(x_ref, weight_ref, keep_ref):
    block_rows, width = keep_ref.shape
    side = weight_ref.shape[0] // block_rows
    strips = []
    for i in range(block_rows):
        keep = jnp.broadcast_to(keep_ref[i : i + 1, :], (16, width)).astype(jnp.bfloat16)
        block = weight_ref[i * side : (i + 1) * side, :].reshape(side // 16, 16, width)
        strips.append((block * keep[None]).reshape(side, width))
    return jnp.dot(x_ref[...], jnp.concatenate(strips, axis=0), preferred_element_type=jnp.float32)


def widen(keep_mask, width):
    return jnp.repeat(keep_mask.astype(jnp.float32), width // keep_mask.shape[1], axis=1)


def project_kernel(n, place_ref, *refs):
    own, other = refs[:n], refs[n : 2 * n]
    gate_ref, up_ref, gate_mask, up_mask = refs[2 * n : 2 * n + 4]
    outs, x = refs[-5:-1], refs[-1]
    rows, half = own[0].shape

    @pl.when(pl.program_id(0) == 0)
    def _():
        core = place_ref[0]
        mine = pl.ds(pl.multiple_of(core * half, half), half)
        others = pl.ds(pl.multiple_of((1 - core) * half, half), half)
        for k in range(n):
            at = pl.ds(pl.multiple_of(place_ref[1 + n + k] * rows, rows), rows)
            x[at, mine] = own[k][...]
            x[at, others] = other[k][...]

    for which, (weight, mask) in enumerate(((gate_ref, gate_mask), (up_ref, up_mask))):
        product = masked_product(x, weight, mask)
        for p in range(n):
            offset = p if which == 0 else mirror(p, n)
            term = product[offset * rows : (offset + 1) * rows]
            if p < n // 2:
                outs[which][p] = term
            else:
                outs[2 + which][p - n // 2] = term.astype(jnp.bfloat16)


def project(place, own, other, weights, masks, strip, after):
    n = len(own)
    rows, half = own[0].shape
    depth, whole = weights[0].shape
    width = whole // STRIPS
    tile = min(width, TILE // 2)
    steps = width // tile
    part = pl.BlockSpec((rows, half), lambda i, *_: (0, 0))
    out = pl.BlockSpec((n // 2, rows, tile), lambda i, *_: (0, 0, i))
    return pl.pallas_call(
        functools.partial(project_kernel, n),
        grid_spec=pltpu.PrefetchScalarGridSpec(
            num_scalar_prefetch=1,
            grid=(steps,),
            in_specs=[part] * (2 * n)
            + [pl.BlockSpec((depth, tile), lambda i, *_: (0, strip * steps + i))] * 2
            + [pl.BlockSpec((masks[0].shape[0], tile), lambda i, *_: (0, strip * steps + i))] * 2
            + [pl.BlockSpec(memory_space=pl.ANY)] * len(after),
            out_specs=[out] * 4,
            scratch_shapes=[pltpu.VMEM((n * rows, depth), jnp.bfloat16)],
        ),
        out_shape=[jax.ShapeDtypeStruct((n // 2, rows, width), jnp.float32)] * 2
        + [jax.ShapeDtypeStruct((n // 2, rows, width), jnp.bfloat16)] * 2,
        compiler_params=pltpu.CompilerParams(vmem_limit_bytes=VMEM_BYTES),
        cost_estimate=pl.CostEstimate(
            flops=4 * n * rows * depth * width, bytes_accessed=4 * depth * width, transcendentals=0
        ),
        name="project",
    )(place, *own, *other, *weights, *masks, *after)


def total_of(refs):
    total = refs[0][...].astype(jnp.float32)
    for ref in refs[1:]:
        total += ref[...].astype(jnp.float32)
    return total


def add_kernel(n, *refs):
    refs[-2][...] = total_of(refs[:n]).astype(jnp.bfloat16)
    refs[-1][...] = total_of(refs[n : 2 * n]).astype(jnp.bfloat16)


def add_slots(gate_parts, up_parts, first, count, after):
    _, rows, width = gate_parts[0].shape
    n = len(gate_parts)
    return pl.pallas_call(
        functools.partial(add_kernel, n),
        grid=(count,),
        in_specs=[pl.BlockSpec((1, rows, width), lambda i: (first + i, 0, 0))] * (2 * n)
        + [pl.BlockSpec(memory_space=pl.ANY)] * len(after),
        out_specs=[pl.BlockSpec((1, rows, width), lambda i: (i, 0, 0))] * 2,
        out_shape=[jax.ShapeDtypeStruct((count, rows, width), jnp.bfloat16)] * 2,
        compiler_params=pltpu.CompilerParams(vmem_limit_bytes=VMEM_BYTES),
        name="add_slots",
    )(*gate_parts, *up_parts, *after)


def activate_kernel(n, *refs):
    out_ref = refs[-1]
    width = out_ref.shape[1] // STRIPS
    for i in range(STRIPS):
        gate = total_of(refs[2 * n * i : 2 * n * i + n])
        up = total_of(refs[2 * n * i + n : 2 * n * (i + 1)])
        result = gate / (1.0 + jnp.exp(-gate)) * up
        out_ref[:, i * width : (i + 1) * width] = result.reshape(-1, width).astype(jnp.bfloat16)


def activate(strips, batch):
    n = len(strips[0][0])
    _, rows, width = strips[0][0][0].shape
    piece = rows // (2 * BATCHES)
    parts = [part for gate_parts, up_parts in strips for part in gate_parts + up_parts]
    parts = [part.reshape(part.shape[0] * 2, rows // 2, width) for part in parts]
    return pl.pallas_call(
        functools.partial(activate_kernel, n),
        grid=(1,),
        in_specs=[pl.BlockSpec((2, piece, width), lambda i: (0, batch, 0))] * len(parts),
        out_specs=pl.BlockSpec((2 * piece, width * STRIPS), lambda i: (0, 0)),
        out_shape=jax.ShapeDtypeStruct((2 * piece, width * STRIPS), jnp.bfloat16),
        compiler_params=pltpu.CompilerParams(vmem_limit_bytes=VMEM_BYTES),
        name="hidden",
    )(*parts)


def down_kernel(n, place_ref, *refs):
    parts = refs[:n]
    weight_ref, keep_ref = refs[n : n + 2]
    mine_ref, other_ref, h = refs[-3:]
    rows = parts[0].shape[0]
    step = pl.program_id(0)

    @pl.when(step == 0)
    def _():
        for p in range(n):
            h[p * rows : (p + 1) * rows] = parts[p][...]

    product = masked_product(h, weight_ref, keep_ref)
    core = place_ref[0]
    half = rows // 2
    for p in range(n):
        slot = place_ref[1 + p]
        low = product[p * rows : p * rows + half]
        high = product[p * rows + half : (p + 1) * rows]
        mine_ref[slot] = jnp.where(core == 0, low, high)
        other_ref[slot] = jnp.where(core == 0, high, low).astype(jnp.bfloat16)


def down(place, parts, weight, keep, after):
    n = len(parts)
    rows = parts[0].shape[0]
    depth, width = weight.shape
    tile = min(width, TILE)
    out = pl.BlockSpec((n, rows // 2, tile), lambda i, *_: (0, 0, i))
    return pl.pallas_call(
        functools.partial(down_kernel, n),
        grid_spec=pltpu.PrefetchScalarGridSpec(
            num_scalar_prefetch=1,
            grid=(width // tile,),
            in_specs=[pl.BlockSpec((rows, depth), lambda i, *_: (0, 0))] * n
            + [pl.BlockSpec((depth, tile), lambda i, *_: (0, i))]
            + [pl.BlockSpec((keep.shape[0], tile), lambda i, *_: (0, i))]
            + [pl.BlockSpec(memory_space=pl.ANY)] * len(after),
            out_specs=[out, out],
            scratch_shapes=[pltpu.VMEM((n * rows, depth), jnp.bfloat16)],
        ),
        out_shape=[
            jax.ShapeDtypeStruct((n, rows // 2, width), jnp.float32),
            jax.ShapeDtypeStruct((n, rows // 2, width), jnp.bfloat16),
        ],
        compiler_params=pltpu.CompilerParams(vmem_limit_bytes=VMEM_BYTES),
        cost_estimate=pl.CostEstimate(
            flops=2 * n * rows * depth * width, bytes_accessed=2 * depth * width, transcendentals=0
        ),
        name="down",
    )(place, *parts, weight, keep, *after)


def hold_kernel(value_ref, *refs):
    refs[-1][...] = value_ref[...]


def hold(value, after):
    if not after:
        return value
    spec = pl.BlockSpec(memory_space=pltpu.VMEM)
    return pl.pallas_call(
        hold_kernel,
        in_specs=[spec] + [pl.BlockSpec(memory_space=pl.ANY)] * len(after),
        out_specs=spec,
        out_shape=jax.ShapeDtypeStruct(value.shape, value.dtype),
        compiler_params=pltpu.CompilerParams(vmem_limit_bytes=VMEM_BYTES),
        name="hold",
    )(value, *after)


def mirror(p, n):
    out = 0
    while n > 1:
        out, p, n = out * 2 + p % 2, p // 2, n // 2
    return out


def local(n_tok, n_hid, tokens, gate_weight, up_weight, down_weight, gate_keep, up_keep, down_keep):
    n_z = n_hid // 2
    tok, hid = lax.axis_index("tok"), lax.axis_index("hid")
    z, core = hid // 2, hid % 2
    offsets = [jnp.where(core == 0, p, mirror(p, n_tok)) for p in range(n_tok)]
    place = jnp.stack([core] + [tok ^ z ^ off for off in offsets] + [tok ^ z ^ k for k in range(n_z)])
    place = place.astype(jnp.int32)

    def send(value, to):
        perm = []
        for t in range(n_tok):
            for zz in range(n_z):
                for c in range(2):
                    a, b, d = to(t, zz, c)
                    perm.append((t * n_hid + zz * 2 + c, a * n_hid + b * 2 + d))
        return lax.ppermute(value, AXES, perm)

    def across_tok(value, p):
        return send(value, lambda t, zz, c: (t ^ (p if c == 0 else mirror(p, n_tok)), zz, c))

    def across_z(value, j):
        return send(value, lambda t, zz, c: (t, zz ^ j, c))

    def across_core(value):
        return send(value, lambda t, zz, c: (t, zz, 1 - c))

    def halve(gate_kept, up_kept, gate_sent, up_sent, after):
        left = n_tok // 2
        gate_parts, up_parts = [gate_kept], [up_kept]
        while True:
            turned = mirror(left, n_tok)
            gate_parts.append(send(gate_sent, lambda t, zz, c: (t ^ left, zz, c)))
            up_parts.append(send(up_sent, lambda t, zz, c: (t ^ turned, zz, c)))
            if left == 1:
                return gate_parts, up_parts, gate_sent
            left //= 2
            gate_sent, up_sent = add_slots(gate_parts, up_parts, left, left, after)

    def gather(part):
        parts, left = [part], 1
        while left < n_tok:
            parts += [across_tok(part, left) for part in parts]
            left *= 2
        return parts

    def combine(mine, theirs):
        paired = across_core(theirs)
        sums = [mine[j] + paired[j].astype(jnp.float32) for j in range(n_z)]
        return sums[0], [part.astype(jnp.bfloat16) for part in sums[1:]]

    gate_wide = widen(gate_keep, gate_weight.shape[1])
    up_wide = widen(up_keep, up_weight.shape[1])
    down_wide = widen(down_keep, down_weight.shape[1])
    own = [send(tokens, lambda t, zz, c: (zz, t ^ k, c)) for k in range(n_z)]
    other = [across_core(block) for block in own]
    weights, masks = (gate_weight, up_weight), (gate_wide, up_wide)
    sums, after = [], ()
    for i in range(STRIPS):
        sums.append(project(place, own, other, weights, masks, i, after))
        after = (sums[i][2],)
    strips = []
    for i in range(STRIPS):
        gate_parts, up_parts, last = halve(*sums[i], after)
        strips.append((gate_parts, up_parts))
        after = (last,)
    hidden = [gather(activate(strips, s)) for s in range(BATCHES)]
    out, beside = [], []
    for s, parts in enumerate(hidden):
        for later in hidden[s + 1 : s + 2]:
            beside = beside + later[1:]
        mine, theirs = down(place, parts, down_weight, down_wide, ())
        total, sent = combine(mine, hold(theirs, beside[:2] if s else beside))
        beside = [across_z(sent[j - 1], j) for j in range(1, n_z)]
        for part in beside:
            total += part.astype(jnp.float32)
        out.append(total.astype(jnp.bfloat16))
    return jnp.concatenate(out, axis=0)


def solution(mesh):
    n_tok, n_hid = mesh.shape["tok"], mesh.shape["hid"]
    return jax.shard_map(
        functools.partial(local, n_tok, n_hid),
        mesh=mesh,
        in_specs=(
            P("tok", "hid"),
            P("tok", "hid"),
            P("tok", "hid"),
            P("hid", "tok"),
            P("tok", "hid"),
            P("tok", "hid"),
            P("hid", "tok"),
        ),
        out_specs=P("hid", "tok"),
        check_vma=False,
    )
```

```python
import functools

import jax
import jax.numpy as jnp
from jax import lax
from jax.experimental import pallas as pl
from jax.experimental.pallas import tpu as pltpu
from jax.sharding import PartitionSpec as P

AXES = ("tok", "hid")
BATCHES = 2
STRIPS = 2
TILE = 512
VMEM_BYTES = 44 * 1024 * 1024


def masked_product(x_ref, weight_ref, keep_ref):
    block_rows, width = keep_ref.shape
    side = weight_ref.shape[0] // block_rows
    strips = []
    for i in range(block_rows):
        keep = jnp.broadcast_to(keep_ref[i : i + 1, :], (16, width)).astype(jnp.bfloat16)
        block = weight_ref[i * side : (i + 1) * side, :].reshape(side // 16, 16, width)
        strips.append((block * keep[None]).reshape(side, width))
    return jnp.dot(x_ref[...], jnp.concatenate(strips, axis=0), preferred_element_type=jnp.float32)


def widen(keep_mask, width):
    return jnp.repeat(keep_mask.astype(jnp.float32), width // keep_mask.shape[1], axis=1)


def project_kernel(n, place_ref, *refs):
    own, other = refs[:n], refs[n : 2 * n]
    gate_ref, up_ref, gate_mask, up_mask = refs[2 * n : 2 * n + 4]
    outs, x = refs[-5:-1], refs[-1]
    rows, half = own[0].shape

    @pl.when(pl.program_id(0) == 0)
    def _():
        core = place_ref[0]
        mine = pl.ds(pl.multiple_of(core * half, half), half)
        others = pl.ds(pl.multiple_of((1 - core) * half, half), half)
        for k in range(n):
            at = pl.ds(pl.multiple_of(place_ref[1 + n + k] * rows, rows), rows)
            x[at, mine] = own[k][...]
            x[at, others] = other[k][...]

    for which, (weight, mask) in enumerate(((gate_ref, gate_mask), (up_ref, up_mask))):
        product = masked_product(x, weight, mask)
        for p in range(n):
            offset = p if which == 0 else mirror(p, n)
            term = product[offset * rows : (offset + 1) * rows]
            if p < n // 2:
                outs[which][p] = term
            else:
                outs[2 + which][p - n // 2] = term.astype(jnp.bfloat16)


def project(place, own, other, weights, masks, strip, after):
    n = len(own)
    rows, half = own[0].shape
    depth, whole = weights[0].shape
    width = whole // STRIPS
    tile = min(width, TILE // 2)
    steps = width // tile
    part = pl.BlockSpec((rows, half), lambda i, *_: (0, 0))
    out = pl.BlockSpec((n // 2, rows, tile), lambda i, *_: (0, 0, i))
    return pl.pallas_call(
        functools.partial(project_kernel, n),
        grid_spec=pltpu.PrefetchScalarGridSpec(
            num_scalar_prefetch=1,
            grid=(steps,),
            in_specs=[part] * (2 * n)
            + [pl.BlockSpec((depth, tile), lambda i, *_: (0, strip * steps + i))] * 2
            + [pl.BlockSpec((masks[0].shape[0], tile), lambda i, *_: (0, strip * steps + i))] * 2
            + [pl.BlockSpec(memory_space=pl.ANY)] * len(after),
            out_specs=[out] * 4,
            scratch_shapes=[pltpu.VMEM((n * rows, depth), jnp.bfloat16)],
        ),
        out_shape=[jax.ShapeDtypeStruct((n // 2, rows, width), jnp.float32)] * 2
        + [jax.ShapeDtypeStruct((n // 2, rows, width), jnp.bfloat16)] * 2,
        compiler_params=pltpu.CompilerParams(vmem_limit_bytes=VMEM_BYTES),
        cost_estimate=pl.CostEstimate(
            flops=4 * n * rows * depth * width, bytes_accessed=4 * depth * width, transcendentals=0
        ),
        name="project",
    )(place, *own, *other, *weights, *masks, *after)


def total_of(refs):
    total = refs[0][...].astype(jnp.float32)
    for ref in refs[1:]:
        total += ref[...].astype(jnp.float32)
    return total


def add_kernel(n, *refs):
    refs[-2][...] = total_of(refs[:n]).astype(jnp.bfloat16)
    refs[-1][...] = total_of(refs[n : 2 * n]).astype(jnp.bfloat16)


def add_slots(gate_parts, up_parts, first, count, after):
    _, rows, width = gate_parts[0].shape
    n = len(gate_parts)
    return pl.pallas_call(
        functools.partial(add_kernel, n),
        grid=(count,),
        in_specs=[pl.BlockSpec((1, rows, width), lambda i: (first + i, 0, 0))] * (2 * n)
        + [pl.BlockSpec(memory_space=pl.ANY)] * len(after),
        out_specs=[pl.BlockSpec((1, rows, width), lambda i: (i, 0, 0))] * 2,
        out_shape=[jax.ShapeDtypeStruct((count, rows, width), jnp.bfloat16)] * 2,
        compiler_params=pltpu.CompilerParams(vmem_limit_bytes=VMEM_BYTES),
        name="add_slots",
    )(*gate_parts, *up_parts, *after)


def activate_kernel(n, *refs):
    out_ref = refs[-1]
    width = out_ref.shape[1] // STRIPS
    for i in range(STRIPS):
        gate = total_of(refs[2 * n * i : 2 * n * i + n])
        up = total_of(refs[2 * n * i + n : 2 * n * (i + 1)])
        result = gate / (1.0 + jnp.exp(-gate)) * up
        out_ref[:, i * width : (i + 1) * width] = result.reshape(-1, width).astype(jnp.bfloat16)


def activate(strips, batch):
    n = len(strips[0][0])
    _, rows, width = strips[0][0][0].shape
    piece = rows // (2 * BATCHES)
    parts = [part for gate_parts, up_parts in strips for part in gate_parts + up_parts]
    parts = [part.reshape(part.shape[0] * 2, rows // 2, width) for part in parts]
    return pl.pallas_call(
        functools.partial(activate_kernel, n),
        grid=(1,),
        in_specs=[pl.BlockSpec((2, piece, width), lambda i: (0, batch, 0))] * len(parts),
        out_specs=pl.BlockSpec((2 * piece, width * STRIPS), lambda i: (0, 0)),
        out_shape=jax.ShapeDtypeStruct((2 * piece, width * STRIPS), jnp.bfloat16),
        compiler_params=pltpu.CompilerParams(vmem_limit_bytes=VMEM_BYTES),
        name="hidden",
    )(*parts)


def down_kernel(n, place_ref, *refs):
    parts = refs[:n]
    weight_ref, keep_ref = refs[n : n + 2]
    mine_ref, other_ref, h = refs[-3:]
    rows = parts[0].shape[0]
    step = pl.program_id(0)

    @pl.when(step == 0)
    def _():
        for p in range(n):
            h[p * rows : (p + 1) * rows] = parts[p][...]

    product = masked_product(h, weight_ref, keep_ref)
    core = place_ref[0]
    half = rows // 2
    for p in range(n):
        slot = place_ref[1 + p]
        low = product[p * rows : p * rows + half]
        high = product[p * rows + half : (p + 1) * rows]
        mine_ref[slot] = jnp.where(core == 0, low, high)
        other_ref[slot] = jnp.where(core == 0, high, low).astype(jnp.bfloat16)


def down(place, parts, weight, keep, after):
    n = len(parts)
    rows = parts[0].shape[0]
    depth, width = weight.shape
    tile = min(width, TILE)
    out = pl.BlockSpec((n, rows // 2, tile), lambda i, *_: (0, 0, i))
    return pl.pallas_call(
        functools.partial(down_kernel, n),
        grid_spec=pltpu.PrefetchScalarGridSpec(
            num_scalar_prefetch=1,
            grid=(width // tile,),
            in_specs=[pl.BlockSpec((rows, depth), lambda i, *_: (0, 0))] * n
            + [pl.BlockSpec((depth, tile), lambda i, *_: (0, i))]
            + [pl.BlockSpec((keep.shape[0], tile), lambda i, *_: (0, i))]
            + [pl.BlockSpec(memory_space=pl.ANY)] * len(after),
            out_specs=[out, out],
            scratch_shapes=[pltpu.VMEM((n * rows, depth), jnp.bfloat16)],
        ),
        out_shape=[
            jax.ShapeDtypeStruct((n, rows // 2, width), jnp.float32),
            jax.ShapeDtypeStruct((n, rows // 2, width), jnp.bfloat16),
        ],
        compiler_params=pltpu.CompilerParams(vmem_limit_bytes=VMEM_BYTES),
        cost_estimate=pl.CostEstimate(
            flops=2 * n * rows * depth * width, bytes_accessed=2 * depth * width, transcendentals=0
        ),
        name="down",
    )(place, *parts, weight, keep, *after)


def hold_kernel(value_ref, *refs):
    refs[-1][...] = value_ref[...]


def hold(value, after):
    if not after:
        return value
    spec = pl.BlockSpec(memory_space=pltpu.VMEM)
    return pl.pallas_call(
        hold_kernel,
        in_specs=[spec] + [pl.BlockSpec(memory_space=pl.ANY)] * len(after),
        out_specs=spec,
        out_shape=jax.ShapeDtypeStruct(value.shape, value.dtype),
        compiler_params=pltpu.CompilerParams(vmem_limit_bytes=VMEM_BYTES),
        name="hold",
    )(value, *after)


def mirror(p, n):
    out = 0
    while n > 1:
        out, p, n = out * 2 + p % 2, p // 2, n // 2
    return out


def local(n_tok, n_hid, tokens, gate_weight, up_weight, down_weight, gate_keep, up_keep, down_keep):
    n_z = n_hid // 2
    tok, hid = lax.axis_index("tok"), lax.axis_index("hid")
    z, core = hid // 2, hid % 2
    offsets = [jnp.where(core == 0, p, mirror(p, n_tok)) for p in range(n_tok)]
    place = jnp.stack([core] + [tok ^ z ^ off for off in offsets] + [tok ^ z ^ k for k in range(n_z)])
    place = place.astype(jnp.int32)

    def send(value, to):
        perm = []
        for t in range(n_tok):
            for zz in range(n_z):
                for c in range(2):
                    a, b, d = to(t, zz, c)
                    perm.append((t * n_hid + zz * 2 + c, a * n_hid + b * 2 + d))
        return lax.ppermute(value, AXES, perm)

    def across_tok(value, p):
        return send(value, lambda t, zz, c: (t ^ (p if c == 0 else mirror(p, n_tok)), zz, c))

    def across_z(value, j):
        return send(value, lambda t, zz, c: (t, zz ^ j, c))

    def across_core(value):
        return send(value, lambda t, zz, c: (t, zz, 1 - c))

    def halve(gate_kept, up_kept, gate_sent, up_sent, after):
        left = n_tok // 2
        gate_parts, up_parts = [gate_kept], [up_kept]
        while True:
            turned = mirror(left, n_tok)
            gate_parts.append(send(gate_sent, lambda t, zz, c: (t ^ left, zz, c)))
            up_parts.append(send(up_sent, lambda t, zz, c: (t ^ turned, zz, c)))
            if left == 1:
                return gate_parts, up_parts, gate_sent
            left //= 2
            gate_sent, up_sent = add_slots(gate_parts, up_parts, left, left, after)

    def gather(part):
        parts, left = [part], 1
        while left < n_tok:
            parts += [across_tok(part, left) for part in parts]
            left *= 2
        return parts

    def combine(mine, theirs):
        paired = across_core(theirs)
        sums = [mine[j] + paired[j].astype(jnp.float32) for j in range(n_z)]
        return sums[0], [part.astype(jnp.bfloat16) for part in sums[1:]]

    gate_wide = widen(gate_keep, gate_weight.shape[1])
    up_wide = widen(up_keep, up_weight.shape[1])
    down_wide = widen(down_keep, down_weight.shape[1])
    own = [send(tokens, lambda t, zz, c: (zz, t ^ k, c)) for k in range(n_z)]
    other = [across_core(block) for block in own]
    weights, masks = (gate_weight, up_weight), (gate_wide, up_wide)
    sums, after = [], ()
    for i in range(STRIPS):
        sums.append(project(place, own, other, weights, masks, i, after))
        after = (sums[i][2],)
    strips = []
    for i in range(STRIPS):
        gate_parts, up_parts, last = halve(*sums[i], after)
        strips.append((gate_parts, up_parts))
        after = (last,)
    hidden = [gather(activate(strips, s)) for s in range(BATCHES)]
    out, beside = [], []
    for s, parts in enumerate(hidden):
        for later in hidden[s + 1 : s + 2]:
            beside = beside + later[1:]
        mine, theirs = down(place, parts, down_weight, down_wide, ())
        total, sent = combine(mine, hold(theirs, beside[1:2] if s else beside))
        beside = [across_z(sent[j - 1], j) for j in range(1, n_z)]
        for part in beside:
            total += part.astype(jnp.float32)
        out.append(total.astype(jnp.bfloat16))
    return jnp.concatenate(out, axis=0)


def solution(mesh):
    n_tok, n_hid = mesh.shape["tok"], mesh.shape["hid"]
    return jax.shard_map(
        functools.partial(local, n_tok, n_hid),
        mesh=mesh,
        in_specs=(
            P("tok", "hid"),
            P("tok", "hid"),
            P("tok", "hid"),
            P("hid", "tok"),
            P("tok", "hid"),
            P("tok", "hid"),
            P("hid", "tok"),
        ),
        out_specs=P("hid", "tok"),
        check_vma=False,
    )
```

```python
import functools

import jax
import jax.numpy as jnp
from jax import lax
from jax.experimental import pallas as pl
from jax.experimental.pallas import tpu as pltpu
from jax.sharding import PartitionSpec as P

AXES = ("tok", "hid")
BATCHES = 2
STRIPS = 2
TILE = 512
VMEM_BYTES = 44 * 1024 * 1024


def masked_product(x_ref, weight_ref, keep_ref):
    block_rows, width = keep_ref.shape
    side = weight_ref.shape[0] // block_rows
    strips = []
    for i in range(block_rows):
        keep = jnp.broadcast_to(keep_ref[i : i + 1, :], (16, width)).astype(jnp.bfloat16)
        block = weight_ref[i * side : (i + 1) * side, :].reshape(side // 16, 16, width)
        strips.append((block * keep[None]).reshape(side, width))
    return jnp.dot(x_ref[...], jnp.concatenate(strips, axis=0), preferred_element_type=jnp.float32)


def widen(keep_mask, width):
    return jnp.repeat(keep_mask.astype(jnp.float32), width // keep_mask.shape[1], axis=1)


def project_kernel(n, place_ref, *refs):
    own, other = refs[:n], refs[n : 2 * n]
    gate_ref, up_ref, gate_mask, up_mask = refs[2 * n : 2 * n + 4]
    outs, x = refs[-5:-1], refs[-1]
    rows, half = own[0].shape

    @pl.when(pl.program_id(0) == 0)
    def _():
        core = place_ref[0]
        mine = pl.ds(pl.multiple_of(core * half, half), half)
        others = pl.ds(pl.multiple_of((1 - core) * half, half), half)
        for k in range(n):
            at = pl.ds(pl.multiple_of(place_ref[1 + n + k] * rows, rows), rows)
            x[at, mine] = own[k][...]
            x[at, others] = other[k][...]

    for which, (weight, mask) in enumerate(((gate_ref, gate_mask), (up_ref, up_mask))):
        product = masked_product(x, weight, mask)
        for p in range(n):
            offset = p if which == 0 else mirror(p, n)
            term = product[offset * rows : (offset + 1) * rows]
            if p < n // 2:
                outs[which][p] = term
            else:
                outs[2 + which][p - n // 2] = term.astype(jnp.bfloat16)


def project(place, own, other, weights, masks, strip, after):
    n = len(own)
    rows, half = own[0].shape
    depth, whole = weights[0].shape
    width = whole // STRIPS
    tile = min(width, TILE)
    steps = width // tile
    part = pl.BlockSpec((rows, half), lambda i, *_: (0, 0))
    out = pl.BlockSpec((n // 2, rows, tile), lambda i, *_: (0, 0, i))
    return pl.pallas_call(
        functools.partial(project_kernel, n),
        grid_spec=pltpu.PrefetchScalarGridSpec(
            num_scalar_prefetch=1,
            grid=(steps,),
            in_specs=[part] * (2 * n)
            + [pl.BlockSpec((depth, tile), lambda i, *_: (0, strip * steps + i))] * 2
            + [pl.BlockSpec((masks[0].shape[0], tile), lambda i, *_: (0, strip * steps + i))] * 2
            + [pl.BlockSpec(memory_space=pl.ANY)] * len(after),
            out_specs=[out] * 4,
            scratch_shapes=[pltpu.VMEM((n * rows, depth), jnp.bfloat16)],
        ),
        out_shape=[jax.ShapeDtypeStruct((n // 2, rows, width), jnp.float32)] * 2
        + [jax.ShapeDtypeStruct((n // 2, rows, width), jnp.bfloat16)] * 2,
        compiler_params=pltpu.CompilerParams(vmem_limit_bytes=VMEM_BYTES),
        cost_estimate=pl.CostEstimate(
            flops=4 * n * rows * depth * width, bytes_accessed=4 * depth * width, transcendentals=0
        ),
        name="project",
    )(place, *own, *other, *weights, *masks, *after)


def total_of(refs):
    total = refs[0][...].astype(jnp.float32)
    for ref in refs[1:]:
        total += ref[...].astype(jnp.float32)
    return total


def add_kernel(n, *refs):
    refs[-2][...] = total_of(refs[:n]).astype(jnp.bfloat16)
    refs[-1][...] = total_of(refs[n : 2 * n]).astype(jnp.bfloat16)


def add_slots(gate_parts, up_parts, first, count, after):
    _, rows, width = gate_parts[0].shape
    n = len(gate_parts)
    return pl.pallas_call(
        functools.partial(add_kernel, n),
        grid=(count,),
        in_specs=[pl.BlockSpec((1, rows, width), lambda i: (first + i, 0, 0))] * (2 * n)
        + [pl.BlockSpec(memory_space=pl.ANY)] * len(after),
        out_specs=[pl.BlockSpec((1, rows, width), lambda i: (i, 0, 0))] * 2,
        out_shape=[jax.ShapeDtypeStruct((count, rows, width), jnp.bfloat16)] * 2,
        compiler_params=pltpu.CompilerParams(vmem_limit_bytes=VMEM_BYTES),
        name="add_slots",
    )(*gate_parts, *up_parts, *after)


def activate_kernel(n, *refs):
    out_ref = refs[-1]
    width = out_ref.shape[1] // STRIPS
    for i in range(STRIPS):
        gate = total_of(refs[2 * n * i : 2 * n * i + n])
        up = total_of(refs[2 * n * i + n : 2 * n * (i + 1)])
        result = gate / (1.0 + jnp.exp(-gate)) * up
        out_ref[:, i * width : (i + 1) * width] = result.reshape(-1, width).astype(jnp.bfloat16)


def activate(strips, batch):
    n = len(strips[0][0])
    _, rows, width = strips[0][0][0].shape
    piece = rows // (2 * BATCHES)
    parts = [part for gate_parts, up_parts in strips for part in gate_parts + up_parts]
    parts = [part.reshape(part.shape[0] * 2, rows // 2, width) for part in parts]
    return pl.pallas_call(
        functools.partial(activate_kernel, n),
        grid=(1,),
        in_specs=[pl.BlockSpec((2, piece, width), lambda i: (0, batch, 0))] * len(parts),
        out_specs=pl.BlockSpec((2 * piece, width * STRIPS), lambda i: (0, 0)),
        out_shape=jax.ShapeDtypeStruct((2 * piece, width * STRIPS), jnp.bfloat16),
        compiler_params=pltpu.CompilerParams(vmem_limit_bytes=VMEM_BYTES),
        name="hidden",
    )(*parts)


def down_kernel(n, place_ref, *refs):
    parts = refs[:n]
    weight_ref, keep_ref = refs[n : n + 2]
    mine_ref, other_ref, h = refs[-3:]
    rows = parts[0].shape[0]
    step = pl.program_id(0)

    @pl.when(step == 0)
    def _():
        for p in range(n):
            h[p * rows : (p + 1) * rows] = parts[p][...]

    product = masked_product(h, weight_ref, keep_ref)
    core = place_ref[0]
    half = rows // 2
    for p in range(n):
        slot = place_ref[1 + p]
        low = product[p * rows : p * rows + half]
        high = product[p * rows + half : (p + 1) * rows]
        mine_ref[slot] = jnp.where(core == 0, low, high)
        other_ref[slot] = jnp.where(core == 0, high, low).astype(jnp.bfloat16)


def down(place, parts, weight, keep, after):
    n = len(parts)
    rows = parts[0].shape[0]
    depth, width = weight.shape
    tile = min(width, TILE)
    out = pl.BlockSpec((n, rows // 2, tile), lambda i, *_: (0, 0, i))
    return pl.pallas_call(
        functools.partial(down_kernel, n),
        grid_spec=pltpu.PrefetchScalarGridSpec(
            num_scalar_prefetch=1,
            grid=(width // tile,),
            in_specs=[pl.BlockSpec((rows, depth), lambda i, *_: (0, 0))] * n
            + [pl.BlockSpec((depth, tile), lambda i, *_: (0, i))]
            + [pl.BlockSpec((keep.shape[0], tile), lambda i, *_: (0, i))]
            + [pl.BlockSpec(memory_space=pl.ANY)] * len(after),
            out_specs=[out, out],
            scratch_shapes=[pltpu.VMEM((n * rows, depth), jnp.bfloat16)],
        ),
        out_shape=[
            jax.ShapeDtypeStruct((n, rows // 2, width), jnp.float32),
            jax.ShapeDtypeStruct((n, rows // 2, width), jnp.bfloat16),
        ],
        compiler_params=pltpu.CompilerParams(vmem_limit_bytes=VMEM_BYTES),
        cost_estimate=pl.CostEstimate(
            flops=2 * n * rows * depth * width, bytes_accessed=2 * depth * width, transcendentals=0
        ),
        name="down",
    )(place, *parts, weight, keep, *after)


def hold_kernel(value_ref, *refs):
    refs[-1][...] = value_ref[...]


def hold(value, after):
    if not after:
        return value
    spec = pl.BlockSpec(memory_space=pltpu.VMEM)
    return pl.pallas_call(
        hold_kernel,
        in_specs=[spec] + [pl.BlockSpec(memory_space=pl.ANY)] * len(after),
        out_specs=spec,
        out_shape=jax.ShapeDtypeStruct(value.shape, value.dtype),
        compiler_params=pltpu.CompilerParams(vmem_limit_bytes=VMEM_BYTES),
        name="hold",
    )(value, *after)


def mirror(p, n):
    out = 0
    while n > 1:
        out, p, n = out * 2 + p % 2, p // 2, n // 2
    return out


def local(n_tok, n_hid, tokens, gate_weight, up_weight, down_weight, gate_keep, up_keep, down_keep):
    n_z = n_hid // 2
    tok, hid = lax.axis_index("tok"), lax.axis_index("hid")
    z, core = hid // 2, hid % 2
    offsets = [jnp.where(core == 0, p, mirror(p, n_tok)) for p in range(n_tok)]
    place = jnp.stack([core] + [tok ^ z ^ off for off in offsets] + [tok ^ z ^ k for k in range(n_z)])
    place = place.astype(jnp.int32)

    def send(value, to):
        perm = []
        for t in range(n_tok):
            for zz in range(n_z):
                for c in range(2):
                    a, b, d = to(t, zz, c)
                    perm.append((t * n_hid + zz * 2 + c, a * n_hid + b * 2 + d))
        return lax.ppermute(value, AXES, perm)

    def across_tok(value, p):
        return send(value, lambda t, zz, c: (t ^ (p if c == 0 else mirror(p, n_tok)), zz, c))

    def across_z(value, j):
        return send(value, lambda t, zz, c: (t, zz ^ j, c))

    def across_core(value):
        return send(value, lambda t, zz, c: (t, zz, 1 - c))

    def halve(gate_kept, up_kept, gate_sent, up_sent, after):
        left = n_tok // 2
        gate_parts, up_parts = [gate_kept], [up_kept]
        while True:
            turned = mirror(left, n_tok)
            gate_parts.append(send(gate_sent, lambda t, zz, c: (t ^ left, zz, c)))
            up_parts.append(send(up_sent, lambda t, zz, c: (t ^ turned, zz, c)))
            if left == 1:
                return gate_parts, up_parts, gate_sent
            left //= 2
            gate_sent, up_sent = add_slots(gate_parts, up_parts, left, left, after)

    def gather(part):
        parts, left = [part], 1
        while left < n_tok:
            parts += [across_tok(part, left) for part in parts]
            left *= 2
        return parts

    def combine(mine, theirs):
        paired = across_core(theirs)
        sums = [mine[j] + paired[j].astype(jnp.float32) for j in range(n_z)]
        return sums[0], [part.astype(jnp.bfloat16) for part in sums[1:]]

    gate_wide = widen(gate_keep, gate_weight.shape[1])
    up_wide = widen(up_keep, up_weight.shape[1])
    down_wide = widen(down_keep, down_weight.shape[1])
    own = [send(tokens, lambda t, zz, c: (zz, t ^ k, c)) for k in range(n_z)]
    other = [across_core(block) for block in own]
    weights, masks = (gate_weight, up_weight), (gate_wide, up_wide)
    sums, after = [], ()
    for i in range(STRIPS):
        sums.append(project(place, own, other, weights, masks, i, after))
        after = (sums[i][2],)
    strips = []
    for i in range(STRIPS):
        gate_parts, up_parts, last = halve(*sums[i], after)
        strips.append((gate_parts, up_parts))
        after = (last,)
    hidden = [gather(activate(strips, s)) for s in range(BATCHES)]
    out, beside = [], []
    for s, parts in enumerate(hidden):
        for later in hidden[s + 1 : s + 2]:
            beside = beside + later[1:]
        mine, theirs = down(place, parts, down_weight, down_wide, ())
        total, sent = combine(mine, hold(theirs, beside[:2] if s else beside))
        beside = [across_z(sent[j - 1], j) for j in range(1, n_z)]
        for part in beside:
            total += part.astype(jnp.float32)
        out.append(total.astype(jnp.bfloat16))
    return jnp.concatenate(out, axis=0)


def solution(mesh):
    n_tok, n_hid = mesh.shape["tok"], mesh.shape["hid"]
    return jax.shard_map(
        functools.partial(local, n_tok, n_hid),
        mesh=mesh,
        in_specs=(
            P("tok", "hid"),
            P("tok", "hid"),
            P("tok", "hid"),
            P("hid", "tok"),
            P("tok", "hid"),
            P("tok", "hid"),
            P("hid", "tok"),
        ),
        out_specs=P("hid", "tok"),
        check_vma=False,
    )
```
